512 devices in a mesh: gx: 16 (over y, x_hi, core), gy: 32 (over x_lo, z).
Axes of the slice: x: 4 (x_hi: 2, x_lo: 2; x = x_hi * 2 + x_lo), y: 4, z: 16, core: 2. Of those that a mesh axis runs over, the one named last changes fastest.
Arguments:
- abundance_start: float32 [1, 12, 1024, 4096], P(None, None, 'gx', 'gy'), may hold values from 0 to 1
- measured: bfloat16 [1, 32, 1024, 4096], P(None, None, 'gx', 'gy'), may hold values from 0 to 11, as said below
- spectra: float32 [32, 12], replicated, may hold values from 0.02 to 0.3
- taps_x: float32 [33], replicated, may hold values from 0.01 to 0.05
- taps_y: float32 [33], replicated, may hold values from 0.01 to 0.05
Outputs:
- abundance: float32 [1, 12, 1024, 4096], P(None, None, 'gx', 'gy')
The draws below stay inside these ranges and needn't reach their ends.
Inputs may be any that keep to these rules, and one draw needn't show every extreme that they name: `measured`: nonnegative intensities.
All inputs are finite; a program needn't handle non-finite values.
Results may differ from the reference program's by a relative error of at most 0.0003.
Values sent between devices are 32-bit elements; how exact they have to be, the bound alone decides.
No kernel may reach another device: no remote copies, remote signals or barrier semaphores. Data moves between devices by JAX's collectives and lax.ppermute only.
A program may use at most 64 MiB of HBM per device.

```python
import jax
import jax.numpy as jnp
from jax import lax

FLUOR = 12
CHAN = 32
TAPS = 33
ITERS = 2
PLANES = 1
NX = 1024
NY = 4096


def draw_measured(key, part):
    key = jax.random.fold_in(key, 7)
    key_dark, key_level, key_tone, key_noise = jax.random.split(key, 4)
    region_cells = 64
    count_x = NX // region_cells + 1
    count_y = NY // region_cells + 1
    dark = jax.random.randint(key_dark, (PLANES, count_x, count_y), 0, 2).astype(jnp.float32)
    region_x = jnp.arange(NX) // region_cells
    region_y = jnp.arange(NY) // region_cells
    tone = jax.random.uniform(key_tone, (CHAN,), jnp.float32, 0.5, 1.5)
    bright = jax.random.uniform(key_level, (PLANES, count_x, count_y), jnp.float32, 1.5, 4.0)
    level = (1.0 - dark) * bright + dark * 0.05
    noise = jax.random.uniform(key_noise, (PLANES, CHAN, NX, NY), jnp.float32, 0.8, 1.2)
    field = level[:, region_x][:, :, region_y]
    values = field[:, None, :, :] * tone[None, :, None, None] * noise
    return values.astype(jnp.bfloat16)


def steps_of(rng, dims, cuts, least, largest):
    loudness = 1.0
    for position, shards_of in cuts:
        heights = jax.random.uniform(jax.random.fold_in(jax.random.fold_in(rng, 6), position), (shards_of,), jnp.float32, least / len(cuts), largest / len(cuts))
        loudness = loudness * jnp.repeat(jnp.exp(heights), dims[position] // shards_of).reshape((-1,) + (1,) * (len(dims) - 1 - position))
    return loudness


def setup_inputs(seed: int = 0) -> dict:
    key_list = jax.random.split(jax.random.key(seed), 6)
    return {
        "abundance_start": jnp.clip(1.0 * jax.random.uniform(key_list[0], (PLANES, FLUOR, NX, NY), jnp.float32) ** steps_of(key_list[0], (PLANES, FLUOR, NX, NY), ((2, 16), (3, 32)), -0.2, 0.2), 0.0, 1.0),
        "measured": draw_measured(jax.random.fold_in(key_list[5], 71), 0),
        "spectra": jnp.clip(jax.random.uniform(key_list[2], (CHAN, FLUOR), jnp.float32, 0.02, 0.3), 0.02, 0.3),
        "taps_x": jnp.clip(jax.random.uniform(key_list[3], (TAPS,), jnp.float32, 0.01, 0.05), 0.01, 0.05),
        "taps_y": jnp.clip(jax.random.uniform(key_list[4], (TAPS,), jnp.float32, 0.01, 0.05), 0.01, 0.05),
    }


precise = lax.Precision.HIGHEST
tiny_floor = 1e-6


def smear(planes, profile_x, profile_y):
    margin = TAPS // 2
    stacked = planes[:, None]
    kernel_x = profile_x.reshape(1, 1, -1, 1)
    kernel_y = profile_y.reshape(1, 1, 1, -1)
    along_x = lax.conv_general_dilated(stacked, kernel_x, (1, 1), ((margin, margin), (0, 0)), precision=precise)
    along_y = lax.conv_general_dilated(along_x, kernel_y, (1, 1), ((0, 0), (margin, margin)), precision=precise)
    return along_y[:, 0]


def reference(abundance_start, measured, spectra, taps_x, taps_y):
    flipped_x = taps_x[::-1]
    flipped_y = taps_y[::-1]

    def forward_plane(plane):
        return smear(plane, taps_x, taps_y)

    def adjoint_plane(pair):
        image, observed = pair
        mixed_image = jnp.einsum('cf,fxy->cxy', spectra, image, precision=precise)
        misfit = mixed_image - observed.astype(jnp.float32)
        projected = jnp.einsum('cf,cxy->fxy', spectra, misfit, precision=precise)
        return smear(projected, flipped_x, flipped_y)

    def probe_plane(plane):
        probe_image = jnp.einsum('cf,fxy->cxy', spectra, smear(plane, taps_x, taps_y), precision=precise)
        return jnp.sum(probe_image * probe_image)

    abundance = abundance_start
    for iteration in range(ITERS):
        blurred = lax.map(forward_plane, abundance)
        gradient = lax.map(adjoint_plane, (blurred, measured))
        grad_sq = jnp.sum(gradient * gradient)
        image_sq = jnp.sum(lax.map(probe_plane, gradient))
        step_length = grad_sq / (image_sq + tiny_floor)
        abundance = jnp.maximum(abundance - step_length * gradient, 0.0)
    return abundance
```

```python
import functools

import jax
import jax.numpy as jnp
from jax import lax
from jax.experimental import pallas as pl
from jax.experimental.pallas import tpu as pltpu
from jax.sharding import Mesh
from jax.sharding import PartitionSpec as P

TAPS = 33
ITERS = 2
FLUOR = 12
CHAN = 32
ROWS = 64
COLS = 128

HALF = TAPS // 2
A_HALO = 3 * HALF
P_HALO = 2 * HALF
G_HALO = HALF
A_ROWS = ROWS + 2 * A_HALO
P_ROWS = ROWS + 2 * P_HALO
G_ROWS = ROWS + 2 * G_HALO

GX = ("y", "x_hi", "core")
GY = ("x_lo", "z")
NEAR = ("y", "x_hi", "core", "x_lo")
FAR = "z"

tiny_floor = 1e-06
f32 = jnp.float32
bf16 = jnp.bfloat16


def smem():
    return pl.BlockSpec(memory_space=pltpu.SMEM)


def vmem():
    return pl.BlockSpec(memory_space=pltpu.VMEM)


def kernel(body, ins, outs, cost, scratch=()):
    return pl.pallas_call(
        body,
        in_specs=[smem() if kind == "s" else vmem() for kind in ins],
        out_specs=[vmem() for _ in outs],
        out_shape=[jax.ShapeDtypeStruct(shape, dtype) for shape, dtype in outs],
        scratch_shapes=list(scratch),
        compiler_params=pltpu.CompilerParams(vmem_limit_bytes=32 * 2**20),
        cost_estimate=pl.CostEstimate(flops=cost, bytes_accessed=cost // 100, transcendentals=0),
    )


def roll(x, by):
    by = by % 128
    return x if by == 0 else pltpu.roll(x, by, axis=x.ndim - 1)


def lane_of(shape):
    return lax.broadcasted_iota(jnp.int32, shape, len(shape) - 1)


def split(x):
    high = x.astype(bf16)
    return high, (x - high.astype(f32)).astype(bf16)


def dot(a, b):
    return jnp.dot(a, b, preferred_element_type=f32)


def dot_right(x, high, low):
    x_high, x_low = split(x)
    return dot(x_high, high) + dot(x_low, high) + dot(x_high, low)


def stacked(x, depth):
    high, low = split(x)
    parts = [high, low, high]
    spare = depth - 3 * x.shape[0]
    if spare:
        parts.append(jnp.zeros((spare, x.shape[1]), bf16))
    return jnp.concatenate(parts, axis=0)


def side_position(index, halo):
    left = index - COLS - halo
    right = index - halo
    position = jnp.where(index < COLS, index, jnp.where(index < COLS + halo, left, right))
    return jnp.where(index < COLS + 2 * halo, position, 1 << 20)


def tap_matrix(taps_ref, offset):
    out = jnp.zeros(offset.shape, f32)
    for t in range(TAPS):
        out = jnp.where(offset == t, taps_ref[t], out)
    return out


def inside(position, base, size):
    where = position + base
    return jnp.logical_and(where >= 0, where < size)


def exact_dot(a, b):
    return lax.dot_general(a, b, (((1,), (0,)), ((), ())), precision=lax.Precision.HIGHEST, preferred_element_type=f32)


def rows_cols(shape):
    return lax.broadcasted_iota(jnp.int32, shape, 0), lax.broadcasted_iota(jnp.int32, shape, 1)


def put_pair(x, high_ref, low_ref):
    high, low = split(x)
    high_ref[...] = high
    low_ref[...] = low


def put_left(x, part, ref):
    high, low = split(x)
    ref[...] = jnp.where(part < 2, high.astype(f32), low.astype(f32)).astype(bf16)


def matrices_body(sizes, at_ref, tx_ref, ty_ref, myh, myl, pyh, pyl, byh, byl, mx, px, bx):
    size_x, size_y = sizes
    base_x = at_ref[0] * ROWS
    base_y = at_ref[1] * COLS
    r, c = rows_cols((256, 256))
    source = side_position(r, P_HALO)
    target = side_position(c, G_HALO)
    okay = jnp.logical_and(inside(source, base_y, size_y), inside(target, base_y, size_y))
    put_pair(jnp.where(okay, tap_matrix(ty_ref, target - source + HALF), 0.0), pyh, pyl)
    source = side_position(r, A_HALO)
    middle = c - P_HALO
    okay = jnp.logical_and(inside(source, base_y, size_y), inside(middle, base_y, size_y))
    first = jnp.where(okay, tap_matrix(ty_ref, source - middle + HALF), 0.0)
    middle = r - P_HALO
    second = jnp.where(inside(target, base_y, size_y), tap_matrix(ty_ref, target - middle + HALF), 0.0)
    put_pair(exact_dot(first, second), myh, myl)
    r, c = rows_cols((256, 128))
    source = side_position(r, G_HALO)
    okay = inside(source, base_y, size_y)
    put_pair(jnp.where(okay, tap_matrix(ty_ref, source - c + HALF), 0.0), byh, byl)
    r, c = rows_cols((128, 512))
    part = c // A_ROWS
    source = c - part * A_ROWS - A_HALO
    middle = r - P_HALO
    okay = jnp.logical_and(inside(source, base_x, size_x), inside(middle, base_x, size_x))
    okay = jnp.logical_and(okay, part < 3)
    first = jnp.where(okay, tap_matrix(tx_ref, source - middle + HALF), 0.0)
    r, c = rows_cols((G_ROWS, 128))
    target = r - G_HALO
    middle = c - P_HALO
    second = jnp.where(inside(target, base_x, size_x), tap_matrix(tx_ref, target - middle + HALF), 0.0)
    r, c = rows_cols((G_ROWS, 512))
    put_left(exact_dot(second, first), c // A_ROWS, mx)
    r, c = rows_cols((G_ROWS, 384))
    part = c // P_ROWS
    source = c - part * P_ROWS - P_HALO
    target = r - G_HALO
    okay = jnp.logical_and(inside(source, base_x, size_x), inside(target, base_x, size_x))
    put_left(jnp.where(okay, tap_matrix(tx_ref, target - source + HALF), 0.0), part, px)
    r, c = rows_cols((ROWS, 384))
    part = c // G_ROWS
    source = c - part * G_ROWS - G_HALO
    okay = jnp.logical_and(inside(source, base_x, size_x), part < 3)
    put_left(jnp.where(okay, tap_matrix(tx_ref, source - r + HALF), 0.0), part, bx)


def project_body(spectra_ref, a_ref, m_ref, p_ref, left_ref, right_ref):
    step = 16
    for start in range(0, ROWS, step):
        acc = [jnp.zeros((step, COLS), f32) for _ in range(FLUOR)]
        for c in range(CHAN):
            seen = m_ref[c, start : start + step, :].astype(f32)
            for f in range(FLUOR):
                acc[f] = acc[f] + spectra_ref[c, f] * seen
        for f in range(FLUOR):
            p_ref[f, start : start + step, :] = acc[f]
    lane = lane_of((32, 128))
    lane8 = lane_of((8, 128))
    for f in range(FLUOR):
        for ref, a_from, p_from in ((left_ref, 0, 0), (right_ref, COLS - A_HALO, COLS - P_HALO)):
            top = roll(a_ref[f, :32, :], -a_from)
            low = roll(a_ref[f, 32:, :], A_HALO - a_from)
            side = roll(p_ref[f, :32, :], 2 * A_HALO - p_from)
            ref[f, :32, :] = jnp.where(lane < A_HALO, top, jnp.where(lane < 2 * A_HALO, low, side))
            rest = roll(p_ref[f, 32:40, :], -p_from)
            for k in range(1, 4):
                piece = roll(p_ref[f, 32 + 8 * k : 40 + 8 * k, :], 32 * k - p_from)
                rest = jnp.where(lane8 < 32 * k, rest, piece)
            ref[f, 32:, :] = rest


def widen_body(a_ref, p_ref, left_ref, right_ref, pyh, pyl, side_ref, w_ref, up_ref, down_ref, ps_ref):
    lane = lane_of((32, 128))
    lane8 = lane_of((8, 128))
    for f in range(FLUOR):
        left = left_ref[f, :32, :]
        right = right_ref[f, :32, :]
        side_ref[f, :32, :] = jnp.where(
            lane < A_HALO, left, jnp.where(lane < 2 * A_HALO, roll(right, A_HALO), 0.0)
        )
        side_ref[f, 32:, :] = jnp.where(
            lane < A_HALO, roll(left, -A_HALO), jnp.where(lane < 2 * A_HALO, right, 0.0)
        )
        ps_ref[:32, :] = jnp.where(
            lane < P_HALO, roll(left, -2 * A_HALO), jnp.where(lane < 2 * P_HALO, roll(right, P_HALO - 2 * A_HALO), 0.0)
        )
        left = left_ref[f, 32:, :]
        right = right_ref[f, 32:, :]
        for k in range(4):
            ps_ref[32 + 8 * k : 40 + 8 * k, :] = jnp.where(
                lane8 < P_HALO, roll(left, -32 * k), jnp.where(lane8 < 2 * P_HALO, roll(right, P_HALO - 32 * k), 0.0)
            )
        w = dot_right(jnp.concatenate([p_ref[f], ps_ref[...]], axis=1), pyh[...], pyl[...])
        w_ref[f] = w
        for ref, a_from, w_from in ((up_ref, 0, 0), (down_ref, ROWS - A_HALO, ROWS - P_HALO)):
            ref[f, :A_HALO, :] = a_ref[f, a_from : a_from + A_HALO, :]
            ref[f, A_HALO : 2 * A_HALO, :] = side_ref[f, a_from : a_from + A_HALO, :]
            w_side = roll(w[w_from : w_from + P_HALO, COLS:], 2 * A_HALO)
            ref[f, A_HALO : A_HALO + P_HALO, :] = jnp.where(
                lane < 2 * A_HALO, side_ref[f, a_from : a_from + P_HALO, :], w_side
            )
            ref[f, 2 * A_HALO :, :] = w[w_from : w_from + P_HALO, :COLS]


def gradient(f, abundance, myh, myl, mx, v_ref):
    u = dot_right(abundance, myh[...], myl[...])
    v_ref[f] = dot(mx[...], stacked(u, 512))


def mix(gram_ref, v_ref, d_ref, g_ref):
    step = 8
    for start in range(0, G_ROWS, step):
        part = [v_ref[f, start : start + step, :] for f in range(FLUOR)]
        for f in range(FLUOR):
            acc = -d_ref[f, start : start + step, :]
            for k in range(FLUOR):
                acc = acc + gram_ref[f, k] * part[k]
            g_ref[f, start : start + step, :] = acc


def sums(gram_ref, g_ref, byh, byl, bx, z_ref, sum_ref):
    for f in range(FLUOR):
        y = dot(bx[...], stacked(g_ref[f], 384))
        z_ref[f] = dot_right(y, byh[...], byl[...])
    grad = jnp.zeros((8, 128), f32)
    image = jnp.zeros((8, 128), f32)
    for start in range(0, ROWS, 8):
        part = [z_ref[f, start : start + 8, :] for f in range(FLUOR)]
        for f in range(FLUOR):
            acc = gram_ref[f, 0] * part[0]
            for k in range(1, FLUOR):
                acc = acc + gram_ref[f, k] * part[k]
            image = image + acc * part[f]
            g = g_ref[f, G_HALO + start : G_HALO + start + 8, :COLS]
            grad = grad + g * g
    grad = jnp.sum(grad, axis=0, keepdims=True)
    image = jnp.sum(image, axis=0, keepdims=True)
    lane = lane_of((1, 128))
    sum_ref[...] = jnp.where(lane < 64, grad + roll(grad, 64), image + roll(image, 64))


def step_length(total_ref):
    total = jnp.sum(total_ref[...], axis=0, keepdims=True)
    lane = lane_of((1, 128))
    grad = jnp.sum(jnp.where(lane < 64, total, 0.0), axis=1, keepdims=True)
    image = jnp.sum(jnp.where(lane < 64, 0.0, total), axis=1, keepdims=True)
    return grad / (image + tiny_floor)


def first_body(
    gram_ref, a_ref, side_ref, w_ref, above_ref, below_ref, myh, myl, mx, px,
    ext_ref, d_ref, g_ref, left_ref, right_ref, v_ref, we_ref,
):
    lane = lane_of((P_HALO, 128))
    for f in range(FLUOR):
        top = slice(0, A_HALO)
        mid = slice(A_HALO, A_HALO + ROWS)
        low = slice(A_HALO + ROWS, A_ROWS)
        ext_ref[f, top, :COLS] = above_ref[f, :A_HALO, :]
        ext_ref[f, mid, :COLS] = a_ref[f]
        ext_ref[f, low, :COLS] = below_ref[f, :A_HALO, :]
        ext_ref[f, top, COLS:] = above_ref[f, A_HALO : 2 * A_HALO, :]
        ext_ref[f, mid, COLS:] = side_ref[f]
        ext_ref[f, low, COLS:] = below_ref[f, A_HALO : 2 * A_HALO, :]
        for ref, at in ((above_ref, 0), (below_ref, P_HALO + ROWS)):
            we_ref[at : at + P_HALO, :COLS] = ref[f, 2 * A_HALO :, :]
            w_side = roll(ref[f, A_HALO : A_HALO + P_HALO, :], -2 * A_HALO)
            we_ref[at : at + P_HALO, COLS:] = jnp.where(lane < 2 * G_HALO, w_side, 0.0)
        we_ref[P_HALO : P_HALO + ROWS, :] = w_ref[f]
        d_ref[f] = dot(px[...], stacked(we_ref[...], 384))
        gradient(f, ext_ref[f], myh, myl, mx, v_ref)
    mix(gram_ref, v_ref, d_ref, g_ref)
    lane = lane_of((24, 128))
    for f in range(FLUOR):
        for ref, start in ((left_ref, G_HALO), (right_ref, COLS - G_HALO - 32)):
            out = roll(g_ref[f, :24, :COLS], -start)
            for k in range(1, 4):
                piece = roll(g_ref[f, 24 * k : 24 * k + 24, :COLS], 32 * k - start)
                out = jnp.where(lane < 32 * k, out, piece)
            ref[f] = out


def probe_body(gram_ref, g_ref, byh, byl, bx, sum_ref, z_ref):
    sums(gram_ref, g_ref, byh, byl, bx, z_ref, sum_ref)


def outer_body(g_ref, left_ref, right_ref, side_ref, send_ref):
    lane = lane_of((24, 128))
    for f in range(FLUOR):
        for k in range(4):
            own = roll(g_ref[f, 24 * k : 24 * k + 24, COLS:], 32)
            left = roll(left_ref[f], -32 * k)
            right = roll(right_ref[f], 64 - 32 * k)
            side_ref[f, 24 * k : 24 * k + 24, :] = jnp.where(
                lane < 32, left, jnp.where(lane < 64, own, jnp.where(lane < 96, right, 0.0))
            )
        send_ref[f, :32, :] = g_ref[f, 2 * G_HALO : 2 * G_HALO + 32, :COLS]
        send_ref[f, 32:, :] = side_ref[f, 2 * G_HALO : 2 * G_HALO + 32, :]


def second_body(
    gram_ref, total_ref, ext_ref, d_ref, g_ref, side_ref, above_ref, below_ref, myh, myl, mx, byh, byl, bx,
    a_out, g_out, sum_ref, v_ref, n_ref, z_ref, x_ref,
):
    t = step_length(total_ref)
    for f in range(FLUOR):
        for rows, main, side in (
            (slice(0, 32), above_ref[f, :32, :], above_ref[f, 32:, :]),
            (slice(32, 32 + G_ROWS), g_ref[f, :, :COLS], side_ref[f]),
            (slice(32 + G_ROWS, A_ROWS), below_ref[f, :32, :], below_ref[f, 32:, :]),
        ):
            x_ref[rows, :COLS] = jnp.maximum(ext_ref[f, rows, :COLS] - t * main, 0.0)
            x_ref[rows, COLS:] = jnp.maximum(ext_ref[f, rows, COLS:] - t * side, 0.0)
        a_out[f] = x_ref[A_HALO : A_HALO + ROWS, :COLS]
        gradient(f, x_ref[...], myh, myl, mx, v_ref)
    mix(gram_ref, v_ref, d_ref, n_ref)
    sums(gram_ref, n_ref, byh, byl, bx, z_ref, sum_ref)
    for f in range(FLUOR):
        g_out[f] = n_ref[f, G_HALO : G_HALO + ROWS, :COLS]


def last_body(total_ref, a_ref, g_ref, out_ref):
    t = step_length(total_ref)
    for f in range(FLUOR):
        out_ref[f] = jnp.maximum(a_ref[f] - t * g_ref[f], 0.0)


def both_ways(to_low, to_high, axes):
    count = 1
    for axis in axes:
        count *= lax.axis_size(axis)
    up = [(i, (i + 1) % count) for i in range(count)]
    down = [(i, (i - 1) % count) for i in range(count)]
    return lax.ppermute(to_high, axes, up), lax.ppermute(to_low, axes, down)


def spread(row, axes):
    names = axes if isinstance(axes, tuple) else (axes,)
    count = 1
    for axis in names:
        count *= lax.axis_size(axis)
    sent = jnp.broadcast_to(row.reshape(1, 1, 128), (count, 1, 128))
    return lax.all_to_all(sent, axes, 0, 0, tiled=True)


def local(sizes, abundance_start, measured, spectra, taps_x, taps_y):
    a0 = abundance_start[0]
    at = jnp.stack([lax.axis_index(GX), lax.axis_index(GY)]).astype(jnp.int32)
    wide = (256, 256)
    half = (256, 128)
    tile = (FLUOR, ROWS, COLS)

    p, left, right = kernel(
        project_body, "svv", [(tile, f32)] + [((FLUOR, 40, 128), f32)] * 2, 10**8
    )(spectra, a0, measured[0])
    from_left, from_right = both_ways(left, right, GY)
    gram = jnp.einsum("cf,cg->fg", spectra, spectra, precision=lax.Precision.HIGHEST)
    myh, myl, pyh, pyl, byh, byl, mx, px, bx = kernel(
        functools.partial(matrices_body, sizes),
        "sss",
        [(wide, bf16)] * 4 + [(half, bf16)] * 2
        + [((G_ROWS, 512), bf16), ((G_ROWS, 384), bf16), ((ROWS, 384), bf16)],
        10**9,
    )(at, taps_x, taps_y)
    side, w, up, down = kernel(
        widen_body,
        "vvvvvv",
        [(tile, f32), ((FLUOR, ROWS, 256), f32)] + [((FLUOR, 128, 128), f32)] * 2,
        10**8,
        [pltpu.VMEM((ROWS, 128), f32)],
    )(a0, p, from_left, from_right, pyh, pyl)
    from_above, from_below = both_ways(up, down, GX)
    ext, d, g, left, right = kernel(
        first_body,
        "s" + "v" * 9,
        [((FLUOR, A_ROWS, 256), f32)] + [((FLUOR, G_ROWS, 256), f32)] * 2 + [((FLUOR, 24, 128), f32)] * 2,
        10**9,
        [pltpu.VMEM((FLUOR, G_ROWS, 256), f32), pltpu.VMEM((P_ROWS, 256), f32)],
    )(gram, a0, side, w, from_above, from_below, myh, myl, mx, px)
    from_left, from_right = both_ways(left, right, GY)
    (partial,) = kernel(probe_body, "svvvv", [((1, 128), f32)], 10**9, [pltpu.VMEM(tile, f32)])(
        gram, g, byh, byl, bx
    )
    near = jnp.sum(spread(partial, NEAR), axis=0)
    g_side, send = kernel(
        outer_body, "vvv", [((FLUOR, G_ROWS, 128), f32), ((FLUOR, 64, 128), f32)], 10**8
    )(g, from_left, from_right)
    from_above, from_below = both_ways(send, send, GX)
    total = spread(near, FAR)
    a1, g1, partial = kernel(
        second_body,
        "s" + "v" * 13,
        [(tile, f32)] * 2 + [((1, 128), f32)],
        10**9,
        [
            pltpu.VMEM((FLUOR, G_ROWS, 256), f32),
            pltpu.VMEM((FLUOR, G_ROWS, 256), f32),
            pltpu.VMEM(tile, f32),
            pltpu.VMEM((A_ROWS, 256), f32),
        ],
    )(gram, total.reshape(-1, 128), ext, d, g, g_side, from_above, from_below, myh, myl, mx, byh, byl, bx)
    near = jnp.sum(spread(partial, NEAR), axis=0)
    total = spread(near, FAR)
    (out,) = kernel(last_body, "vvv", [(tile, f32)], 10**7)(total.reshape(-1, 128), a1, g1)
    return out[None]


def solution(mesh):
    count_x, count_y = mesh.shape["gx"], mesh.shape["gy"]
    parts = Mesh(
        mesh.devices.reshape(count_x // 4, 2, 2, 2, count_y // 2), ("y", "x_hi", "core", "x_lo", "z")
    )
    sizes = (count_x * ROWS, count_y * COLS)
    tiles = P(None, None, GX, GY)
    return jax.shard_map(
        functools.partial(local, sizes),
        mesh=parts,
        in_specs=(tiles, tiles, P(), P(), P()),
        out_specs=tiles,
        check_vma=False,
    )
```

```python
import functools

import jax
import jax.numpy as jnp
from jax import lax
from jax.experimental import pallas as pl
from jax.experimental.pallas import tpu as pltpu
from jax.sharding import Mesh
from jax.sharding import PartitionSpec as P

TAPS = 33
ITERS = 2
FLUOR = 12
CHAN = 32
ROWS = 64
COLS = 128

HALF = TAPS // 2
A_HALO = 3 * HALF
P_HALO = 2 * HALF
G_HALO = HALF
A_ROWS = ROWS + 2 * A_HALO
P_ROWS = ROWS + 2 * P_HALO
G_ROWS = ROWS + 2 * G_HALO

GX = ("y", "x_hi", "core")
GY = ("x_lo", "z")
NEAR = ("y", "x_hi", "core", "x_lo")
FAR = "z"

tiny_floor = 1e-06
f32 = jnp.float32
bf16 = jnp.bfloat16


SPACES = {"s": pltpu.SMEM, "v": pltpu.VMEM, "a": pl.ANY}


def kernel(body, ins, outs, cost, scratch=()):
    return pl.pallas_call(
        body,
        in_specs=[pl.BlockSpec(memory_space=SPACES[kind]) for kind in ins],
        out_specs=[pl.BlockSpec(memory_space=pltpu.VMEM) for _ in outs],
        out_shape=[jax.ShapeDtypeStruct(shape, dtype) for shape, dtype in outs],
        scratch_shapes=list(scratch),
        compiler_params=pltpu.CompilerParams(vmem_limit_bytes=32 * 2**20),
        cost_estimate=pl.CostEstimate(flops=cost, bytes_accessed=cost // 100, transcendentals=0),
    )


def roll(x, by):
    by = by % 128
    return x if by == 0 else pltpu.roll(x, by, axis=x.ndim - 1)


def lane_of(shape):
    return lax.broadcasted_iota(jnp.int32, shape, len(shape) - 1)


def split(x):
    high = x.astype(bf16)
    return high, (x - high.astype(f32)).astype(bf16)


def dot(a, b):
    return jnp.dot(a, b, preferred_element_type=f32)


def dot_right(x, high, low):
    x_high, x_low = split(x)
    return dot(x_high, high) + dot(x_low, high) + dot(x_high, low)


def stacked(x, depth):
    high, low = split(x)
    parts = [high, low, high]
    spare = depth - 3 * x.shape[0]
    if spare:
        parts.append(jnp.zeros((spare, x.shape[1]), bf16))
    return jnp.concatenate(parts, axis=0)


def side_position(index, halo):
    left = index - COLS - halo
    right = index - halo
    position = jnp.where(index < COLS, index, jnp.where(index < COLS + halo, left, right))
    return jnp.where(index < COLS + 2 * halo, position, 1 << 20)


def tap_matrix(taps_ref, offset):
    out = jnp.zeros(offset.shape, f32)
    for t in range(TAPS):
        out = jnp.where(offset == t, taps_ref[t], out)
    return out


def inside(position, base, size):
    where = position + base
    return jnp.logical_and(where >= 0, where < size)


def exact_dot(a, b):
    return lax.dot_general(a, b, (((1,), (0,)), ((), ())), precision=lax.Precision.HIGHEST, preferred_element_type=f32)


def rows_cols(shape):
    return lax.broadcasted_iota(jnp.int32, shape, 0), lax.broadcasted_iota(jnp.int32, shape, 1)


def put_pair(x, high_ref, low_ref):
    high, low = split(x)
    high_ref[...] = high
    low_ref[...] = low


def put_left(x, part, ref):
    high, low = split(x)
    ref[...] = jnp.where(part < 2, high.astype(f32), low.astype(f32)).astype(bf16)


def matrices_body(sizes, at_ref, tx_ref, ty_ref, spectra_ref, gram_ref, myh, myl, pyh, pyl, byh, byl, mx, px, bx):
    spectra = spectra_ref[...]
    gram_ref[...] = lax.dot_general(
        spectra, spectra, (((1,), (1,)), ((), ())), precision=lax.Precision.HIGHEST, preferred_element_type=f32
    )
    size_x, size_y = sizes
    base_x = at_ref[0] * ROWS
    base_y = at_ref[1] * COLS
    r, c = rows_cols((256, 256))
    source = side_position(r, P_HALO)
    target = side_position(c, G_HALO)
    okay = jnp.logical_and(inside(source, base_y, size_y), inside(target, base_y, size_y))
    put_pair(jnp.where(okay, tap_matrix(ty_ref, target - source + HALF), 0.0), pyh, pyl)
    source = side_position(r, A_HALO)
    middle = c - P_HALO
    okay = jnp.logical_and(inside(source, base_y, size_y), inside(middle, base_y, size_y))
    first = jnp.where(okay, tap_matrix(ty_ref, source - middle + HALF), 0.0)
    middle = r - P_HALO
    second = jnp.where(inside(target, base_y, size_y), tap_matrix(ty_ref, target - middle + HALF), 0.0)
    put_pair(exact_dot(first, second), myh, myl)
    r, c = rows_cols((256, 128))
    source = side_position(r, G_HALO)
    okay = inside(source, base_y, size_y)
    put_pair(jnp.where(okay, tap_matrix(ty_ref, source - c + HALF), 0.0), byh, byl)
    r, c = rows_cols((128, 512))
    part = c // A_ROWS
    source = c - part * A_ROWS - A_HALO
    middle = r - P_HALO
    okay = jnp.logical_and(inside(source, base_x, size_x), inside(middle, base_x, size_x))
    okay = jnp.logical_and(okay, part < 3)
    first = jnp.where(okay, tap_matrix(tx_ref, source - middle + HALF), 0.0)
    r, c = rows_cols((G_ROWS, 128))
    target = r - G_HALO
    middle = c - P_HALO
    second = jnp.where(inside(target, base_x, size_x), tap_matrix(tx_ref, target - middle + HALF), 0.0)
    r, c = rows_cols((G_ROWS, 512))
    put_left(exact_dot(second, first), c // A_ROWS, mx)
    r, c = rows_cols((G_ROWS, 384))
    part = c // P_ROWS
    source = c - part * P_ROWS - P_HALO
    target = r - G_HALO
    okay = jnp.logical_and(inside(source, base_x, size_x), inside(target, base_x, size_x))
    put_left(jnp.where(okay, tap_matrix(tx_ref, target - source + HALF), 0.0), part, px)
    r, c = rows_cols((ROWS, 384))
    part = c // G_ROWS
    source = c - part * G_ROWS - G_HALO
    okay = jnp.logical_and(inside(source, base_x, size_x), part < 3)
    put_left(jnp.where(okay, tap_matrix(tx_ref, source - r + HALF), 0.0), part, bx)


def choose(odd, if_odd, if_even):
    return jnp.where(odd == 1, if_odd, if_even)


def project_body(at_ref, spectra_ref, a_any, m_any, p_ref, ya_ref, yb_ref, xa_ref, xb_ref, a_ref, m_ref, sems):
    step = 16
    copies = [
        pltpu.make_async_copy(m_any.at[:, pl.ds(k * step, step), :], m_ref.at[:, pl.ds(k * step, step), :], sems.at[k])
        for k in range(ROWS // step)
    ]
    for copy in copies:
        copy.start()
    copy_a = pltpu.make_async_copy(a_any, a_ref, sems.at[ROWS // step])
    copy_a.start()
    for k, copy in enumerate(copies):
        copy.wait()
        start = k * step
        acc = [jnp.zeros((step, COLS), f32) for _ in range(FLUOR)]
        for c in range(CHAN):
            seen = m_ref[c, start : start + step, :].astype(f32)
            for f in range(FLUOR):
                acc[f] = acc[f] + spectra_ref[f, c] * seen
        for f in range(FLUOR):
            p_ref[f, start : start + step, :] = acc[f]
    copy_a.wait()
    odd_x = at_ref[0] % 2
    odd_y = at_ref[1] % 2
    for ref, top in ((xa_ref, odd_x == 1), (xb_ref, odd_x == 0)):
        a_from = pl.multiple_of(jnp.where(top, 0, ROWS - A_HALO), 16)
        p_from = pl.multiple_of(jnp.where(top, 0, ROWS - P_HALO), 16)
        for f in range(FLUOR):
            ref[f, :A_HALO, :] = a_ref[f, pl.ds(a_from, A_HALO), :]
            ref[f, A_HALO:, :] = p_ref[f, pl.ds(p_from, P_HALO), :]
    lane = lane_of((32, 128))
    lane8 = lane_of((8, 128))
    for f in range(FLUOR):
        edges = []
        for a_from, p_from in ((0, 0), (COLS - A_HALO, COLS - P_HALO)):
            top = roll(a_ref[f, :32, :], -a_from)
            low = roll(a_ref[f, 32:, :], A_HALO - a_from)
            side = roll(p_ref[f, :32, :], 2 * A_HALO - p_from)
            main = jnp.where(lane < A_HALO, top, jnp.where(lane < 2 * A_HALO, low, side))
            rest = roll(p_ref[f, 32:40, :], -p_from)
            for k in range(1, 4):
                piece = roll(p_ref[f, 32 + 8 * k : 40 + 8 * k, :], 32 * k - p_from)
                rest = jnp.where(lane8 < 32 * k, rest, piece)
            edges.append((main, rest))
        (left, left_rest), (right, right_rest) = edges
        ya_ref[f, :32, :] = choose(odd_y, left, right)
        yb_ref[f, :32, :] = choose(odd_y, right, left)
        ya_ref[f, 32:, :] = choose(odd_y, left_rest, right_rest)
        yb_ref[f, 32:, :] = choose(odd_y, right_rest, left_rest)


def corner_body(at_ref, ya_ref, yb_ref, side_ref, ps_ref, xa_ref, xb_ref):
    odd_x = at_ref[0] % 2
    odd_y = at_ref[1] % 2
    lane = lane_of((32, 128))
    lane8 = lane_of((8, 128))
    for f in range(FLUOR):
        first = ya_ref[f, :32, :]
        second = yb_ref[f, :32, :]
        left = choose(odd_y, first, second)
        right = choose(odd_y, second, first)
        side_ref[f, :32, :] = jnp.where(lane < A_HALO, left, jnp.where(lane < 2 * A_HALO, roll(right, A_HALO), 0.0))
        side_ref[f, 32:, :] = jnp.where(lane < A_HALO, roll(left, -A_HALO), jnp.where(lane < 2 * A_HALO, right, 0.0))
        ps_ref[f, :32, :] = jnp.where(
            lane < P_HALO, roll(left, -2 * A_HALO), jnp.where(lane < 2 * P_HALO, roll(right, P_HALO - 2 * A_HALO), 0.0)
        )
        first = ya_ref[f, 32:, :]
        second = yb_ref[f, 32:, :]
        left = choose(odd_y, first, second)
        right = choose(odd_y, second, first)
        for k in range(4):
            ps_ref[f, 32 + 8 * k : 40 + 8 * k, :] = jnp.where(
                lane8 < P_HALO, roll(left, -32 * k), jnp.where(lane8 < 2 * P_HALO, roll(right, P_HALO - 32 * k), 0.0)
            )
    spare = 2 * A_HALO
    lane16 = lane_of((16, 128))
    for ref, top in ((xa_ref, odd_x == 1), (xb_ref, odd_x == 0)):
        a_from = pl.multiple_of(jnp.where(top, 0, ROWS - A_HALO), 16)
        p_from = pl.multiple_of(jnp.where(top, 0, ROWS - P_HALO), 16)
        for f in range(FLUOR):
            p_top = ps_ref[f, pl.ds(p_from, 32), :]
            a_side = side_ref[f, pl.ds(a_from, A_HALO), :]
            ref[f, :32, :] = jnp.where(lane < spare, a_side[:32], roll(p_top, spare))
            ref[f, 32:48, :] = jnp.where(lane16 < spare, a_side[32:], roll(p_top[:16], spare - P_HALO))
            ref[f, 48:, :] = jnp.where(lane8 < P_HALO, roll(p_top[16:24], -P_HALO), p_top[24:])


def gradient(f, abundance, myh, myl, mx, v_ref):
    u = dot_right(abundance, myh[...], myl[...])
    v_ref[f] = dot(mx[...], stacked(u, 512))


def mix(gram_ref, v_ref, d_ref, g_ref):
    step = 8
    for start in range(0, G_ROWS, step):
        part = [v_ref[f, start : start + step, :] for f in range(FLUOR)]
        for f in range(FLUOR):
            acc = -d_ref[f, start : start + step, :]
            for k in range(FLUOR):
                acc = acc + gram_ref[f, k] * part[k]
            g_ref[f, start : start + step, :] = acc


def sums(gram_ref, g_ref, byh, byl, bx, z_ref, sum_ref):
    for f in range(FLUOR):
        y = dot(bx[...], stacked(g_ref[f], 384))
        z_ref[f] = dot_right(y, byh[...], byl[...])
    grad = jnp.zeros((8, 128), f32)
    image = jnp.zeros((8, 128), f32)
    for start in range(0, ROWS, 8):
        part = [z_ref[f, start : start + 8, :] for f in range(FLUOR)]
        for f in range(FLUOR):
            acc = gram_ref[f, 0] * part[0]
            for k in range(1, FLUOR):
                acc = acc + gram_ref[f, k] * part[k]
            image = image + acc * part[f]
            g = g_ref[f, G_HALO + start : G_HALO + start + 8, :COLS]
            grad = grad + g * g
    grad = jnp.sum(grad, axis=0, keepdims=True)
    image = jnp.sum(image, axis=0, keepdims=True)
    lane = lane_of((1, 128))
    row = jnp.where(lane < 64, grad + roll(grad, 64), image + roll(image, 64))
    sum_ref[...] = jnp.broadcast_to(row, sum_ref.shape)


def step_length(total_ref):
    total = jnp.sum(total_ref[...], axis=0, keepdims=True)
    lane = lane_of((1, 128))
    grad = jnp.sum(jnp.where(lane < 64, total, 0.0), axis=1, keepdims=True)
    image = jnp.sum(jnp.where(lane < 64, 0.0, total), axis=1, keepdims=True)
    return grad / (image + tiny_floor)


def first_body(
    at_ref, gram_ref, a_ref, side_ref, p_ref, ps_ref, xa_ref, xb_ref, ca_ref, cb_ref, myh, myl, pyh, pyl, mx, px,
    ext_ref, d_ref, g_ref, ya_ref, yb_ref, v_ref, pe_ref,
):
    odd_x = at_ref[0] % 2
    odd_y = at_ref[1] % 2
    lane = lane_of((32, 128))
    lane16 = lane_of((16, 128))
    lane8 = lane_of((8, 128))
    spare = 2 * A_HALO
    sources = ((xa_ref, ca_ref, odd_x == 1), (xb_ref, cb_ref, odd_x == 0))
    for f in range(FLUOR):
        mid = slice(A_HALO, A_HALO + ROWS)
        ext_ref[f, mid, :COLS] = a_ref[f]
        ext_ref[f, mid, COLS:] = side_ref[f]
        mid = slice(P_HALO, P_HALO + ROWS)
        pe_ref[mid, :COLS] = p_ref[f]
        pe_ref[mid, COLS:] = ps_ref[f]
        for main, corner, above in sources:
            a_at = pl.multiple_of(jnp.where(above, 0, A_HALO + ROWS), 16)
            p_at = jnp.where(above, 0, P_HALO + ROWS)
            ext_ref[f, pl.ds(a_at, A_HALO), :COLS] = main[f, :A_HALO, :]
            ext_ref[f, pl.ds(a_at, A_HALO), COLS:] = corner[f, :A_HALO, :]
            pe_ref[pl.ds(pl.multiple_of(p_at, 16), P_HALO), :COLS] = main[f, A_HALO:, :]
            left = roll(corner[f, :32, :], -spare)
            right = roll(corner[f, 32:48, :], P_HALO - spare)
            pe_ref[pl.ds(pl.multiple_of(p_at, 16), 16), COLS:] = jnp.where(
                lane16 < P_HALO, left[:16], jnp.where(lane16 < 2 * P_HALO, right, 0.0)
            )
            last = corner[f, 48:, :]
            pe_ref[pl.ds(pl.multiple_of(p_at + 16, 16), 8), COLS:] = jnp.where(
                lane8 < P_HALO, left[16:24], jnp.where(lane8 < 2 * P_HALO, roll(last, P_HALO), 0.0)
            )
            pe_ref[pl.ds(pl.multiple_of(p_at + 24, 8), 8), COLS:] = jnp.where(
                lane8 < P_HALO, left[24:], jnp.where(lane8 < 2 * P_HALO, last, 0.0)
            )
        d_ref[f] = dot(px[...], stacked(dot_right(pe_ref[...], pyh[...], pyl[...]), 384))
        gradient(f, ext_ref[f], myh, myl, mx, v_ref)
    mix(gram_ref, v_ref, d_ref, g_ref)
    lane = lane_of((24, 128))
    for f in range(FLUOR):
        edges = []
        for start in (G_HALO, COLS - G_HALO - 32):
            out = roll(g_ref[f, :24, :COLS], -start)
            for k in range(1, 4):
                piece = roll(g_ref[f, 24 * k : 24 * k + 24, :COLS], 32 * k - start)
                out = jnp.where(lane < 32 * k, out, piece)
            edges.append(out)
        ya_ref[f] = choose(odd_y, edges[0], edges[1])
        yb_ref[f] = choose(odd_y, edges[1], edges[0])


def probe_body(gram_ref, g_ref, byh, byl, bx, sum_ref, z_ref):
    sums(gram_ref, g_ref, byh, byl, bx, z_ref, sum_ref)


def relay_body(near_ref, out_ref):
    out_ref[...] = jnp.broadcast_to(jnp.sum(near_ref[...], axis=0, keepdims=True), out_ref.shape)


def outer_body(at_ref, g_ref, ya_ref, yb_ref, side_ref, send_ref):
    odd_y = at_ref[1] % 2
    lane = lane_of((24, 128))
    for f in range(FLUOR):
        left = choose(odd_y, ya_ref[f], yb_ref[f])
        right = choose(odd_y, yb_ref[f], ya_ref[f])
        for k in range(4):
            own = roll(g_ref[f, 24 * k : 24 * k + 24, COLS:], 32)
            side_ref[f, 24 * k : 24 * k + 24, :] = jnp.where(
                lane < 32,
                roll(left, -32 * k),
                jnp.where(lane < 64, own, jnp.where(lane < 96, roll(right, 64 - 32 * k), 0.0)),
            )
        send_ref[f, :32, :] = g_ref[f, 2 * G_HALO : 2 * G_HALO + 32, :COLS]
        send_ref[f, 32:, :] = side_ref[f, 2 * G_HALO : 2 * G_HALO + 32, :]


def second_body(
    at_ref, gram_ref, total_ref, ext_ref, d_ref, g_ref, side_ref, xa_ref, xb_ref, myh, myl, mx, byh, byl, bx,
    a_out, g_out, sum_ref, v_ref, n_ref, z_ref, x_ref,
):
    odd_x = at_ref[0] % 2
    t = step_length(total_ref)
    for f in range(FLUOR):
        mid = slice(32, 32 + G_ROWS)
        x_ref[mid, :COLS] = jnp.maximum(ext_ref[f, mid, :COLS] - t * g_ref[f, :, :COLS], 0.0)
        x_ref[mid, COLS:] = jnp.maximum(ext_ref[f, mid, COLS:] - t * side_ref[f], 0.0)
        for ref, above in ((xa_ref, odd_x == 1), (xb_ref, odd_x == 0)):
            rows = pl.ds(pl.multiple_of(jnp.where(above, 0, 32 + G_ROWS), 16), 32)
            x_ref[rows, :COLS] = jnp.maximum(ext_ref[f, rows, :COLS] - t * ref[f, :32, :], 0.0)
            x_ref[rows, COLS:] = jnp.maximum(ext_ref[f, rows, COLS:] - t * ref[f, 32:, :], 0.0)
        a_out[f] = x_ref[A_HALO : A_HALO + ROWS, :COLS]
        gradient(f, x_ref[...], myh, myl, mx, v_ref)
    mix(gram_ref, v_ref, d_ref, n_ref)
    sums(gram_ref, n_ref, byh, byl, bx, z_ref, sum_ref)
    for f in range(FLUOR):
        g_out[f] = n_ref[f, G_HALO : G_HALO + ROWS, :COLS]


def last_body(total_ref, a_ref, g_ref, out_ref):
    t = step_length(total_ref)
    for f in range(FLUOR):
        out_ref[f] = jnp.maximum(a_ref[f] - t * g_ref[f], 0.0)


def length(axes):
    count = 1
    for axis in axes:
        count *= lax.axis_size(axis)
    return count


def trade(first, second, axes):
    count = length(axes)
    pairs_first = [(i, i ^ 1) for i in range(count)]
    pairs_second = [(i, (i + (1 if i % 2 else -1)) % count) for i in range(count)]
    got_second = lax.ppermute(second, axes, pairs_second)
    return lax.ppermute(first, axes, pairs_first), got_second


def spread(rows, axes):
    got = lax.all_to_all(rows.reshape(rows.shape[0], 1, 128), axes, 0, 0, tiled=True)
    return got.reshape(rows.shape[0], 128)


def local(sizes, abundance_start, measured, spectra, taps_x, taps_y):
    a0 = abundance_start[0]
    at = jnp.stack([lax.axis_index(GX), lax.axis_index(GY)]).astype(jnp.int32)
    wide = (256, 256)
    half = (256, 128)
    tile = (FLUOR, ROWS, COLS)
    near_count, far_count = length(NEAR), length((FAR,))

    p, ya, yb, xa, xb = kernel(
        project_body,
        "ssaa",
        [(tile, f32)] + [((FLUOR, 40, 128), f32)] * 2 + [((FLUOR, A_HALO + P_HALO, 128), f32)] * 2,
        10**8,
        [pltpu.VMEM(tile, f32), pltpu.VMEM((CHAN, ROWS, COLS), bf16), pltpu.SemaphoreType.DMA((5,))],
    )(at, spectra.T, a0, measured[0])
    xa, xb = trade(xa, xb, GX)
    ya, yb = trade(ya, yb, GY)
    gram, myh, myl, pyh, pyl, byh, byl, mx, px, bx = kernel(
        functools.partial(matrices_body, sizes),
        "sssv",
        [((FLUOR, FLUOR), f32)] + [(wide, bf16)] * 4 + [(half, bf16)] * 2
        + [((G_ROWS, 512), bf16), ((G_ROWS, 384), bf16), ((ROWS, 384), bf16)],
        10**9,
    )(at, taps_x, taps_y, spectra.T)
    side, ps, ca, cb = kernel(
        corner_body, "svv", [(tile, f32)] * 2 + [((FLUOR, 56, 128), f32)] * 2, 10**8
    )(at, ya, yb)
    ca, cb = trade(ca, cb, GX)
    ext, d, g, ya, yb = kernel(
        first_body,
        "ss" + "v" * 14,
        [((FLUOR, A_ROWS, 256), f32)] + [((FLUOR, G_ROWS, 256), f32)] * 2 + [((FLUOR, 24, 128), f32)] * 2,
        10**9,
        [pltpu.VMEM((FLUOR, G_ROWS, 256), f32), pltpu.VMEM((P_ROWS, 256), f32)],
    )(at, gram, a0, side, p, ps, xa, xb, ca, cb, myh, myl, pyh, pyl, mx, px)
    ya, yb = trade(ya, yb, GY)
    (partial,) = kernel(probe_body, "svvvv", [((near_count, 128), f32)], 10**9, [pltpu.VMEM(tile, f32)])(
        gram, g, byh, byl, bx
    )
    g_side, send = kernel(
        outer_body, "svvv", [((FLUOR, G_ROWS, 128), f32), ((FLUOR, 64, 128), f32)], 10**8
    )(at, g, ya, yb)
    xa, xb = trade(send, send, GX)
    relay = kernel(relay_body, "v", [((far_count, 128), f32)], 10**6)
    (near,) = relay(spread(partial, NEAR))
    total = spread(near, FAR)
    a1, g1, partial = kernel(
        second_body,
        "ss" + "v" * 13,
        [(tile, f32)] * 2 + [((near_count, 128), f32)],
        10**9,
        [
            pltpu.VMEM((FLUOR, G_ROWS, 256), f32),
            pltpu.VMEM((FLUOR, G_ROWS, 256), f32),
            pltpu.VMEM(tile, f32),
            pltpu.VMEM((A_ROWS, 256), f32),
        ],
    )(at, gram, total, ext, d, g, g_side, xa, xb, myh, myl, mx, byh, byl, bx)
    (near,) = relay(spread(partial, NEAR))
    total = spread(near, FAR)
    (out,) = kernel(last_body, "vvv", [(tile, f32)], 10**7)(total, a1, g1)
    return out[None]


def solution(mesh):
    count_x, count_y = mesh.shape["gx"], mesh.shape["gy"]
    parts = Mesh(
        mesh.devices.reshape(count_x // 4, 2, 2, 2, count_y // 2), ("y", "x_hi", "core", "x_lo", "z")
    )
    sizes = (count_x * ROWS, count_y * COLS)
    tiles = P(None, None, GX, GY)
    return jax.shard_map(
        functools.partial(local, sizes),
        mesh=parts,
        in_specs=(tiles, tiles, P(), P(), P()),
        out_specs=tiles,
        check_vma=False,
    )
```

```python
import functools

import jax
import jax.numpy as jnp
from jax import lax
from jax.experimental import pallas as pl
from jax.experimental.pallas import tpu as pltpu
from jax.sharding import Mesh
from jax.sharding import PartitionSpec as P

TAPS = 33
ITERS = 2
FLUOR = 12
CHAN = 32
ROWS = 64
COLS = 128

HALF = TAPS // 2
A_HALO = 3 * HALF
P_HALO = 2 * HALF
G_HALO = HALF
A_ROWS = ROWS + 2 * A_HALO
P_ROWS = ROWS + 2 * P_HALO
G_ROWS = ROWS + 2 * G_HALO

GX = ("y", "x_hi", "core")
GY = ("x_lo", "z")
NEAR = ("y", "x_hi", "core", "x_lo")
FAR = "z"

tiny_floor = 1e-06
f32 = jnp.float32
bf16 = jnp.bfloat16


SPACES = {"s": pltpu.SMEM, "v": pltpu.VMEM, "h": pltpu.HBM}


def kernel(body, ins, outs, cost, scratch=(), limit=32 * 2**20):
    return pl.pallas_call(
        body,
        in_specs=[pl.BlockSpec(memory_space=SPACES[kind]) for kind in ins],
        out_specs=[pl.BlockSpec(memory_space=pltpu.VMEM) for _ in outs],
        out_shape=[jax.ShapeDtypeStruct(shape, dtype) for shape, dtype in outs],
        scratch_shapes=list(scratch),
        compiler_params=pltpu.CompilerParams(vmem_limit_bytes=limit),
        cost_estimate=pl.CostEstimate(flops=cost, bytes_accessed=cost // 100, transcendentals=0),
    )


def index(axes):
    place = 0
    for axis in axes:
        place = place * lax.axis_size(axis) + lax.axis_index(axis)
    return place


def roll(x, by):
    by = by % 128
    return x if by == 0 else pltpu.roll(x, by, axis=x.ndim - 1)


def lane_of(shape):
    return lax.broadcasted_iota(jnp.int32, shape, len(shape) - 1)


def split(x):
    high = x.astype(bf16)
    return high, (x - high.astype(f32)).astype(bf16)


def dot(a, b):
    return jnp.dot(a, b, preferred_element_type=f32)


def dot_right(x, w):
    high, low = split(x)
    return dot(jnp.concatenate([high, low, high], axis=1), w)


def stacked(x, depth):
    high, low = split(x)
    parts = [high, low, high]
    spare = depth - 3 * x.shape[0]
    if spare:
        parts.append(jnp.zeros((spare, x.shape[1]), bf16))
    return jnp.concatenate(parts, axis=0)


def side_position(index, halo):
    left = index - COLS - halo
    right = index - halo
    position = jnp.where(index < COLS, index, jnp.where(index < COLS + halo, left, right))
    return jnp.where(index < COLS + 2 * halo, position, 1 << 20)


def tap_matrix(taps_ref, offset):
    out = jnp.zeros(offset.shape, f32)
    for t in range(TAPS):
        out = jnp.where(offset == t, taps_ref[t], out)
    return out


def inside(position, base, size):
    where = position + base
    return jnp.logical_and(where >= 0, where < size)


def exact_dot(a, b):
    return lax.dot_general(a, b, (((1,), (0,)), ((), ())), precision=lax.Precision.HIGHEST, preferred_element_type=f32)


def rows_cols(shape):
    return lax.broadcasted_iota(jnp.int32, shape, 0), lax.broadcasted_iota(jnp.int32, shape, 1)


def put_right(x, ref):
    high, low = split(x)
    rows = x.shape[0]
    ref[:rows, :] = high
    ref[rows : 2 * rows, :] = high
    ref[2 * rows :, :] = low


def put_left(x, part, ref):
    high, low = split(x)
    ref[...] = jnp.where(part < 2, high.astype(f32), low.astype(f32)).astype(bf16)


def matrices_body(sizes, tx_ref, ty_ref, spectra_ref, after_ref, gram_ref, my, py, by, mx, px, bx):
    spectra = spectra_ref[...]
    gram_ref[...] = lax.dot_general(
        spectra, spectra, (((1,), (1,)), ((), ())), precision=lax.Precision.HIGHEST, preferred_element_type=f32
    )
    size_x, size_y = sizes
    base_x = index(GX) * ROWS
    base_y = index(GY) * COLS
    r, c = rows_cols((256, 256))
    source = side_position(r, P_HALO)
    target = side_position(c, G_HALO)
    okay = jnp.logical_and(inside(source, base_y, size_y), inside(target, base_y, size_y))
    put_right(jnp.where(okay, tap_matrix(ty_ref, target - source + HALF), 0.0), py)
    source = side_position(r, A_HALO)
    middle = c - P_HALO
    okay = jnp.logical_and(inside(source, base_y, size_y), inside(middle, base_y, size_y))
    first = jnp.where(okay, tap_matrix(ty_ref, source - middle + HALF), 0.0)
    middle = r - P_HALO
    second = jnp.where(inside(target, base_y, size_y), tap_matrix(ty_ref, target - middle + HALF), 0.0)
    put_right(exact_dot(first, second), my)
    r, c = rows_cols((256, 128))
    source = side_position(r, G_HALO)
    okay = inside(source, base_y, size_y)
    put_right(jnp.where(okay, tap_matrix(ty_ref, source - c + HALF), 0.0), by)
    r, c = rows_cols((128, 512))
    part = c // A_ROWS
    source = c - part * A_ROWS - A_HALO
    middle = r - P_HALO
    okay = jnp.logical_and(inside(source, base_x, size_x), inside(middle, base_x, size_x))
    okay = jnp.logical_and(okay, part < 3)
    first = jnp.where(okay, tap_matrix(tx_ref, source - middle + HALF), 0.0)
    r, c = rows_cols((G_ROWS, 128))
    target = r - G_HALO
    middle = c - P_HALO
    second = jnp.where(inside(target, base_x, size_x), tap_matrix(tx_ref, target - middle + HALF), 0.0)
    r, c = rows_cols((G_ROWS, 512))
    put_left(exact_dot(second, first), c // A_ROWS, mx)
    r, c = rows_cols((G_ROWS, 384))
    part = c // P_ROWS
    source = c - part * P_ROWS - P_HALO
    target = r - G_HALO
    okay = jnp.logical_and(inside(source, base_x, size_x), inside(target, base_x, size_x))
    put_left(jnp.where(okay, tap_matrix(tx_ref, target - source + HALF), 0.0), part, px)
    r, c = rows_cols((ROWS, 384))
    part = c // G_ROWS
    source = c - part * G_ROWS - G_HALO
    okay = jnp.logical_and(inside(source, base_x, size_x), part < 3)
    put_left(jnp.where(okay, tap_matrix(tx_ref, source - r + HALF), 0.0), part, bx)


def choose(odd, if_odd, if_even):
    return jnp.where(odd == 1, if_odd, if_even)


def edge_rows(odd_x, pairing, depth):
    top = odd_x == 1 if pairing == 0 else odd_x == 0
    return pl.multiple_of(jnp.where(top, 0, ROWS - depth), 16)


def pack_x(odd_x, pairing, a_ref, p_ref, out_ref):
    a_rows = pl.ds(edge_rows(odd_x, pairing, A_HALO), A_HALO)
    p_rows = pl.ds(edge_rows(odd_x, pairing, P_HALO), P_HALO)
    for f in range(FLUOR):
        out_ref[f, :A_HALO, :] = a_ref[f, a_rows, :]
        out_ref[f, A_HALO:, :] = p_ref[f, p_rows, :]


def project_body(s_hbm, a_hbm, m_hbm, p_ref, xb_ref, xa_ref, ya_ref, yb_ref, spectra_ref, a_ref, m_ref, sems):
    step = 16
    copy_s = pltpu.make_async_copy(s_hbm, spectra_ref, sems.at[5])
    copy_s.start()
    copies = [
        pltpu.make_async_copy(m_hbm.at[:, pl.ds(k * step, step), :], m_ref.at[:, pl.ds(k * step, step), :], sems.at[k])
        for k in range(ROWS // step)
    ]
    for copy in copies:
        copy.start()
    copy_a = pltpu.make_async_copy(a_hbm, a_ref, sems.at[ROWS // step])
    copy_a.start()
    copy_s.wait()
    for k, copy in enumerate(copies):
        copy.wait()
        start = k * step
        acc = [jnp.zeros((step, COLS), f32) for _ in range(FLUOR)]
        for c in range(CHAN):
            seen = m_ref[c, start : start + step, :].astype(f32)
            for f in range(FLUOR):
                acc[f] = acc[f] + spectra_ref[f, c] * seen
        for f in range(FLUOR):
            p_ref[f, start : start + step, :] = acc[f]
    copy_a.wait()
    odd_x = index(GX) % 2
    pack_x(odd_x, 1, a_ref, p_ref, xb_ref)
    pack_x(odd_x, 0, a_ref, p_ref, xa_ref)
    odd_y = index(GY) % 2
    lane = lane_of((32, 128))
    lane8 = lane_of((8, 128))
    for f in range(FLUOR):
        edges = []
        for a_from, p_from in ((0, 0), (COLS - A_HALO, COLS - P_HALO)):
            top = roll(a_ref[f, :32, :], -a_from)
            low = roll(a_ref[f, 32:, :], A_HALO - a_from)
            side = roll(p_ref[f, :32, :], 2 * A_HALO - p_from)
            main = jnp.where(lane < A_HALO, top, jnp.where(lane < 2 * A_HALO, low, side))
            rest = roll(p_ref[f, 32:40, :], -p_from)
            for k in range(1, 4):
                piece = roll(p_ref[f, 32 + 8 * k : 40 + 8 * k, :], 32 * k - p_from)
                rest = jnp.where(lane8 < 32 * k, rest, piece)
            edges.append((main, rest))
        (left, left_rest), (right, right_rest) = edges
        ya_ref[f, :32, :] = choose(odd_y, left, right)
        yb_ref[f, :32, :] = choose(odd_y, right, left)
        ya_ref[f, 32:, :] = choose(odd_y, left_rest, right_rest)
        yb_ref[f, 32:, :] = choose(odd_y, right_rest, left_rest)


def pack_corner(odd_x, pairing, side_ref, ps_ref, out_ref):
    lane = lane_of((32, 128))
    lane8 = lane_of((8, 128))
    lane16 = lane_of((16, 128))
    spare = 2 * A_HALO
    a_rows = pl.ds(edge_rows(odd_x, pairing, A_HALO), A_HALO)
    p_rows = pl.ds(edge_rows(odd_x, pairing, P_HALO), P_HALO)
    for f in range(FLUOR):
        p_top = ps_ref[f, p_rows, :]
        a_side = side_ref[f, a_rows, :]
        out_ref[f, :32, :] = jnp.where(lane < spare, a_side[:32], roll(p_top, spare))
        out_ref[f, 32:48, :] = jnp.where(lane16 < spare, a_side[32:], roll(p_top[:16], spare - P_HALO))
        out_ref[f, 48:, :] = jnp.where(lane8 < P_HALO, roll(p_top[16:24], -P_HALO), p_top[24:])


def corner_body(ya_ref, yb_ref, side_ref, ps_ref, cb_ref, ca_ref):
    odd_x = index(GX) % 2
    odd_y = index(GY) % 2
    lane = lane_of((32, 128))
    lane8 = lane_of((8, 128))
    for f in range(FLUOR):
        first = ya_ref[f, :32, :]
        second = yb_ref[f, :32, :]
        left = choose(odd_y, first, second)
        right = choose(odd_y, second, first)
        side_ref[f, :32, :] = jnp.where(lane < A_HALO, left, jnp.where(lane < 2 * A_HALO, roll(right, A_HALO), 0.0))
        side_ref[f, 32:, :] = jnp.where(lane < A_HALO, roll(left, -A_HALO), jnp.where(lane < 2 * A_HALO, right, 0.0))
        ps_ref[f, :32, :] = jnp.where(
            lane < P_HALO, roll(left, -2 * A_HALO), jnp.where(lane < 2 * P_HALO, roll(right, P_HALO - 2 * A_HALO), 0.0)
        )
        first = ya_ref[f, 32:, :]
        second = yb_ref[f, 32:, :]
        left = choose(odd_y, first, second)
        right = choose(odd_y, second, first)
        for k in range(4):
            ps_ref[f, 32 + 8 * k : 40 + 8 * k, :] = jnp.where(
                lane8 < P_HALO, roll(left, -32 * k), jnp.where(lane8 < 2 * P_HALO, roll(right, P_HALO - 32 * k), 0.0)
            )
    pack_corner(odd_x, 0, side_ref, ps_ref, ca_ref)
    pack_corner(odd_x, 1, side_ref, ps_ref, cb_ref)


GROUP = 4


def along_y(x, w, put):
    for f in range(0, FLUOR, GROUP):
        part = x(slice(f, f + GROUP))
        out = dot_right(part.reshape(-1, part.shape[2]), w)
        out = out.reshape(GROUP, part.shape[1], out.shape[1])
        for k in range(GROUP):
            put(f + k, out[k])


X_GROUP = 4


def along_x(m, stack, out_ref):
    for f in range(0, FLUOR, X_GROUP):
        out = dot(m, jnp.concatenate([stack(f + k) for k in range(X_GROUP)], axis=1))
        for k in range(X_GROUP):
            out_ref[f + k] = out[:, 256 * k : 256 * k + 256]


def wide(main, side):
    return jnp.concatenate([main, side], axis=2)


def mix(gram_ref, v_ref, d_ref, g_ref):
    step = 8
    for start in range(0, G_ROWS, step):
        part = [v_ref[f, start : start + step, :] for f in range(FLUOR)]
        for f in range(FLUOR):
            acc = -d_ref[f, start : start + step, :]
            for k in range(FLUOR):
                acc = acc + gram_ref[f, k] * part[k]
            g_ref[f, start : start + step, :] = acc


def sums(gram_ref, g_ref, by, bx, y_ref, z_ref, sum_ref):
    along_x(bx[...], lambda f: stacked(g_ref[f], 384), y_ref)

    def put(f, z):
        z_ref[f] = z

    along_y(lambda part: y_ref[part], by[...], put)
    grad = jnp.zeros((8, 128), f32)
    image = jnp.zeros((8, 128), f32)
    for start in range(0, ROWS, 8):
        part = [z_ref[f, start : start + 8, :] for f in range(FLUOR)]
        for f in range(FLUOR):
            acc = gram_ref[f, 0] * part[0]
            for k in range(1, FLUOR):
                acc = acc + gram_ref[f, k] * part[k]
            image = image + acc * part[f]
            g = g_ref[f, G_HALO + start : G_HALO + start + 8, :COLS]
            grad = grad + g * g
    grad = jnp.sum(grad, axis=0, keepdims=True)
    image = jnp.sum(image, axis=0, keepdims=True)
    lane = lane_of((1, 128))
    row = jnp.where(lane < 64, grad + roll(grad, 64), image + roll(image, 64))
    sum_ref[...] = jnp.broadcast_to(row, sum_ref.shape)


def step_length(total_ref):
    total = jnp.sum(total_ref[...], axis=0, keepdims=True)
    lane = lane_of((1, 128))
    grad = jnp.sum(jnp.where(lane < 64, total, 0.0), axis=1, keepdims=True)
    image = jnp.sum(jnp.where(lane < 64, 0.0, total), axis=1, keepdims=True)
    return grad / (image + tiny_floor)


def put_stack(ref, f, start, depth, x):
    high, low = split(x)
    for at, part in ((0, high), (depth, low), (2 * depth, high)):
        ref[f, pl.ds(pl.multiple_of(start + at, 16), x.shape[0]), :] = part


def along_half(x, w_ref, start, put):
    w = jnp.concatenate([w_ref[256 * k + start : 256 * k + start + 128, :] for k in range(3)], axis=0)
    along_y(x, w, put)


def store(ref):
    def put(f, x):
        ref[f] = x

    return put


def own_body(
    a_ref, side_ref, p_ref, ps_ref, xb_ref, xa_ref, my, py, u_ref, w_ref, ua_ref, ub_ref, wa_ref, wb_ref
):
    along_y(lambda part: wide(p_ref[part], ps_ref[part]), py[...], store(w_ref))
    along_y(lambda part: wide(a_ref[part], side_ref[part]), my[...], store(u_ref))
    along_half(lambda part: xa_ref[part, :A_HALO, :], my, 0, store(ua_ref))
    along_half(lambda part: xb_ref[part, :A_HALO, :], my, 0, store(ub_ref))
    along_half(lambda part: xa_ref[part, A_HALO:, :], py, 0, store(wa_ref))
    along_half(lambda part: xb_ref[part, A_HALO:, :], py, 0, store(wb_ref))


def first_body(
    gram_ref, u_ref, w_ref, ua_ref, ub_ref, wa_ref, wb_ref, cb_ref, ca_ref, my, py, mx, px,
    d_ref, g_ref, ya_ref, yb_ref, v_ref, su_ref, sw_ref, side_ref,
):
    odd_x = index(GX) % 2
    odd_y = index(GY) % 2
    lane = lane_of((32, 128))
    lane16 = lane_of((16, 128))
    lane8 = lane_of((8, 128))
    spare = 2 * A_HALO
    su_ref[:, 3 * A_ROWS :, :] = jnp.zeros((FLUOR, 512 - 3 * A_ROWS, 256), bf16)
    for u_part, w_part, corner, above in (
        (ua_ref, wa_ref, ca_ref, odd_x == 1),
        (ub_ref, wb_ref, cb_ref, odd_x == 0),
    ):
        for f in range(FLUOR):
            left = roll(corner[f, :32, :], -spare)
            right = roll(corner[f, 32:48, :], P_HALO - spare)
            last = corner[f, 48:, :]
            side_ref[f, :16, :] = jnp.where(lane16 < P_HALO, left[:16], jnp.where(lane16 < 2 * P_HALO, right, 0.0))
            side_ref[f, 16:24, :] = jnp.where(
                lane8 < P_HALO, left[16:24], jnp.where(lane8 < 2 * P_HALO, roll(last, P_HALO), 0.0)
            )
            side_ref[f, 24:, :] = jnp.where(lane8 < P_HALO, left[24:], jnp.where(lane8 < 2 * P_HALO, last, 0.0))
        a_at = jnp.where(above, 0, A_HALO + ROWS)
        p_at = jnp.where(above, 0, P_HALO + ROWS)
        along_half(
            lambda part: side_ref[part],
            py,
            128,
            lambda f, x: put_stack(sw_ref, f, p_at, P_ROWS, x + w_part[f]),
        )
        along_half(
            lambda part: corner[part, :A_HALO, :],
            my,
            128,
            lambda f, x: put_stack(su_ref, f, a_at, A_ROWS, x + u_part[f]),
        )
    for f in range(FLUOR):
        put_stack(sw_ref, f, P_HALO, P_ROWS, w_ref[f])
        put_stack(su_ref, f, A_HALO, A_ROWS, u_ref[f])
    along_x(px[...], lambda f: sw_ref[f], d_ref)
    along_x(mx[...], lambda f: su_ref[f], v_ref)
    mix(gram_ref, v_ref, d_ref, g_ref)
    lane = lane_of((24, 128))
    for f in range(FLUOR):
        edges = []
        for start in (G_HALO, COLS - G_HALO - 32):
            out = roll(g_ref[f, :24, :COLS], -start)
            for k in range(1, 4):
                piece = roll(g_ref[f, 24 * k : 24 * k + 24, :COLS], 32 * k - start)
                out = jnp.where(lane < 32 * k, out, piece)
            edges.append(out)
        ya_ref[f] = choose(odd_y, edges[0], edges[1])
        yb_ref[f] = choose(odd_y, edges[1], edges[0])


def probe_body(gram_ref, g_ref, by, bx, sum_ref, y_ref, z_ref):
    sums(gram_ref, g_ref, by, bx, y_ref, z_ref, sum_ref)


def relay(near_ref, out_ref):
    out_ref[...] = jnp.broadcast_to(jnp.sum(near_ref[...], axis=0, keepdims=True), out_ref.shape)


def outer_body(near_ref, g_ref, ya_ref, yb_ref, far_ref, side_ref, send_ref):
    relay(near_ref, far_ref)
    odd_y = index(GY) % 2
    lane = lane_of((24, 128))
    for f in range(FLUOR):
        left = choose(odd_y, ya_ref[f], yb_ref[f])
        right = choose(odd_y, yb_ref[f], ya_ref[f])
        for k in range(4):
            own = roll(g_ref[f, 24 * k : 24 * k + 24, COLS:], 32)
            side_ref[f, 24 * k : 24 * k + 24, :] = jnp.where(
                lane < 32,
                roll(left, -32 * k),
                jnp.where(lane < 64, own, jnp.where(lane < 96, roll(right, 64 - 32 * k), 0.0)),
            )
        send_ref[f, :32, :] = g_ref[f, 2 * G_HALO : 2 * G_HALO + 32, :COLS]
        send_ref[f, 32:, :] = side_ref[f, 2 * G_HALO : 2 * G_HALO + 32, :]


def second_body(
    gram_ref, total_ref, a_ref, side_ref, za_ref, zb_ref, ca_ref, cb_ref, d_ref, g_ref, gs_ref, xa_ref, xb_ref,
    my, mx, by, bx,
    a_out, g_out, sum_ref, v_ref, n_ref, y_ref, z_ref, x_ref, u_ref,
):
    odd_x = index(GX) % 2
    t = step_length(total_ref)
    for f in range(FLUOR):
        tile = jnp.maximum(a_ref[f] - t * g_ref[f, G_HALO : G_HALO + ROWS, :COLS], 0.0)
        a_out[f] = tile
        x_ref[f, A_HALO : A_HALO + ROWS, :COLS] = tile
        x_ref[f, A_HALO : A_HALO + ROWS, COLS:] = jnp.maximum(
            side_ref[f] - t * gs_ref[f, G_HALO : G_HALO + ROWS, :], 0.0
        )
        for above, main, corner, far, near in (
            (True, choose(odd_x, za_ref[f, :A_HALO, :], zb_ref[f, :A_HALO, :]),
             choose(odd_x, ca_ref[f, :A_HALO, :], cb_ref[f, :A_HALO, :]), choose(odd_x, xa_ref[f], xb_ref[f]),
             slice(0, G_HALO)),
            (False, choose(odd_x, zb_ref[f, :A_HALO, :], za_ref[f, :A_HALO, :]),
             choose(odd_x, cb_ref[f, :A_HALO, :], ca_ref[f, :A_HALO, :]), choose(odd_x, xb_ref[f], xa_ref[f]),
             slice(G_ROWS - G_HALO, G_ROWS)),
        ):
            parts = [far[:32], g_ref[f, near, :COLS]], [far[32:], gs_ref[f, near, :]]
            if not above:
                parts = [part[::-1] for part in parts]
            rows = slice(0, A_HALO) if above else slice(A_HALO + ROWS, A_ROWS)
            x_ref[f, rows, :COLS] = jnp.maximum(main - t * jnp.concatenate(parts[0], axis=0), 0.0)
            x_ref[f, rows, COLS:] = jnp.maximum(corner - t * jnp.concatenate(parts[1], axis=0), 0.0)

    def put(f, u):
        u_ref[f] = u

    along_y(lambda part: x_ref[part], my[...], put)
    along_x(mx[...], lambda f: stacked(u_ref[f], 512), v_ref)
    mix(gram_ref, v_ref, d_ref, n_ref)
    sums(gram_ref, n_ref, by, bx, y_ref, z_ref, sum_ref)
    for f in range(FLUOR):
        g_out[f] = n_ref[f, G_HALO : G_HALO + ROWS, :COLS]


def last_body(total_ref, a_ref, g_ref, out_ref):
    t = step_length(total_ref)
    for f in range(FLUOR):
        out_ref[f] = jnp.maximum(a_ref[f] - t * g_ref[f], 0.0)


TILE = (FLUOR, ROWS, COLS)
G_SHAPE = (FLUOR, G_ROWS, 256)
PROBE_SCRATCH = (pltpu.VMEM((FLUOR, ROWS, 256), f32), pltpu.VMEM(TILE, f32))
OWN_COST = 10**10
NEAR_COUNT = 32
FAR_COUNT = 16

first_call = kernel(
    first_body,
    "s" + "v" * 12,
    [(G_SHAPE, f32)] * 2 + [((FLUOR, 24, 128), f32)] * 2,
    10**9,
    [
        pltpu.VMEM(G_SHAPE, f32),
        pltpu.VMEM((FLUOR, 512, 256), bf16),
        pltpu.VMEM((FLUOR, 3 * P_ROWS, 256), bf16),
        pltpu.VMEM((FLUOR, P_HALO, 128), f32),
    ],
)
probe_call = kernel(probe_body, "svvv", [((NEAR_COUNT, 128), f32)], 10**9, PROBE_SCRATCH)
second_call = kernel(
    second_body,
    "s" + "v" * 16,
    [(TILE, f32)] * 2 + [((NEAR_COUNT, 128), f32)],
    10**9,
    [
        pltpu.VMEM(G_SHAPE, f32),
        pltpu.VMEM(G_SHAPE, f32),
        *PROBE_SCRATCH,
        pltpu.VMEM((FLUOR, A_ROWS, 256), f32),
        pltpu.VMEM((FLUOR, A_ROWS, 256), f32),
    ],
)


def length(axes):
    count = 1
    for axis in axes:
        count *= lax.axis_size(axis)
    return count


def trade(first, second, axes):
    return trade_first(first, axes), trade_second(second, axes)


def trade_first(edge, axes):
    return lax.ppermute(edge, axes, [(i, i ^ 1) for i in range(length(axes))])


def trade_second(edge, axes):
    count = length(axes)
    return lax.ppermute(edge, axes, [(i, (i + (1 if i % 2 else -1)) % count) for i in range(count)])


def spread(rows, axes):
    got = lax.all_to_all(rows.reshape(rows.shape[0], 1, 128), axes, 0, 0, tiled=True)
    return got.reshape(rows.shape[0], 128)


def local(sizes, abundance_start, measured, spectra, taps_x, taps_y):
    assert (length(NEAR), length((FAR,))) == (NEAR_COUNT, FAR_COUNT)

    edge = (FLUOR, A_HALO + P_HALO, 128)
    a0 = abundance_start[0]
    p, xb, xa, ya, yb = kernel(
        project_body,
        "hhh",
        [(TILE, f32)] + [(edge, f32)] * 2 + [((FLUOR, 40, 128), f32)] * 2,
        10**7,
        [
            pltpu.SMEM((FLUOR, CHAN), f32),
            pltpu.VMEM(TILE, f32),
            pltpu.VMEM((CHAN, ROWS, COLS), bf16),
            pltpu.SemaphoreType.DMA((6,)),
        ],
        60_000_000,
    )(spectra.T, a0, measured[0])
    za, zb = trade(xa, xb, GX)
    ya, yb = trade(ya, yb, GY)
    corner = (FLUOR, 56, 128)
    side, ps, cb, ca = kernel(corner_body, "vv", [(TILE, f32)] * 2 + [(corner, f32)] * 2, 10**7)(ya, yb)
    ca, cb = trade(ca, cb, GX)
    gram, my, py, by, mx, px, bx = kernel(
        functools.partial(matrices_body, sizes),
        "ssvv",
        [((FLUOR, FLUOR), f32)] + [((768, 256), bf16)] * 2 + [((768, 128), bf16)]
        + [((G_ROWS, 512), bf16), ((G_ROWS, 384), bf16), ((ROWS, 384), bf16)],
        10**9,
    )(taps_x, taps_y, spectra.T, ps)
    halves = kernel(
        own_body,
        "v" * 8,
        [((FLUOR, rows, 256), f32) for rows in (ROWS, ROWS, A_HALO, A_HALO, P_HALO, P_HALO)],
        OWN_COST,
    )(a0, side, p, ps, zb, za, my, py)
    d, g, ya, yb = first_call(gram, *halves, cb, ca, my, py, mx, px)
    ya, yb = trade(ya, yb, GY)
    (partial,) = probe_call(gram, g, by, bx)
    near = spread(partial, NEAR)
    far, g_side, send = kernel(
        outer_body,
        "vvvv",
        [((FAR_COUNT, 128), f32), ((FLUOR, G_ROWS, 128), f32), ((FLUOR, 64, 128), f32)],
        10**8,
    )(near, g, ya, yb)
    xa, xb = trade(send, send, GX)
    total = spread(far, FAR)
    a1, g1, partial = second_call(
        gram, total, a0, side, za, zb, ca, cb, d, g, g_side, xa, xb, my, mx, by, bx
    )
    (far,) = kernel(relay, "v", [((FAR_COUNT, 128), f32)], 10**6)(spread(partial, NEAR))
    total = spread(far, FAR)
    (out,) = kernel(last_body, "vvv", [(TILE, f32)], 10**7)(total, a1, g1)
    return out[None]


def solution(mesh):
    count_x, count_y = mesh.shape["gx"], mesh.shape["gy"]
    parts = Mesh(
        mesh.devices.reshape(count_x // 4, 2, 2, 2, count_y // 2), ("y", "x_hi", "core", "x_lo", "z")
    )
    sizes = (count_x * ROWS, count_y * COLS)
    tiles = P(None, None, GX, GY)
    return jax.shard_map(
        functools.partial(local, sizes),
        mesh=parts,
        in_specs=(tiles, tiles, P(), P(), P()),
        out_specs=tiles,
        check_vma=False,
    )
```

```python
import functools

import jax
import jax.numpy as jnp
from jax import lax
from jax.experimental import pallas as pl
from jax.experimental.pallas import tpu as pltpu
from jax.sharding import Mesh
from jax.sharding import PartitionSpec as P

TAPS = 33
ITERS = 2
FLUOR = 12
CHAN = 32
ROWS = 64
COLS = 128

HALF = TAPS // 2
A_HALO = 3 * HALF
P_HALO = 2 * HALF
G_HALO = HALF
A_ROWS = ROWS + 2 * A_HALO
P_ROWS = ROWS + 2 * P_HALO
G_ROWS = ROWS + 2 * G_HALO

GX = ("y", "x_hi", "core")
GY = ("x_lo", "z")
NEAR = ("y", "x_hi", "core", "x_lo")
FAR = "z"

tiny_floor = 1e-06
f32 = jnp.float32
bf16 = jnp.bfloat16


SPACES = {"s": pltpu.SMEM, "v": pltpu.VMEM, "h": pltpu.HBM}


def kernel(body, ins, outs, cost, scratch=(), limit=32 * 2**20, space=pltpu.VMEM):
    return pl.pallas_call(
        body,
        in_specs=[pl.BlockSpec(memory_space=SPACES[kind]) for kind in ins],
        out_specs=[pl.BlockSpec(memory_space=space) for _ in outs],
        out_shape=[jax.ShapeDtypeStruct(shape, dtype) for shape, dtype in outs],
        scratch_shapes=list(scratch),
        compiler_params=pltpu.CompilerParams(vmem_limit_bytes=limit),
        cost_estimate=pl.CostEstimate(flops=cost, bytes_accessed=cost // 100, transcendentals=0),
    )


def index(axes):
    place = 0
    for axis in axes:
        place = place * lax.axis_size(axis) + lax.axis_index(axis)
    return place


def roll(x, by):
    by = by % 128
    return x if by == 0 else pltpu.roll(x, by, axis=x.ndim - 1)


def lane_of(shape):
    return lax.broadcasted_iota(jnp.int32, shape, len(shape) - 1)


def split(x):
    high = x.astype(bf16)
    return high, (x - high.astype(f32)).astype(bf16)


def dot(a, b):
    return jnp.dot(a, b, preferred_element_type=f32)


def dot_right(x, w):
    high, low = split(x)
    return dot(jnp.concatenate([high, low, high], axis=1), w)


def stacked(x, depth):
    high, low = split(x)
    parts = [high, low, high]
    spare = depth - 3 * x.shape[0]
    if spare:
        parts.append(jnp.zeros((spare, x.shape[1]), bf16))
    return jnp.concatenate(parts, axis=0)


def side_position(index, halo):
    left = index - COLS - halo
    right = index - halo
    position = jnp.where(index < COLS, index, jnp.where(index < COLS + halo, left, right))
    return jnp.where(index < COLS + 2 * halo, position, 1 << 20)


def tap_matrix(taps_ref, offset):
    out = jnp.zeros(offset.shape, f32)
    for t in range(TAPS):
        out = jnp.where(offset == t, taps_ref[t], out)
    return out


def inside(position, base, size):
    where = position + base
    return jnp.logical_and(where >= 0, where < size)


def exact_dot(a, b):
    return lax.dot_general(a, b, (((1,), (0,)), ((), ())), precision=lax.Precision.HIGHEST, preferred_element_type=f32)


def rows_cols(shape):
    return lax.broadcasted_iota(jnp.int32, shape, 0), lax.broadcasted_iota(jnp.int32, shape, 1)


def put_right(x, ref):
    high, low = split(x)
    rows = x.shape[0]
    ref[:rows, :] = high
    ref[rows : 2 * rows, :] = high
    ref[2 * rows :, :] = low


def put_left(x, part, ref):
    high, low = split(x)
    ref[...] = jnp.where(part < 2, high.astype(f32), low.astype(f32)).astype(bf16)


def matrices_body(sizes, tx_ref, ty_ref, spectra_ref, gram_ref, my, py, by, mx, px, bx):
    spectra = spectra_ref[...]
    gram_ref[...] = lax.dot_general(
        spectra, spectra, (((1,), (1,)), ((), ())), precision=lax.Precision.HIGHEST, preferred_element_type=f32
    )
    size_x, size_y = sizes
    base_x = index(GX) * ROWS
    base_y = index(GY) * COLS
    r, c = rows_cols((256, 256))
    source = side_position(r, P_HALO)
    target = side_position(c, G_HALO)
    okay = jnp.logical_and(inside(source, base_y, size_y), inside(target, base_y, size_y))
    put_right(jnp.where(okay, tap_matrix(ty_ref, target - source + HALF), 0.0), py)
    source = side_position(r, A_HALO)
    middle = c - P_HALO
    okay = jnp.logical_and(inside(source, base_y, size_y), inside(middle, base_y, size_y))
    first = jnp.where(okay, tap_matrix(ty_ref, source - middle + HALF), 0.0)
    middle = r - P_HALO
    second = jnp.where(inside(target, base_y, size_y), tap_matrix(ty_ref, target - middle + HALF), 0.0)
    put_right(exact_dot(first, second), my)
    r, c = rows_cols((256, 128))
    source = side_position(r, G_HALO)
    okay = inside(source, base_y, size_y)
    put_right(jnp.where(okay, tap_matrix(ty_ref, source - c + HALF), 0.0), by)
    r, c = rows_cols((128, 512))
    part = c // A_ROWS
    source = c - part * A_ROWS - A_HALO
    middle = r - P_HALO
    okay = jnp.logical_and(inside(source, base_x, size_x), inside(middle, base_x, size_x))
    okay = jnp.logical_and(okay, part < 3)
    first = jnp.where(okay, tap_matrix(tx_ref, source - middle + HALF), 0.0)
    r, c = rows_cols((G_ROWS, 128))
    target = r - G_HALO
    middle = c - P_HALO
    second = jnp.where(inside(target, base_x, size_x), tap_matrix(tx_ref, target - middle + HALF), 0.0)
    r, c = rows_cols((G_ROWS, 512))
    put_left(exact_dot(second, first), c // A_ROWS, mx)
    r, c = rows_cols((G_ROWS, 384))
    part = c // P_ROWS
    source = c - part * P_ROWS - P_HALO
    target = r - G_HALO
    okay = jnp.logical_and(inside(source, base_x, size_x), inside(target, base_x, size_x))
    put_left(jnp.where(okay, tap_matrix(tx_ref, target - source + HALF), 0.0), part, px)
    r, c = rows_cols((ROWS, 384))
    part = c // G_ROWS
    source = c - part * G_ROWS - G_HALO
    okay = jnp.logical_and(inside(source, base_x, size_x), part < 3)
    put_left(jnp.where(okay, tap_matrix(tx_ref, source - r + HALF), 0.0), part, bx)


def choose(odd, if_odd, if_even):
    return jnp.where(odd == 1, if_odd, if_even)


def edge_rows(odd_x, pairing, depth):
    top = odd_x == 1 if pairing == 0 else odd_x == 0
    return pl.multiple_of(jnp.where(top, 0, ROWS - depth), 16)


def project_body(
    s_hbm, a_hbm, m_hbm, p_hbm, xb_hbm, xa_hbm, ya_hbm, yb_hbm,
    spectra_ref, a_ref, m_ref, p_ref, ya_ref, yb_ref, sems, out_sems,
):
    step = 32
    copy_s = pltpu.make_async_copy(s_hbm, spectra_ref, sems.at[5])
    copy_s.start()
    copies = [
        pltpu.make_async_copy(m_hbm.at[:, pl.ds(k * step, step), :], m_ref.at[:, pl.ds(k * step, step), :], sems.at[k])
        for k in range(ROWS // step)
    ]
    for copy in copies:
        copy.start()
    copy_a = pltpu.make_async_copy(a_hbm, a_ref, sems.at[ROWS // step])
    copy_a.start()
    odd_x = index(GX) % 2
    edges = []
    copy_s.wait()
    for k, copy in enumerate(copies):
        copy.wait()
        start = k * step
        acc = [jnp.zeros((step, COLS), f32) for _ in range(FLUOR)]
        for c in range(CHAN):
            seen = m_ref[c, start : start + step, :].astype(f32)
            for f in range(FLUOR):
                acc[f] = acc[f] + spectra_ref[f, c] * seen
        for f in range(FLUOR):
            p_ref[f, start : start + step, :] = acc[f]
        if k == 0:
            copy_a.wait()
            for pairing, x_hbm in ((1, xb_hbm), (0, xa_hbm)):
                rows = pl.ds(edge_rows(odd_x, pairing, A_HALO), A_HALO)
                edges.append(
                    pltpu.make_async_copy(a_ref.at[:, rows, :], x_hbm.at[:, pl.ds(0, A_HALO), :], out_sems.at[pairing])
                )
                edges[-1].start()
    for k, x_hbm in ((1, xb_hbm), (0, xa_hbm)):
        rows = pl.ds(edge_rows(odd_x, k, P_HALO), P_HALO)
        edges.append(
            pltpu.make_async_copy(p_ref.at[:, rows, :], x_hbm.at[:, pl.ds(A_HALO, P_HALO), :], out_sems.at[2 + k])
        )
        edges[-1].start()
    edges.append(pltpu.make_async_copy(p_ref, p_hbm, out_sems.at[4]))
    edges[-1].start()
    odd_y = index(GY) % 2
    lane = lane_of((32, 128))
    lane8 = lane_of((8, 128))
    for f in range(FLUOR):
        sides = []
        for a_from, p_from in ((0, 0), (COLS - A_HALO, COLS - P_HALO)):
            top = roll(a_ref[f, :32, :], -a_from)
            low = roll(a_ref[f, 32:, :], A_HALO - a_from)
            side = roll(p_ref[f, :32, :], 2 * A_HALO - p_from)
            main = jnp.where(lane < A_HALO, top, jnp.where(lane < 2 * A_HALO, low, side))
            rest = roll(p_ref[f, 32:40, :], -p_from)
            for k in range(1, 4):
                piece = roll(p_ref[f, 32 + 8 * k : 40 + 8 * k, :], 32 * k - p_from)
                rest = jnp.where(lane8 < 32 * k, rest, piece)
            sides.append((main, rest))
        (left, left_rest), (right, right_rest) = sides
        ya_ref[f, :32, :] = choose(odd_y, left, right)
        yb_ref[f, :32, :] = choose(odd_y, right, left)
        ya_ref[f, 32:, :] = choose(odd_y, left_rest, right_rest)
        yb_ref[f, 32:, :] = choose(odd_y, right_rest, left_rest)
    for k, (ref, y_hbm) in enumerate(((ya_ref, ya_hbm), (yb_ref, yb_hbm))):
        edges.append(pltpu.make_async_copy(ref, y_hbm, out_sems.at[5 + k]))
        edges[-1].start()
    for copy in edges:
        copy.wait()


def pack_corner(odd_x, pairing, side_ref, ps_ref, out_ref):
    lane = lane_of((32, 128))
    lane8 = lane_of((8, 128))
    lane16 = lane_of((16, 128))
    spare = 2 * A_HALO
    a_rows = pl.ds(edge_rows(odd_x, pairing, A_HALO), A_HALO)
    p_rows = pl.ds(edge_rows(odd_x, pairing, P_HALO), P_HALO)
    for f in range(FLUOR):
        p_top = ps_ref[f, p_rows, :]
        a_side = side_ref[f, a_rows, :]
        out_ref[f, :32, :] = jnp.where(lane < spare, a_side[:32], roll(p_top, spare))
        out_ref[f, 32:48, :] = jnp.where(lane16 < spare, a_side[32:], roll(p_top[:16], spare - P_HALO))
        out_ref[f, 48:, :] = jnp.where(lane8 < P_HALO, roll(p_top[16:24], -P_HALO), p_top[24:])


def corner_body(ya_ref, yb_ref, side_ref, ps_ref, cb_ref, ca_ref):
    odd_x = index(GX) % 2
    odd_y = index(GY) % 2
    lane = lane_of((32, 128))
    lane8 = lane_of((8, 128))
    for f in range(FLUOR):
        first = ya_ref[f, :32, :]
        second = yb_ref[f, :32, :]
        left = choose(odd_y, first, second)
        right = choose(odd_y, second, first)
        side_ref[f, :32, :] = jnp.where(lane < A_HALO, left, jnp.where(lane < 2 * A_HALO, roll(right, A_HALO), 0.0))
        side_ref[f, 32:, :] = jnp.where(lane < A_HALO, roll(left, -A_HALO), jnp.where(lane < 2 * A_HALO, right, 0.0))
        ps_ref[f, :32, :] = jnp.where(
            lane < P_HALO, roll(left, -2 * A_HALO), jnp.where(lane < 2 * P_HALO, roll(right, P_HALO - 2 * A_HALO), 0.0)
        )
        first = ya_ref[f, 32:, :]
        second = yb_ref[f, 32:, :]
        left = choose(odd_y, first, second)
        right = choose(odd_y, second, first)
        for k in range(4):
            ps_ref[f, 32 + 8 * k : 40 + 8 * k, :] = jnp.where(
                lane8 < P_HALO, roll(left, -32 * k), jnp.where(lane8 < 2 * P_HALO, roll(right, P_HALO - 32 * k), 0.0)
            )
    pack_corner(odd_x, 0, side_ref, ps_ref, ca_ref)
    pack_corner(odd_x, 1, side_ref, ps_ref, cb_ref)


GROUP = 4


def along_y(x, w, put):
    for f in range(0, FLUOR, GROUP):
        part = x(slice(f, f + GROUP))
        out = dot_right(part.reshape(-1, part.shape[2]), w)
        out = out.reshape(GROUP, part.shape[1], out.shape[1])
        for k in range(GROUP):
            put(f + k, out[k])


X_GROUP = 4


def along_x(m, stack, out_ref):
    for f in range(0, FLUOR, X_GROUP):
        out = dot(m, jnp.concatenate([stack(f + k) for k in range(X_GROUP)], axis=1))
        for k in range(X_GROUP):
            out_ref[f + k] = out[:, 256 * k : 256 * k + 256]


def wide(main, side):
    return jnp.concatenate([main, side], axis=2)


def mix(gram_ref, v_ref, d_ref, g_ref):
    step = 8

    def mixed(part, f):
        acc = gram_ref[f, 0] * part[0]
        for k in range(1, FLUOR):
            acc = acc + gram_ref[f, k] * part[k]
        return acc

    for start in range(0, G_ROWS, step):
        part = [v_ref[f, start : start + step, :COLS] for f in range(FLUOR)]
        for f in range(FLUOR):
            g_ref[f, start : start + step, :COLS] = mixed(part, f) - d_ref[f, start : start + step, :COLS]
    lane = lane_of((step, 128))
    group = G_ROWS // 4
    for start in range(0, group, step):
        rows = [slice(k * group + start, k * group + start + step) for k in range(4)]
        part = []
        for f in range(FLUOR):
            packed = v_ref[f, rows[0], COLS:]
            for k in range(1, 4):
                packed = packed + roll(v_ref[f, rows[k], COLS:], 32 * k)
            part.append(packed)
        for f in range(FLUOR):
            out = mixed(part, f)
            for k in range(4):
                side = jnp.where(lane < 2 * G_HALO, roll(out, -32 * k), 0.0)
                g_ref[f, rows[k], COLS:] = side - d_ref[f, rows[k], COLS:]


def sums(gram_ref, g_ref, by, bx, y_ref, z_ref, sum_ref):
    along_x(bx[...], lambda f: stacked(g_ref[f], 384), y_ref)

    def put(f, z):
        z_ref[f] = z

    along_y(lambda part: y_ref[part], by[...], put)
    grad = jnp.zeros((8, 128), f32)
    image = jnp.zeros((8, 128), f32)
    for start in range(0, ROWS, 8):
        part = [z_ref[f, start : start + 8, :] for f in range(FLUOR)]
        for f in range(FLUOR):
            acc = gram_ref[f, 0] * part[0]
            for k in range(1, FLUOR):
                acc = acc + gram_ref[f, k] * part[k]
            image = image + acc * part[f]
            g = g_ref[f, G_HALO + start : G_HALO + start + 8, :COLS]
            grad = grad + g * g
    grad = jnp.sum(grad, axis=0, keepdims=True)
    image = jnp.sum(image, axis=0, keepdims=True)
    lane = lane_of((1, 128))
    row = jnp.where(lane < 64, grad + roll(grad, 64), image + roll(image, 64))
    sum_ref[...] = jnp.broadcast_to(row, sum_ref.shape)


def step_length(total_ref):
    total = jnp.sum(total_ref[...], axis=0, keepdims=True)
    lane = lane_of((1, 128))
    grad = jnp.sum(jnp.where(lane < 64, total, 0.0), axis=1, keepdims=True)
    image = jnp.sum(jnp.where(lane < 64, 0.0, total), axis=1, keepdims=True)
    return grad / (image + tiny_floor)


def put_stack(ref, f, start, depth, x):
    high, low = split(x)
    for at, part in ((0, high), (depth, low), (2 * depth, high)):
        ref[f, pl.ds(pl.multiple_of(start + at, 16), x.shape[0]), :] = part


def along_half(x, w_ref, start, put):
    w = jnp.concatenate([w_ref[256 * k + start : 256 * k + start + 128, :] for k in range(3)], axis=0)
    along_y(x, w, put)


def store(ref):
    def put(f, x):
        ref[f] = x

    return put


def own_body(
    a_ref, side_ref, p_ref, ps_ref, xb_ref, xa_ref, my, py, u_ref, w_ref, ua_ref, ub_ref, wa_ref, wb_ref
):
    along_y(lambda part: wide(p_ref[part], ps_ref[part]), py[...], store(w_ref))
    along_y(lambda part: wide(a_ref[part], side_ref[part]), my[...], store(u_ref))
    along_half(lambda part: xa_ref[part, :A_HALO, :], my, 0, store(ua_ref))
    along_half(lambda part: xb_ref[part, :A_HALO, :], my, 0, store(ub_ref))
    along_half(lambda part: xa_ref[part, A_HALO:, :], py, 0, store(wa_ref))
    along_half(lambda part: xb_ref[part, A_HALO:, :], py, 0, store(wb_ref))


def first_body(
    gram_ref, u_ref, w_ref, ua_ref, ub_ref, wa_ref, wb_ref, cb_ref, ca_ref, my, py, mx, px,
    d_ref, g_ref, ya_ref, yb_ref, v_ref, su_ref, sw_ref, side_ref,
):
    odd_x = index(GX) % 2
    odd_y = index(GY) % 2
    lane = lane_of((32, 128))
    lane16 = lane_of((16, 128))
    lane8 = lane_of((8, 128))
    spare = 2 * A_HALO
    su_ref[:, 3 * A_ROWS :, :] = jnp.zeros((FLUOR, 512 - 3 * A_ROWS, 256), bf16)
    for u_part, w_part, corner, above in (
        (ua_ref, wa_ref, ca_ref, odd_x == 1),
        (ub_ref, wb_ref, cb_ref, odd_x == 0),
    ):
        for f in range(FLUOR):
            left = roll(corner[f, :32, :], -spare)
            right = roll(corner[f, 32:48, :], P_HALO - spare)
            last = corner[f, 48:, :]
            side_ref[f, :16, :] = jnp.where(lane16 < P_HALO, left[:16], jnp.where(lane16 < 2 * P_HALO, right, 0.0))
            side_ref[f, 16:24, :] = jnp.where(
                lane8 < P_HALO, left[16:24], jnp.where(lane8 < 2 * P_HALO, roll(last, P_HALO), 0.0)
            )
            side_ref[f, 24:, :] = jnp.where(lane8 < P_HALO, left[24:], jnp.where(lane8 < 2 * P_HALO, last, 0.0))
        a_at = jnp.where(above, 0, A_HALO + ROWS)
        p_at = jnp.where(above, 0, P_HALO + ROWS)
        along_half(
            lambda part: side_ref[part],
            py,
            128,
            lambda f, x: put_stack(sw_ref, f, p_at, P_ROWS, x + w_part[f]),
        )
        along_half(
            lambda part: corner[part, :A_HALO, :],
            my,
            128,
            lambda f, x: put_stack(su_ref, f, a_at, A_ROWS, x + u_part[f]),
        )
    for f in range(FLUOR):
        put_stack(sw_ref, f, P_HALO, P_ROWS, w_ref[f])
        put_stack(su_ref, f, A_HALO, A_ROWS, u_ref[f])
    along_x(px[...], lambda f: sw_ref[f], d_ref)
    along_x(mx[...], lambda f: su_ref[f], v_ref)
    mix(gram_ref, v_ref, d_ref, g_ref)
    lane = lane_of((24, 128))
    for f in range(FLUOR):
        edges = []
        for start in (G_HALO, COLS - G_HALO - 32):
            out = roll(g_ref[f, :24, :COLS], -start)
            for k in range(1, 4):
                piece = roll(g_ref[f, 24 * k : 24 * k + 24, :COLS], 32 * k - start)
                out = jnp.where(lane < 32 * k, out, piece)
            edges.append(out)
        ya_ref[f] = choose(odd_y, edges[0], edges[1])
        yb_ref[f] = choose(odd_y, edges[1], edges[0])


def probe_body(gram_ref, g_ref, by, bx, sum_ref, y_ref, z_ref):
    sums(gram_ref, g_ref, by, bx, y_ref, z_ref, sum_ref)


def relay(near_ref, out_ref):
    out_ref[...] = jnp.broadcast_to(jnp.sum(near_ref[...], axis=0, keepdims=True), out_ref.shape)


def outer_body(near_ref, g_ref, ya_ref, yb_ref, far_ref, side_ref, send_ref):
    relay(near_ref, far_ref)
    odd_y = index(GY) % 2
    lane = lane_of((24, 128))
    for f in range(FLUOR):
        left = choose(odd_y, ya_ref[f], yb_ref[f])
        right = choose(odd_y, yb_ref[f], ya_ref[f])
        for k in range(4):
            own = roll(g_ref[f, 24 * k : 24 * k + 24, COLS:], 32)
            side_ref[f, 24 * k : 24 * k + 24, :] = jnp.where(
                lane < 32,
                roll(left, -32 * k),
                jnp.where(lane < 64, own, jnp.where(lane < 96, roll(right, 64 - 32 * k), 0.0)),
            )
        send_ref[f, :32, :] = g_ref[f, 2 * G_HALO : 2 * G_HALO + 32, :COLS]
        send_ref[f, 32:, :] = side_ref[f, 2 * G_HALO : 2 * G_HALO + 32, :]


def second_body(
    gram_ref, total_ref, a_ref, side_ref, za_ref, zb_ref, ca_ref, cb_ref, d_ref, g_ref, gs_ref, xa_ref, xb_ref,
    my, mx, by, bx,
    a_out, g_out, sum_ref, v_ref, n_ref, y_ref, z_ref, x_ref, u_ref,
):
    odd_x = index(GX) % 2
    t = step_length(total_ref)
    for f in range(FLUOR):
        tile = jnp.maximum(a_ref[f] - t * g_ref[f, G_HALO : G_HALO + ROWS, :COLS], 0.0)
        a_out[f] = tile
        x_ref[f, A_HALO : A_HALO + ROWS, :COLS] = tile
        x_ref[f, A_HALO : A_HALO + ROWS, COLS:] = jnp.maximum(
            side_ref[f] - t * gs_ref[f, G_HALO : G_HALO + ROWS, :], 0.0
        )
        for above, main, corner, far, near in (
            (True, choose(odd_x, za_ref[f, :A_HALO, :], zb_ref[f, :A_HALO, :]),
             choose(odd_x, ca_ref[f, :A_HALO, :], cb_ref[f, :A_HALO, :]), choose(odd_x, xa_ref[f], xb_ref[f]),
             slice(0, G_HALO)),
            (False, choose(odd_x, zb_ref[f, :A_HALO, :], za_ref[f, :A_HALO, :]),
             choose(odd_x, cb_ref[f, :A_HALO, :], ca_ref[f, :A_HALO, :]), choose(odd_x, xb_ref[f], xa_ref[f]),
             slice(G_ROWS - G_HALO, G_ROWS)),
        ):
            parts = [far[:32], g_ref[f, near, :COLS]], [far[32:], gs_ref[f, near, :]]
            if not above:
                parts = [part[::-1] for part in parts]
            rows = slice(0, A_HALO) if above else slice(A_HALO + ROWS, A_ROWS)
            x_ref[f, rows, :COLS] = jnp.maximum(main - t * jnp.concatenate(parts[0], axis=0), 0.0)
            x_ref[f, rows, COLS:] = jnp.maximum(corner - t * jnp.concatenate(parts[1], axis=0), 0.0)

    def put(f, u):
        u_ref[f] = u

    along_y(lambda part: x_ref[part], my[...], put)
    along_x(mx[...], lambda f: stacked(u_ref[f], 512), v_ref)
    mix(gram_ref, v_ref, d_ref, n_ref)
    sums(gram_ref, n_ref, by, bx, y_ref, z_ref, sum_ref)
    for f in range(FLUOR):
        g_out[f] = n_ref[f, G_HALO : G_HALO + ROWS, :COLS]


def last_body(total_ref, a_ref, g_ref, out_ref):
    t = step_length(total_ref)
    for f in range(FLUOR):
        out_ref[f] = jnp.maximum(a_ref[f] - t * g_ref[f], 0.0)


TILE = (FLUOR, ROWS, COLS)
G_SHAPE = (FLUOR, G_ROWS, 256)
PROBE_SCRATCH = (pltpu.VMEM((FLUOR, ROWS, 256), f32), pltpu.VMEM(TILE, f32))
OWN_COST = 10**10
NEAR_COUNT = 32
FAR_COUNT = 16

first_call = kernel(
    first_body,
    "s" + "v" * 12,
    [(G_SHAPE, f32)] * 2 + [((FLUOR, 24, 128), f32)] * 2,
    10**9,
    [
        pltpu.VMEM(G_SHAPE, f32),
        pltpu.VMEM((FLUOR, 512, 256), bf16),
        pltpu.VMEM((FLUOR, 3 * P_ROWS, 256), bf16),
        pltpu.VMEM((FLUOR, P_HALO, 128), f32),
    ],
)
probe_call = kernel(probe_body, "svvv", [((NEAR_COUNT, 128), f32)], 10**9, PROBE_SCRATCH)
second_call = kernel(
    second_body,
    "s" + "v" * 16,
    [(TILE, f32)] * 2 + [((NEAR_COUNT, 128), f32)],
    10**9,
    [
        pltpu.VMEM(G_SHAPE, f32),
        pltpu.VMEM(G_SHAPE, f32),
        *PROBE_SCRATCH,
        pltpu.VMEM((FLUOR, A_ROWS, 256), f32),
        pltpu.VMEM((FLUOR, A_ROWS, 256), f32),
    ],
)


def length(axes):
    count = 1
    for axis in axes:
        count *= lax.axis_size(axis)
    return count


def trade(first, second, axes):
    return trade_first(first, axes), trade_second(second, axes)


def trade_first(edge, axes):
    return lax.ppermute(edge, axes, [(i, i ^ 1) for i in range(length(axes))])


def trade_second(edge, axes):
    count = length(axes)
    return lax.ppermute(edge, axes, [(i, (i + (1 if i % 2 else -1)) % count) for i in range(count)])


def spread(rows, axes):
    got = lax.all_to_all(rows.reshape(rows.shape[0], 1, 128), axes, 0, 0, tiled=True)
    return got.reshape(rows.shape[0], 128)


def local(sizes, abundance_start, measured, spectra, taps_x, taps_y):
    assert (length(NEAR), length((FAR,))) == (NEAR_COUNT, FAR_COUNT)

    edge = (FLUOR, A_HALO + P_HALO, 128)
    a0 = abundance_start[0]
    p, xb, xa, ya, yb = kernel(
        project_body,
        "hhh",
        [(TILE, f32)] + [(edge, f32)] * 2 + [((FLUOR, 40, 128), f32)] * 2,
        10**7,
        [
            pltpu.SMEM((FLUOR, CHAN), f32),
            pltpu.VMEM(TILE, f32),
            pltpu.VMEM((CHAN, ROWS, COLS), bf16),
            pltpu.VMEM(TILE, f32),
            pltpu.VMEM((FLUOR, 40, 128), f32),
            pltpu.VMEM((FLUOR, 40, 128), f32),
            pltpu.SemaphoreType.DMA((6,)),
            pltpu.SemaphoreType.DMA((7,)),
        ],
        60_000_000,
        pltpu.HBM,
    )(spectra.T, a0, measured[0])
    za, zb = trade(xa, xb, GX)
    ya, yb = trade(ya, yb, GY)
    corner = (FLUOR, 56, 128)
    side, ps, cb, ca = kernel(corner_body, "vv", [(TILE, f32)] * 2 + [(corner, f32)] * 2, 10**7)(ya, yb)
    ca, cb = trade(ca, cb, GX)
    gram, my, py, by, mx, px, bx = kernel(
        functools.partial(matrices_body, sizes),
        "ssv",
        [((FLUOR, FLUOR), f32)] + [((768, 256), bf16)] * 2 + [((768, 128), bf16)]
        + [((G_ROWS, 512), bf16), ((G_ROWS, 384), bf16), ((ROWS, 384), bf16)],
        10**9,
    )(taps_x, taps_y, spectra.T)
    halves = kernel(
        own_body,
        "v" * 8,
        [((FLUOR, rows, 256), f32) for rows in (ROWS, ROWS, A_HALO, A_HALO, P_HALO, P_HALO)],
        OWN_COST,
    )(a0, side, p, ps, zb, za, my, py)
    d, g, ya, yb = first_call(gram, *halves, cb, ca, my, py, mx, px)
    ya, yb = trade(ya, yb, GY)
    (partial,) = probe_call(gram, g, by, bx)
    near = spread(partial, NEAR)
    far, g_side, send = kernel(
        outer_body,
        "vvvv",
        [((FAR_COUNT, 128), f32), ((FLUOR, G_ROWS, 128), f32), ((FLUOR, 64, 128), f32)],
        10**8,
    )(near, g, ya, yb)
    xa, xb = trade(send, send, GX)
    total = spread(far, FAR)
    a1, g1, partial = second_call(
        gram, total, a0, side, za, zb, ca, cb, d, g, g_side, xa, xb, my, mx, by, bx
    )
    (far,) = kernel(relay, "v", [((FAR_COUNT, 128), f32)], 10**6)(spread(partial, NEAR))
    total = spread(far, FAR)
    (out,) = kernel(last_body, "vvv", [(TILE, f32)], 10**7)(total, a1, g1)
    return out[None]


def solution(mesh):
    count_x, count_y = mesh.shape["gx"], mesh.shape["gy"]
    parts = Mesh(
        mesh.devices.reshape(count_x // 4, 2, 2, 2, count_y // 2), ("y", "x_hi", "core", "x_lo", "z")
    )
    sizes = (count_x * ROWS, count_y * COLS)
    tiles = P(None, None, GX, GY)
    return jax.shard_map(
        functools.partial(local, sizes),
        mesh=parts,
        in_specs=(tiles, tiles, P(), P(), P()),
        out_specs=tiles,
        check_vma=False,
    )
```

```python
import functools

import jax
import jax.numpy as jnp
from jax import lax
from jax.experimental import pallas as pl
from jax.experimental.pallas import tpu as pltpu
from jax.sharding import Mesh
from jax.sharding import PartitionSpec as P

TAPS = 33
ITERS = 2
FLUOR = 12
CHAN = 32
ROWS = 64
COLS = 128

HALF = TAPS // 2
A_HALO = 3 * HALF
P_HALO = 2 * HALF
G_HALO = HALF
A_ROWS = ROWS + 2 * A_HALO
P_ROWS = ROWS + 2 * P_HALO
G_ROWS = ROWS + 2 * G_HALO

GX = ("y", "x_hi", "core")
GY = ("x_lo", "z")
NEAR = ("y", "x_hi", "core", "x_lo")
FAR = "z"

tiny_floor = 1e-06
f32 = jnp.float32
bf16 = jnp.bfloat16


SPACES = {"s": pltpu.SMEM, "v": pltpu.VMEM, "h": pltpu.HBM}


def kernel(body, ins, outs, cost, scratch=(), limit=32 * 2**20, space=pltpu.VMEM):
    return pl.pallas_call(
        body,
        in_specs=[pl.BlockSpec(memory_space=SPACES[kind]) for kind in ins],
        out_specs=[pl.BlockSpec(memory_space=space) for _ in outs],
        out_shape=[jax.ShapeDtypeStruct(shape, dtype) for shape, dtype in outs],
        scratch_shapes=list(scratch),
        compiler_params=pltpu.CompilerParams(vmem_limit_bytes=limit),
        cost_estimate=pl.CostEstimate(flops=cost, bytes_accessed=cost // 100, transcendentals=0),
    )


def index(axes):
    place = 0
    for axis in axes:
        place = place * lax.axis_size(axis) + lax.axis_index(axis)
    return place


def roll(x, by):
    by = by % 128
    return x if by == 0 else pltpu.roll(x, by, axis=x.ndim - 1)


def lane_of(shape):
    return lax.broadcasted_iota(jnp.int32, shape, len(shape) - 1)


def split(x):
    high = x.astype(bf16)
    return high, (x - high.astype(f32)).astype(bf16)


def dot(a, b):
    return jnp.dot(a, b, preferred_element_type=f32)


def dot_right(x, w):
    high, low = split(x)
    return dot(jnp.concatenate([high, low, high], axis=1), w)


def stacked(x, depth):
    high, low = split(x)
    parts = [high, low, high]
    spare = depth - 3 * x.shape[0]
    if spare:
        parts.append(jnp.zeros((spare, x.shape[1]), bf16))
    return jnp.concatenate(parts, axis=0)


def side_position(index, halo):
    left = index - COLS - halo
    right = index - halo
    position = jnp.where(index < COLS, index, jnp.where(index < COLS + halo, left, right))
    return jnp.where(index < COLS + 2 * halo, position, 1 << 20)


def tap_matrix(taps_ref, offset):
    out = jnp.zeros(offset.shape, f32)
    for t in range(TAPS):
        out = jnp.where(offset == t, taps_ref[t], out)
    return out


def inside(position, base, size):
    where = position + base
    return jnp.logical_and(where >= 0, where < size)


def exact_dot(a, b):
    return lax.dot_general(a, b, (((1,), (0,)), ((), ())), precision=lax.Precision.HIGHEST, preferred_element_type=f32)


def rows_cols(shape):
    return lax.broadcasted_iota(jnp.int32, shape, 0), lax.broadcasted_iota(jnp.int32, shape, 1)


def put_right(x, ref):
    high, low = split(x)
    rows = x.shape[0]
    ref[:rows, :] = high
    ref[rows : 2 * rows, :] = high
    ref[2 * rows :, :] = low


def put_left(x, part, ref):
    high, low = split(x)
    ref[...] = jnp.where(part < 2, high.astype(f32), low.astype(f32)).astype(bf16)


def y_matrices_body(size_y, ty_ref, my, py, by):
    base_y = index(GY) * COLS
    r, c = rows_cols((256, 256))
    source = side_position(r, P_HALO)
    target = side_position(c, G_HALO)
    okay = jnp.logical_and(inside(source, base_y, size_y), inside(target, base_y, size_y))
    put_right(jnp.where(okay, tap_matrix(ty_ref, target - source + HALF), 0.0), py)
    source = side_position(r, A_HALO)
    middle = c - P_HALO
    okay = jnp.logical_and(inside(source, base_y, size_y), inside(middle, base_y, size_y))
    first = jnp.where(okay, tap_matrix(ty_ref, source - middle + HALF), 0.0)
    middle = r - P_HALO
    second = jnp.where(inside(target, base_y, size_y), tap_matrix(ty_ref, target - middle + HALF), 0.0)
    put_right(exact_dot(first, second), my)
    r, c = rows_cols((256, 128))
    source = side_position(r, G_HALO)
    okay = inside(source, base_y, size_y)
    put_right(jnp.where(okay, tap_matrix(ty_ref, source - c + HALF), 0.0), by)


def x_matrices_body(size_x, tx_ref, spectra_ref, after_ref, gram_ref, mx, px, bx):
    spectra = spectra_ref[...]
    gram_ref[...] = lax.dot_general(
        spectra, spectra, (((1,), (1,)), ((), ())), precision=lax.Precision.HIGHEST, preferred_element_type=f32
    )
    base_x = index(GX) * ROWS
    r, c = rows_cols((128, 512))
    part = c // A_ROWS
    source = c - part * A_ROWS - A_HALO
    middle = r - P_HALO
    okay = jnp.logical_and(inside(source, base_x, size_x), inside(middle, base_x, size_x))
    okay = jnp.logical_and(okay, part < 3)
    first = jnp.where(okay, tap_matrix(tx_ref, source - middle + HALF), 0.0)
    r, c = rows_cols((G_ROWS, 128))
    target = r - G_HALO
    middle = c - P_HALO
    second = jnp.where(inside(target, base_x, size_x), tap_matrix(tx_ref, target - middle + HALF), 0.0)
    r, c = rows_cols((G_ROWS, 512))
    put_left(exact_dot(second, first), c // A_ROWS, mx)
    r, c = rows_cols((G_ROWS, 384))
    part = c // P_ROWS
    source = c - part * P_ROWS - P_HALO
    target = r - G_HALO
    okay = jnp.logical_and(inside(source, base_x, size_x), inside(target, base_x, size_x))
    put_left(jnp.where(okay, tap_matrix(tx_ref, target - source + HALF), 0.0), part, px)
    r, c = rows_cols((ROWS, 384))
    part = c // G_ROWS
    source = c - part * G_ROWS - G_HALO
    okay = jnp.logical_and(inside(source, base_x, size_x), part < 3)
    put_left(jnp.where(okay, tap_matrix(tx_ref, source - r + HALF), 0.0), part, bx)


def choose(odd, if_odd, if_even):
    return jnp.where(odd == 1, if_odd, if_even)


def edge_rows(odd_x, pairing, depth):
    top = odd_x == 1 if pairing == 0 else odd_x == 0
    return pl.multiple_of(jnp.where(top, 0, ROWS - depth), 16)


def project_body(
    s_hbm, a_hbm, m_hbm, p_hbm, xb_hbm, xa_hbm, ya_hbm, yb_hbm,
    spectra_ref, a_ref, m_ref, p_ref, ya_ref, yb_ref, sems, out_sems,
):
    step = 32
    copy_s = pltpu.make_async_copy(s_hbm, spectra_ref, sems.at[5])
    copy_s.start()
    copies = [
        pltpu.make_async_copy(m_hbm.at[:, pl.ds(k * step, step), :], m_ref.at[:, pl.ds(k * step, step), :], sems.at[k])
        for k in range(ROWS // step)
    ]
    for copy in copies:
        copy.start()
    copy_a = pltpu.make_async_copy(a_hbm, a_ref, sems.at[ROWS // step])
    copy_a.start()
    odd_x = index(GX) % 2
    edges = []
    copy_s.wait()
    for k, copy in enumerate(copies):
        copy.wait()
        start = k * step
        acc = [jnp.zeros((step, COLS), f32) for _ in range(FLUOR)]
        for c in range(CHAN):
            seen = m_ref[c, start : start + step, :].astype(f32)
            for f in range(FLUOR):
                acc[f] = acc[f] + spectra_ref[f, c] * seen
        for f in range(FLUOR):
            p_ref[f, start : start + step, :] = acc[f]
        if k == 0:
            copy_a.wait()
            for pairing, x_hbm in ((1, xb_hbm), (0, xa_hbm)):
                rows = pl.ds(edge_rows(odd_x, pairing, A_HALO), A_HALO)
                edges.append(
                    pltpu.make_async_copy(a_ref.at[:, rows, :], x_hbm.at[:, pl.ds(0, A_HALO), :], out_sems.at[pairing])
                )
                edges[-1].start()
    for k, x_hbm in ((1, xb_hbm), (0, xa_hbm)):
        rows = pl.ds(edge_rows(odd_x, k, P_HALO), P_HALO)
        edges.append(
            pltpu.make_async_copy(p_ref.at[:, rows, :], x_hbm.at[:, pl.ds(A_HALO, P_HALO), :], out_sems.at[2 + k])
        )
        edges[-1].start()
    edges.append(pltpu.make_async_copy(p_ref, p_hbm, out_sems.at[4]))
    edges[-1].start()
    odd_y = index(GY) % 2
    lane = lane_of((32, 128))
    lane8 = lane_of((8, 128))
    for f in range(FLUOR):
        sides = []
        for a_from, p_from in ((0, 0), (COLS - A_HALO, COLS - P_HALO)):
            top = roll(a_ref[f, :32, :], -a_from)
            low = roll(a_ref[f, 32:, :], A_HALO - a_from)
            side = roll(p_ref[f, :32, :], 2 * A_HALO - p_from)
            main = jnp.where(lane < A_HALO, top, jnp.where(lane < 2 * A_HALO, low, side))
            rest = roll(p_ref[f, 32:40, :], -p_from)
            for k in range(1, 4):
                piece = roll(p_ref[f, 32 + 8 * k : 40 + 8 * k, :], 32 * k - p_from)
                rest = jnp.where(lane8 < 32 * k, rest, piece)
            sides.append((main, rest))
        (left, left_rest), (right, right_rest) = sides
        ya_ref[f, :32, :] = choose(odd_y, left, right)
        yb_ref[f, :32, :] = choose(odd_y, right, left)
        ya_ref[f, 32:, :] = choose(odd_y, left_rest, right_rest)
        yb_ref[f, 32:, :] = choose(odd_y, right_rest, left_rest)
    for k, (ref, y_hbm) in enumerate(((ya_ref, ya_hbm), (yb_ref, yb_hbm))):
        edges.append(pltpu.make_async_copy(ref, y_hbm, out_sems.at[5 + k]))
        edges[-1].start()
    for copy in edges:
        copy.wait()


def pack_corner(odd_x, pairing, side_ref, ps_ref, out_ref):
    lane = lane_of((32, 128))
    lane8 = lane_of((8, 128))
    lane16 = lane_of((16, 128))
    spare = 2 * A_HALO
    a_rows = pl.ds(edge_rows(odd_x, pairing, A_HALO), A_HALO)
    p_rows = pl.ds(edge_rows(odd_x, pairing, P_HALO), P_HALO)
    for f in range(FLUOR):
        p_top = ps_ref[f, p_rows, :]
        a_side = side_ref[f, a_rows, :]
        out_ref[f, :32, :] = jnp.where(lane < spare, a_side[:32], roll(p_top, spare))
        out_ref[f, 32:48, :] = jnp.where(lane16 < spare, a_side[32:], roll(p_top[:16], spare - P_HALO))
        out_ref[f, 48:, :] = jnp.where(lane8 < P_HALO, roll(p_top[16:24], -P_HALO), p_top[24:])


def corner_body(ya_ref, yb_ref, side_ref, ps_ref, cb_ref, ca_ref):
    odd_x = index(GX) % 2
    odd_y = index(GY) % 2
    lane = lane_of((32, 128))
    lane8 = lane_of((8, 128))
    for f in range(FLUOR):
        first = ya_ref[f, :32, :]
        second = yb_ref[f, :32, :]
        left = choose(odd_y, first, second)
        right = choose(odd_y, second, first)
        side_ref[f, :32, :] = jnp.where(lane < A_HALO, left, jnp.where(lane < 2 * A_HALO, roll(right, A_HALO), 0.0))
        side_ref[f, 32:, :] = jnp.where(lane < A_HALO, roll(left, -A_HALO), jnp.where(lane < 2 * A_HALO, right, 0.0))
        ps_ref[f, :32, :] = jnp.where(
            lane < P_HALO, roll(left, -2 * A_HALO), jnp.where(lane < 2 * P_HALO, roll(right, P_HALO - 2 * A_HALO), 0.0)
        )
        first = ya_ref[f, 32:, :]
        second = yb_ref[f, 32:, :]
        left = choose(odd_y, first, second)
        right = choose(odd_y, second, first)
        for k in range(4):
            ps_ref[f, 32 + 8 * k : 40 + 8 * k, :] = jnp.where(
                lane8 < P_HALO, roll(left, -32 * k), jnp.where(lane8 < 2 * P_HALO, roll(right, P_HALO - 32 * k), 0.0)
            )
    pack_corner(odd_x, 0, side_ref, ps_ref, ca_ref)
    pack_corner(odd_x, 1, side_ref, ps_ref, cb_ref)


GROUP = 4


def along_y(x, w, put):
    for f in range(0, FLUOR, GROUP):
        part = x(slice(f, f + GROUP))
        out = dot_right(part.reshape(-1, part.shape[2]), w)
        out = out.reshape(GROUP, part.shape[1], out.shape[1])
        for k in range(GROUP):
            put(f + k, out[k])


X_GROUP = 4


def along_x(m, stack, out_ref):
    for f in range(0, FLUOR, X_GROUP):
        out = dot(m, jnp.concatenate([stack(f + k) for k in range(X_GROUP)], axis=1))
        for k in range(X_GROUP):
            out_ref[f + k] = out[:, 256 * k : 256 * k + 256]


def wide(main, side):
    return jnp.concatenate([main, side], axis=2)


def mix(gram_ref, v_ref, d_ref, g_ref):
    step = 8

    def mixed(part, f):
        acc = gram_ref[f, 0] * part[0]
        for k in range(1, FLUOR):
            acc = acc + gram_ref[f, k] * part[k]
        return acc

    for start in range(0, G_ROWS, step):
        part = [v_ref[f, start : start + step, :COLS] for f in range(FLUOR)]
        for f in range(FLUOR):
            g_ref[f, start : start + step, :COLS] = mixed(part, f) - d_ref[f, start : start + step, :COLS]
    lane = lane_of((step, 128))
    group = G_ROWS // 4
    for start in range(0, group, step):
        rows = [slice(k * group + start, k * group + start + step) for k in range(4)]
        part = []
        for f in range(FLUOR):
            packed = v_ref[f, rows[0], COLS:]
            for k in range(1, 4):
                packed = packed + roll(v_ref[f, rows[k], COLS:], 32 * k)
            part.append(packed)
        for f in range(FLUOR):
            out = mixed(part, f)
            for k in range(4):
                side = jnp.where(lane < 2 * G_HALO, roll(out, -32 * k), 0.0)
                g_ref[f, rows[k], COLS:] = side - d_ref[f, rows[k], COLS:]


def sums(gram_ref, g_ref, by, bx, y_ref, z_ref, sum_ref):
    along_x(bx[...], lambda f: stacked(g_ref[f], 384), y_ref)

    def put(f, z):
        z_ref[f] = z

    along_y(lambda part: y_ref[part], by[...], put)
    grad = jnp.zeros((8, 128), f32)
    image = jnp.zeros((8, 128), f32)
    for start in range(0, ROWS, 8):
        part = [z_ref[f, start : start + 8, :] for f in range(FLUOR)]
        for f in range(FLUOR):
            acc = gram_ref[f, 0] * part[0]
            for k in range(1, FLUOR):
                acc = acc + gram_ref[f, k] * part[k]
            image = image + acc * part[f]
            g = g_ref[f, G_HALO + start : G_HALO + start + 8, :COLS]
            grad = grad + g * g
    grad = jnp.sum(grad, axis=0, keepdims=True)
    image = jnp.sum(image, axis=0, keepdims=True)
    lane = lane_of((1, 128))
    row = jnp.where(lane < 64, grad + roll(grad, 64), image + roll(image, 64))
    sum_ref[...] = jnp.broadcast_to(row, sum_ref.shape)


def step_length(total_ref):
    total = jnp.sum(total_ref[...], axis=0, keepdims=True)
    lane = lane_of((1, 128))
    grad = jnp.sum(jnp.where(lane < 64, total, 0.0), axis=1, keepdims=True)
    image = jnp.sum(jnp.where(lane < 64, 0.0, total), axis=1, keepdims=True)
    return grad / (image + tiny_floor)


def put_stack(ref, f, start, depth, x):
    high, low = split(x)
    for at, part in ((0, high), (depth, low), (2 * depth, high)):
        ref[f, pl.ds(pl.multiple_of(start + at, 16), x.shape[0]), :] = part


def along_half(x, w_ref, start, put):
    w = jnp.concatenate([w_ref[256 * k + start : 256 * k + start + 128, :] for k in range(3)], axis=0)
    along_y(x, w, put)


def store(ref):
    def put(f, x):
        ref[f] = x

    return put


def own_body(a_ref, side_ref, p_ref, ps_ref, xb_ref, my, py, u_ref, w_ref, ub_ref, wb_ref):
    along_y(lambda part: wide(p_ref[part], ps_ref[part]), py[...], store(w_ref))
    along_y(lambda part: wide(a_ref[part], side_ref[part]), my[...], store(u_ref))
    along_half(lambda part: xb_ref[part, :A_HALO, :], my, 0, store(ub_ref))
    along_half(lambda part: xb_ref[part, A_HALO:, :], py, 0, store(wb_ref))


def first_rows_body(xa_ref, my, py, ua_ref, wa_ref):
    along_half(lambda part: xa_ref[part, :A_HALO, :], my, 0, store(ua_ref))
    along_half(lambda part: xa_ref[part, A_HALO:, :], py, 0, store(wa_ref))


def first_body(
    gram_ref, u_ref, w_ref, ua_ref, ub_ref, wa_ref, wb_ref, cb_ref, ca_ref, my, py, mx, px,
    d_ref, g_ref, ya_ref, yb_ref, v_ref, su_ref, sw_ref, side_ref,
):
    odd_x = index(GX) % 2
    odd_y = index(GY) % 2
    lane = lane_of((32, 128))
    lane16 = lane_of((16, 128))
    lane8 = lane_of((8, 128))
    spare = 2 * A_HALO
    su_ref[:, 3 * A_ROWS :, :] = jnp.zeros((FLUOR, 512 - 3 * A_ROWS, 256), bf16)
    for u_part, w_part, corner, above in (
        (ua_ref, wa_ref, ca_ref, odd_x == 1),
        (ub_ref, wb_ref, cb_ref, odd_x == 0),
    ):
        for f in range(FLUOR):
            left = roll(corner[f, :32, :], -spare)
            right = roll(corner[f, 32:48, :], P_HALO - spare)
            last = corner[f, 48:, :]
            side_ref[f, :16, :] = jnp.where(lane16 < P_HALO, left[:16], jnp.where(lane16 < 2 * P_HALO, right, 0.0))
            side_ref[f, 16:24, :] = jnp.where(
                lane8 < P_HALO, left[16:24], jnp.where(lane8 < 2 * P_HALO, roll(last, P_HALO), 0.0)
            )
            side_ref[f, 24:, :] = jnp.where(lane8 < P_HALO, left[24:], jnp.where(lane8 < 2 * P_HALO, last, 0.0))
        a_at = jnp.where(above, 0, A_HALO + ROWS)
        p_at = jnp.where(above, 0, P_HALO + ROWS)
        along_half(
            lambda part: side_ref[part],
            py,
            128,
            lambda f, x: put_stack(sw_ref, f, p_at, P_ROWS, x + w_part[f]),
        )
        along_half(
            lambda part: corner[part, :A_HALO, :],
            my,
            128,
            lambda f, x: put_stack(su_ref, f, a_at, A_ROWS, x + u_part[f]),
        )
    for f in range(FLUOR):
        put_stack(sw_ref, f, P_HALO, P_ROWS, w_ref[f])
        put_stack(su_ref, f, A_HALO, A_ROWS, u_ref[f])
    along_x(px[...], lambda f: sw_ref[f], d_ref)
    along_x(mx[...], lambda f: su_ref[f], v_ref)
    mix(gram_ref, v_ref, d_ref, g_ref)
    lane = lane_of((24, 128))
    for f in range(FLUOR):
        edges = []
        for start in (G_HALO, COLS - G_HALO - 32):
            out = roll(g_ref[f, :24, :COLS], -start)
            for k in range(1, 4):
                piece = roll(g_ref[f, 24 * k : 24 * k + 24, :COLS], 32 * k - start)
                out = jnp.where(lane < 32 * k, out, piece)
            edges.append(out)
        ya_ref[f] = choose(odd_y, edges[0], edges[1])
        yb_ref[f] = choose(odd_y, edges[1], edges[0])


def probe_body(gram_ref, g_ref, by, bx, sum_ref, y_ref, z_ref):
    sums(gram_ref, g_ref, by, bx, y_ref, z_ref, sum_ref)


def relay(near_ref, out_ref):
    out_ref[...] = jnp.broadcast_to(jnp.sum(near_ref[...], axis=0, keepdims=True), out_ref.shape)


def outer_body(near_ref, g_ref, ya_ref, yb_ref, far_ref, side_ref, send_ref):
    relay(near_ref, far_ref)
    odd_y = index(GY) % 2
    lane = lane_of((24, 128))
    for f in range(FLUOR):
        left = choose(odd_y, ya_ref[f], yb_ref[f])
        right = choose(odd_y, yb_ref[f], ya_ref[f])
        for k in range(4):
            own = roll(g_ref[f, 24 * k : 24 * k + 24, COLS:], 32)
            side_ref[f, 24 * k : 24 * k + 24, :] = jnp.where(
                lane < 32,
                roll(left, -32 * k),
                jnp.where(lane < 64, own, jnp.where(lane < 96, roll(right, 64 - 32 * k), 0.0)),
            )
        send_ref[f, :32, :] = g_ref[f, 2 * G_HALO : 2 * G_HALO + 32, :COLS]
        send_ref[f, 32:, :] = side_ref[f, 2 * G_HALO : 2 * G_HALO + 32, :]


def second_body(
    gram_ref, total_ref, a_ref, side_ref, za_ref, zb_ref, ca_ref, cb_ref, d_ref, g_ref, gs_ref, xa_ref, xb_ref,
    my, mx, by, bx,
    a_out, g_out, sum_ref, v_ref, n_ref, y_ref, z_ref, x_ref, u_ref,
):
    odd_x = index(GX) % 2
    t = step_length(total_ref)
    for f in range(FLUOR):
        tile = jnp.maximum(a_ref[f] - t * g_ref[f, G_HALO : G_HALO + ROWS, :COLS], 0.0)
        a_out[f] = tile
        x_ref[f, A_HALO : A_HALO + ROWS, :COLS] = tile
        x_ref[f, A_HALO : A_HALO + ROWS, COLS:] = jnp.maximum(
            side_ref[f] - t * gs_ref[f, G_HALO : G_HALO + ROWS, :], 0.0
        )
        for above, main, corner, far, near in (
            (True, choose(odd_x, za_ref[f, :A_HALO, :], zb_ref[f, :A_HALO, :]),
             choose(odd_x, ca_ref[f, :A_HALO, :], cb_ref[f, :A_HALO, :]), choose(odd_x, xa_ref[f], xb_ref[f]),
             slice(0, G_HALO)),
            (False, choose(odd_x, zb_ref[f, :A_HALO, :], za_ref[f, :A_HALO, :]),
             choose(odd_x, cb_ref[f, :A_HALO, :], ca_ref[f, :A_HALO, :]), choose(odd_x, xb_ref[f], xa_ref[f]),
             slice(G_ROWS - G_HALO, G_ROWS)),
        ):
            parts = [far[:32], g_ref[f, near, :COLS]], [far[32:], gs_ref[f, near, :]]
            if not above:
                parts = [part[::-1] for part in parts]
            rows = slice(0, A_HALO) if above else slice(A_HALO + ROWS, A_ROWS)
            x_ref[f, rows, :COLS] = jnp.maximum(main - t * jnp.concatenate(parts[0], axis=0), 0.0)
            x_ref[f, rows, COLS:] = jnp.maximum(corner - t * jnp.concatenate(parts[1], axis=0), 0.0)

    def put(f, u):
        u_ref[f] = u

    along_y(lambda part: x_ref[part], my[...], put)
    along_x(mx[...], lambda f: stacked(u_ref[f], 512), v_ref)
    mix(gram_ref, v_ref, d_ref, n_ref)
    sums(gram_ref, n_ref, by, bx, y_ref, z_ref, sum_ref)
    for f in range(FLUOR):
        g_out[f] = n_ref[f, G_HALO : G_HALO + ROWS, :COLS]


def last_body(total_ref, a_ref, g_ref, out_ref):
    t = step_length(total_ref)
    for f in range(FLUOR):
        out_ref[f] = jnp.maximum(a_ref[f] - t * g_ref[f], 0.0)


TILE = (FLUOR, ROWS, COLS)
G_SHAPE = (FLUOR, G_ROWS, 256)
PROBE_SCRATCH = (pltpu.VMEM((FLUOR, ROWS, 256), f32), pltpu.VMEM(TILE, f32))
OWN_COST = 10**10
NEAR_COUNT = 32
FAR_COUNT = 16

first_call = kernel(
    first_body,
    "s" + "v" * 12,
    [(G_SHAPE, f32)] * 2 + [((FLUOR, 24, 128), f32)] * 2,
    10**9,
    [
        pltpu.VMEM(G_SHAPE, f32),
        pltpu.VMEM((FLUOR, 512, 256), bf16),
        pltpu.VMEM((FLUOR, 3 * P_ROWS, 256), bf16),
        pltpu.VMEM((FLUOR, P_HALO, 128), f32),
    ],
)
probe_call = kernel(probe_body, "svvv", [((NEAR_COUNT, 128), f32)], 10**9, PROBE_SCRATCH)
second_call = kernel(
    second_body,
    "s" + "v" * 16,
    [(TILE, f32)] * 2 + [((NEAR_COUNT, 128), f32)],
    10**9,
    [
        pltpu.VMEM(G_SHAPE, f32),
        pltpu.VMEM(G_SHAPE, f32),
        *PROBE_SCRATCH,
        pltpu.VMEM((FLUOR, A_ROWS, 256), f32),
        pltpu.VMEM((FLUOR, A_ROWS, 256), f32),
    ],
)


def length(axes):
    count = 1
    for axis in axes:
        count *= lax.axis_size(axis)
    return count


def trade(first, second, axes):
    return trade_first(first, axes), trade_second(second, axes)


def trade_first(edge, axes):
    return lax.ppermute(edge, axes, [(i, i ^ 1) for i in range(length(axes))])


def trade_second(edge, axes):
    count = length(axes)
    return lax.ppermute(edge, axes, [(i, (i + (1 if i % 2 else -1)) % count) for i in range(count)])


def spread(rows, axes):
    got = lax.all_to_all(rows.reshape(rows.shape[0], 1, 128), axes, 0, 0, tiled=True)
    return got.reshape(rows.shape[0], 128)


def local(sizes, abundance_start, measured, spectra, taps_x, taps_y):
    assert (length(NEAR), length((FAR,))) == (NEAR_COUNT, FAR_COUNT)

    edge = (FLUOR, A_HALO + P_HALO, 128)
    a0 = abundance_start[0]
    p, xb, xa, ya, yb = kernel(
        project_body,
        "hhh",
        [(TILE, f32)] + [(edge, f32)] * 2 + [((FLUOR, 40, 128), f32)] * 2,
        10**7,
        [
            pltpu.SMEM((FLUOR, CHAN), f32),
            pltpu.VMEM(TILE, f32),
            pltpu.VMEM((CHAN, ROWS, COLS), bf16),
            pltpu.VMEM(TILE, f32),
            pltpu.VMEM((FLUOR, 40, 128), f32),
            pltpu.VMEM((FLUOR, 40, 128), f32),
            pltpu.SemaphoreType.DMA((6,)),
            pltpu.SemaphoreType.DMA((7,)),
        ],
        60_000_000,
        pltpu.HBM,
    )(spectra.T, a0, measured[0])
    za, zb = trade(xa, xb, GX)
    ya, yb = trade(ya, yb, GY)
    my, py, by = kernel(
        functools.partial(y_matrices_body, sizes[1]),
        "s",
        [((768, 256), bf16)] * 2 + [((768, 128), bf16)],
        10**9,
    )(taps_y)
    corner = (FLUOR, 56, 128)
    side, ps, cb, ca = kernel(corner_body, "vv", [(TILE, f32)] * 2 + [(corner, f32)] * 2, 10**7)(ya, yb)
    ca, cb = trade(ca, cb, GX)
    gram, mx, px, bx = kernel(
        functools.partial(x_matrices_body, sizes[0]),
        "svv",
        [((FLUOR, FLUOR), f32), ((G_ROWS, 512), bf16), ((G_ROWS, 384), bf16), ((ROWS, 384), bf16)],
        10**9,
    )(taps_x, spectra.T, ps)
    u, w, ub, wb = kernel(
        own_body,
        "v" * 7,
        [((FLUOR, rows, 256), f32) for rows in (ROWS, ROWS, A_HALO, P_HALO)],
        OWN_COST,
    )(a0, side, p, ps, zb, my, py)
    ua, wa = kernel(first_rows_body, "vvv", [((FLUOR, rows, 256), f32) for rows in (A_HALO, P_HALO)], 10**7)(za, my, py)
    d, g, ya, yb = first_call(gram, u, w, ua, ub, wa, wb, cb, ca, my, py, mx, px)
    ya, yb = trade(ya, yb, GY)
    (partial,) = probe_call(gram, g, by, bx)
    near = spread(partial, NEAR)
    far, g_side, send = kernel(
        outer_body,
        "vvvv",
        [((FAR_COUNT, 128), f32), ((FLUOR, G_ROWS, 128), f32), ((FLUOR, 64, 128), f32)],
        10**8,
    )(near, g, ya, yb)
    xa, xb = trade(send, send, GX)
    total = spread(far, FAR)
    a1, g1, partial = second_call(
        gram, total, a0, side, za, zb, ca, cb, d, g, g_side, xa, xb, my, mx, by, bx
    )
    (far,) = kernel(relay, "v", [((FAR_COUNT, 128), f32)], 10**6)(spread(partial, NEAR))
    total = spread(far, FAR)
    (out,) = kernel(last_body, "vvv", [(TILE, f32)], 10**7)(total, a1, g1)
    return out[None]


def solution(mesh):
    count_x, count_y = mesh.shape["gx"], mesh.shape["gy"]
    parts = Mesh(
        mesh.devices.reshape(count_x // 4, 2, 2, 2, count_y // 2), ("y", "x_hi", "core", "x_lo", "z")
    )
    sizes = (count_x * ROWS, count_y * COLS)
    tiles = P(None, None, GX, GY)
    return jax.shard_map(
        functools.partial(local, sizes),
        mesh=parts,
        in_specs=(tiles, tiles, P(), P(), P()),
        out_specs=tiles,
        check_vma=False,
    )
```

```python
import functools

import jax
import jax.numpy as jnp
from jax import lax
from jax.experimental import pallas as pl
from jax.experimental.pallas import tpu as pltpu
from jax.sharding import Mesh
from jax.sharding import PartitionSpec as P

TAPS = 33
ITERS = 2
FLUOR = 12
CHAN = 32
ROWS = 64
COLS = 128

HALF = TAPS // 2
A_HALO = 3 * HALF
P_HALO = 2 * HALF
G_HALO = HALF
A_ROWS = ROWS + 2 * A_HALO
P_ROWS = ROWS + 2 * P_HALO
G_ROWS = ROWS + 2 * G_HALO

GX = ("y", "x_hi", "core")
GY = ("x_lo", "z")
NEAR = ("y", "x_hi", "core", "x_lo")
FAR = "z"

tiny_floor = 1e-06
f32 = jnp.float32
bf16 = jnp.bfloat16


SPACES = {"s": pltpu.SMEM, "v": pltpu.VMEM, "h": pltpu.HBM}


def kernel(body, ins, outs, cost, scratch=(), limit=32 * 2**20, space=pltpu.VMEM):
    return pl.pallas_call(
        body,
        in_specs=[pl.BlockSpec(memory_space=SPACES[kind]) for kind in ins],
        out_specs=[pl.BlockSpec(memory_space=space) for _ in outs],
        out_shape=[jax.ShapeDtypeStruct(shape, dtype) for shape, dtype in outs],
        scratch_shapes=list(scratch),
        compiler_params=pltpu.CompilerParams(vmem_limit_bytes=limit),
        cost_estimate=pl.CostEstimate(flops=cost, bytes_accessed=cost // 100, transcendentals=0),
    )


def index(axes):
    place = 0
    for axis in axes:
        place = place * lax.axis_size(axis) + lax.axis_index(axis)
    return place


def roll(x, by):
    by = by % 128
    return x if by == 0 else pltpu.roll(x, by, axis=x.ndim - 1)


def lane_of(shape):
    return lax.broadcasted_iota(jnp.int32, shape, len(shape) - 1)


def split(x):
    high = x.astype(bf16)
    return high, (x - high.astype(f32)).astype(bf16)


def dot(a, b):
    return jnp.dot(a, b, preferred_element_type=f32)


def dot_right(x, w):
    high, low = split(x)
    return dot(jnp.concatenate([high, low, high], axis=1), w)


def stacked(x, depth):
    high, low = split(x)
    parts = [high, low, high]
    spare = depth - 3 * x.shape[0]
    if spare:
        parts.append(jnp.zeros((spare, x.shape[1]), bf16))
    return jnp.concatenate(parts, axis=0)


def side_position(index, halo):
    left = index - COLS - halo
    right = index - halo
    position = jnp.where(index < COLS, index, jnp.where(index < COLS + halo, left, right))
    return jnp.where(index < COLS + 2 * halo, position, 1 << 20)


def tap_matrix(taps_ref, offset):
    out = jnp.zeros(offset.shape, f32)
    for t in range(TAPS):
        out = jnp.where(offset == t, taps_ref[t], out)
    return out


def inside(position, base, size):
    where = position + base
    return jnp.logical_and(where >= 0, where < size)


def exact_dot(a, b):
    return lax.dot_general(a, b, (((1,), (0,)), ((), ())), precision=lax.Precision.HIGHEST, preferred_element_type=f32)


def rows_cols(shape):
    return lax.broadcasted_iota(jnp.int32, shape, 0), lax.broadcasted_iota(jnp.int32, shape, 1)


def put_right(x, ref):
    high, low = split(x)
    rows = x.shape[0]
    ref[:rows, :] = high
    ref[rows : 2 * rows, :] = high
    ref[2 * rows :, :] = low


def put_left(x, part, ref):
    high, low = split(x)
    ref[...] = jnp.where(part < 2, high.astype(f32), low.astype(f32)).astype(bf16)


def y_matrices_body(size_y, ty_ref, my, py, by):
    base_y = index(GY) * COLS
    r, c = rows_cols((256, 256))
    source = side_position(r, P_HALO)
    target = side_position(c, G_HALO)
    okay = jnp.logical_and(inside(source, base_y, size_y), inside(target, base_y, size_y))
    put_right(jnp.where(okay, tap_matrix(ty_ref, target - source + HALF), 0.0), py)
    source = side_position(r, A_HALO)
    middle = c - P_HALO
    okay = jnp.logical_and(inside(source, base_y, size_y), inside(middle, base_y, size_y))
    first = jnp.where(okay, tap_matrix(ty_ref, source - middle + HALF), 0.0)
    middle = r - P_HALO
    second = jnp.where(inside(target, base_y, size_y), tap_matrix(ty_ref, target - middle + HALF), 0.0)
    put_right(exact_dot(first, second), my)
    r, c = rows_cols((256, 128))
    source = side_position(r, G_HALO)
    okay = inside(source, base_y, size_y)
    put_right(jnp.where(okay, tap_matrix(ty_ref, source - c + HALF), 0.0), by)


def x_matrices_body(size_x, tx_ref, spectra_ref, after_ref, gram_ref, mx, px, bx):
    spectra = spectra_ref[...]
    gram_ref[...] = lax.dot_general(
        spectra, spectra, (((1,), (1,)), ((), ())), precision=lax.Precision.HIGHEST, preferred_element_type=f32
    )
    base_x = index(GX) * ROWS
    r, c = rows_cols((128, 512))
    part = c // A_ROWS
    source = c - part * A_ROWS - A_HALO
    middle = r - P_HALO
    okay = jnp.logical_and(inside(source, base_x, size_x), inside(middle, base_x, size_x))
    okay = jnp.logical_and(okay, part < 3)
    first = jnp.where(okay, tap_matrix(tx_ref, source - middle + HALF), 0.0)
    r, c = rows_cols((G_ROWS, 128))
    target = r - G_HALO
    middle = c - P_HALO
    second = jnp.where(inside(target, base_x, size_x), tap_matrix(tx_ref, target - middle + HALF), 0.0)
    r, c = rows_cols((G_ROWS, 512))
    put_left(exact_dot(second, first), c // A_ROWS, mx)
    r, c = rows_cols((G_ROWS, 384))
    part = c // P_ROWS
    source = c - part * P_ROWS - P_HALO
    target = r - G_HALO
    okay = jnp.logical_and(inside(source, base_x, size_x), inside(target, base_x, size_x))
    put_left(jnp.where(okay, tap_matrix(tx_ref, target - source + HALF), 0.0), part, px)
    r, c = rows_cols((ROWS, 384))
    part = c // G_ROWS
    source = c - part * G_ROWS - G_HALO
    okay = jnp.logical_and(inside(source, base_x, size_x), part < 3)
    put_left(jnp.where(okay, tap_matrix(tx_ref, source - r + HALF), 0.0), part, bx)


def choose(odd, if_odd, if_even):
    return jnp.where(odd == 1, if_odd, if_even)


def edge_rows(odd_x, pairing, depth):
    top = odd_x == 1 if pairing == 0 else odd_x == 0
    return pl.multiple_of(jnp.where(top, 0, ROWS - depth), 16)


def project_body(
    s_hbm, a_hbm, m_hbm, p_hbm, xb_hbm, xa_hbm, ya_hbm, yb_hbm,
    spectra_ref, a_ref, m_ref, p_ref, ya_ref, yb_ref, sems, out_sems,
):
    step = 32
    copy_s = pltpu.make_async_copy(s_hbm, spectra_ref, sems.at[5])
    copy_s.start()
    copies = [
        pltpu.make_async_copy(m_hbm.at[:, pl.ds(k * step, step), :], m_ref.at[:, pl.ds(k * step, step), :], sems.at[k])
        for k in range(ROWS // step)
    ]
    for copy in copies:
        copy.start()
    copy_a = pltpu.make_async_copy(a_hbm, a_ref, sems.at[ROWS // step])
    copy_a.start()
    odd_x = index(GX) % 2
    edges = []
    copy_s.wait()
    for k, copy in enumerate(copies):
        copy.wait()
        start = k * step
        acc = [jnp.zeros((step, COLS), f32) for _ in range(FLUOR)]
        for c in range(CHAN):
            seen = m_ref[c, start : start + step, :].astype(f32)
            for f in range(FLUOR):
                acc[f] = acc[f] + spectra_ref[f, c] * seen
        for f in range(FLUOR):
            p_ref[f, start : start + step, :] = acc[f]
        if k == 0:
            copy_a.wait()
            for pairing, x_hbm in ((1, xb_hbm), (0, xa_hbm)):
                rows = pl.ds(edge_rows(odd_x, pairing, A_HALO), A_HALO)
                edges.append(
                    pltpu.make_async_copy(a_ref.at[:, rows, :], x_hbm.at[:, pl.ds(0, A_HALO), :], out_sems.at[pairing])
                )
                edges[-1].start()
    for k, x_hbm in ((1, xb_hbm), (0, xa_hbm)):
        rows = pl.ds(edge_rows(odd_x, k, P_HALO), P_HALO)
        edges.append(
            pltpu.make_async_copy(p_ref.at[:, rows, :], x_hbm.at[:, pl.ds(A_HALO, P_HALO), :], out_sems.at[2 + k])
        )
        edges[-1].start()
    edges.append(pltpu.make_async_copy(p_ref, p_hbm, out_sems.at[4]))
    edges[-1].start()
    odd_y = index(GY) % 2
    lane = lane_of((32, 128))
    lane8 = lane_of((8, 128))
    for f in range(FLUOR):
        sides = []
        for a_from, p_from in ((0, 0), (COLS - A_HALO, COLS - P_HALO)):
            top = roll(a_ref[f, :32, :], -a_from)
            low = roll(a_ref[f, 32:, :], A_HALO - a_from)
            side = roll(p_ref[f, :32, :], 2 * A_HALO - p_from)
            main = jnp.where(lane < A_HALO, top, jnp.where(lane < 2 * A_HALO, low, side))
            rest = roll(p_ref[f, 32:40, :], -p_from)
            for k in range(1, 4):
                piece = roll(p_ref[f, 32 + 8 * k : 40 + 8 * k, :], 32 * k - p_from)
                rest = jnp.where(lane8 < 32 * k, rest, piece)
            sides.append((main, rest))
        (left, left_rest), (right, right_rest) = sides
        ya_ref[f, :32, :] = choose(odd_y, left, right)
        yb_ref[f, :32, :] = choose(odd_y, right, left)
        ya_ref[f, 32:, :] = choose(odd_y, left_rest, right_rest)
        yb_ref[f, 32:, :] = choose(odd_y, right_rest, left_rest)
    for k, (ref, y_hbm) in enumerate(((ya_ref, ya_hbm), (yb_ref, yb_hbm))):
        edges.append(pltpu.make_async_copy(ref, y_hbm, out_sems.at[5 + k]))
        edges[-1].start()
    for copy in edges:
        copy.wait()


REST = FLUOR * A_HALO


def pack_corner(odd_x, pairing, side_ref, ps_ref, out_ref):
    lane = lane_of((32, 128))
    lane4 = lane_of((4, 128))
    lane16 = lane_of((16, 128))
    spare = 2 * A_HALO
    a_rows = pl.ds(edge_rows(odd_x, pairing, A_HALO), A_HALO)
    p_rows = pl.ds(edge_rows(odd_x, pairing, P_HALO), P_HALO)
    for f in range(FLUOR):
        p_top = ps_ref[f, p_rows, :]
        a_side = side_ref[f, a_rows, :]
        at = A_HALO * f
        out_ref[at : at + 32, :] = jnp.where(lane < spare, a_side[:32], roll(p_top, spare))
        out_ref[at + 32 : at + 48, :] = jnp.where(lane16 < spare, a_side[32:], roll(p_top[:16], spare - P_HALO))
        rest = roll(p_top[16:20], -P_HALO)
        for k in range(1, 4):
            rest = jnp.where(lane4 < 32 * k, rest, roll(p_top[16 + 4 * k : 20 + 4 * k], 32 * k - P_HALO))
        out_ref[REST + 4 * f : REST + 4 * f + 4, :] = rest


def corner_body(ya_ref, yb_ref, side_ref, ps_ref, cb_ref, ca_ref):
    odd_x = index(GX) % 2
    odd_y = index(GY) % 2
    lane = lane_of((32, 128))
    lane8 = lane_of((8, 128))
    for f in range(FLUOR):
        first = ya_ref[f, :32, :]
        second = yb_ref[f, :32, :]
        left = choose(odd_y, first, second)
        right = choose(odd_y, second, first)
        side_ref[f, :32, :] = jnp.where(lane < A_HALO, left, jnp.where(lane < 2 * A_HALO, roll(right, A_HALO), 0.0))
        side_ref[f, 32:, :] = jnp.where(lane < A_HALO, roll(left, -A_HALO), jnp.where(lane < 2 * A_HALO, right, 0.0))
        ps_ref[f, :32, :] = jnp.where(
            lane < P_HALO, roll(left, -2 * A_HALO), jnp.where(lane < 2 * P_HALO, roll(right, P_HALO - 2 * A_HALO), 0.0)
        )
        first = ya_ref[f, 32:, :]
        second = yb_ref[f, 32:, :]
        left = choose(odd_y, first, second)
        right = choose(odd_y, second, first)
        for k in range(4):
            ps_ref[f, 32 + 8 * k : 40 + 8 * k, :] = jnp.where(
                lane8 < P_HALO, roll(left, -32 * k), jnp.where(lane8 < 2 * P_HALO, roll(right, P_HALO - 32 * k), 0.0)
            )
    pack_corner(odd_x, 0, side_ref, ps_ref, ca_ref)
    pack_corner(odd_x, 1, side_ref, ps_ref, cb_ref)


GROUP = 4


def along_y(x, w, put):
    for f in range(0, FLUOR, GROUP):
        part = x(slice(f, f + GROUP))
        out = dot_right(part.reshape(-1, part.shape[2]), w)
        out = out.reshape(GROUP, part.shape[1], out.shape[1])
        for k in range(GROUP):
            put(f + k, out[k])


X_GROUP = 4


def along_x(m, stack, out_ref):
    for f in range(0, FLUOR, X_GROUP):
        out = dot(m, jnp.concatenate([stack(f + k) for k in range(X_GROUP)], axis=1))
        for k in range(X_GROUP):
            out_ref[f + k] = out[:, 256 * k : 256 * k + 256]


def wide(main, side):
    return jnp.concatenate([main, side], axis=2)


def mix(gram_ref, v_ref, d_ref, g_ref):
    step = 8

    def mixed(part, f):
        acc = gram_ref[f, 0] * part[0]
        for k in range(1, FLUOR):
            acc = acc + gram_ref[f, k] * part[k]
        return acc

    for start in range(0, G_ROWS, step):
        part = [v_ref[f, start : start + step, :COLS] for f in range(FLUOR)]
        for f in range(FLUOR):
            g_ref[f, start : start + step, :COLS] = mixed(part, f) - d_ref[f, start : start + step, :COLS]
    lane = lane_of((step, 128))
    group = G_ROWS // 4
    for start in range(0, group, step):
        rows = [slice(k * group + start, k * group + start + step) for k in range(4)]
        part = []
        for f in range(FLUOR):
            packed = v_ref[f, rows[0], COLS:]
            for k in range(1, 4):
                packed = packed + roll(v_ref[f, rows[k], COLS:], 32 * k)
            part.append(packed)
        for f in range(FLUOR):
            out = mixed(part, f)
            for k in range(4):
                side = jnp.where(lane < 2 * G_HALO, roll(out, -32 * k), 0.0)
                g_ref[f, rows[k], COLS:] = side - d_ref[f, rows[k], COLS:]


def sums(gram_ref, g_ref, by, bx, y_ref, z_ref, sum_ref):
    along_x(bx[...], lambda f: stacked(g_ref[f], 384), y_ref)

    def put(f, z):
        z_ref[f] = z

    along_y(lambda part: y_ref[part], by[...], put)
    grad = jnp.zeros((8, 128), f32)
    image = jnp.zeros((8, 128), f32)
    for start in range(0, ROWS, 8):
        part = [z_ref[f, start : start + 8, :] for f in range(FLUOR)]
        for f in range(FLUOR):
            acc = gram_ref[f, 0] * part[0]
            for k in range(1, FLUOR):
                acc = acc + gram_ref[f, k] * part[k]
            image = image + acc * part[f]
            g = g_ref[f, G_HALO + start : G_HALO + start + 8, :COLS]
            grad = grad + g * g
    grad = jnp.sum(grad, axis=0, keepdims=True)
    image = jnp.sum(image, axis=0, keepdims=True)
    lane = lane_of((1, 128))
    row = jnp.where(lane < 64, grad + roll(grad, 64), image + roll(image, 64))
    sum_ref[...] = jnp.broadcast_to(row, sum_ref.shape)


def step_length(total_ref):
    total = jnp.sum(total_ref[...], axis=0, keepdims=True)
    lane = lane_of((1, 128))
    grad = jnp.sum(jnp.where(lane < 64, total, 0.0), axis=1, keepdims=True)
    image = jnp.sum(jnp.where(lane < 64, 0.0, total), axis=1, keepdims=True)
    return grad / (image + tiny_floor)


def put_stack(ref, f, start, depth, x):
    high, low = split(x)
    for at, part in ((0, high), (depth, low), (2 * depth, high)):
        ref[f, pl.ds(pl.multiple_of(start + at, 16), x.shape[0]), :] = part


def along_half(x, w_ref, start, put):
    w = jnp.concatenate([w_ref[256 * k + start : 256 * k + start + 128, :] for k in range(3)], axis=0)
    along_y(x, w, put)


def store(ref):
    def put(f, x):
        ref[f] = x

    return put


def own_body(a_ref, side_ref, p_ref, ps_ref, xb_ref, my, py, u_ref, w_ref, ub_ref, wb_ref):
    along_y(lambda part: wide(p_ref[part], ps_ref[part]), py[...], store(w_ref))
    along_y(lambda part: wide(a_ref[part], side_ref[part]), my[...], store(u_ref))
    along_half(lambda part: xb_ref[part, :A_HALO, :], my, 0, store(ub_ref))
    along_half(lambda part: xb_ref[part, A_HALO:, :], py, 0, store(wb_ref))


def first_rows_body(xa_ref, my, py, ua_ref, wa_ref):
    along_half(lambda part: xa_ref[part, :A_HALO, :], my, 0, store(ua_ref))
    along_half(lambda part: xa_ref[part, A_HALO:, :], py, 0, store(wa_ref))


def first_body(
    gram_ref, u_ref, w_ref, ua_ref, ub_ref, wa_ref, wb_ref, cb_ref, ca_ref, my, py, mx, px,
    d_ref, g_ref, ya_ref, yb_ref, v_ref, su_ref, sw_ref, side_ref,
):
    odd_x = index(GX) % 2
    odd_y = index(GY) % 2
    lane = lane_of((32, 128))
    lane16 = lane_of((16, 128))
    lane8 = lane_of((8, 128))
    spare = 2 * A_HALO
    su_ref[:, 3 * A_ROWS :, :] = jnp.zeros((FLUOR, 512 - 3 * A_ROWS, 256), bf16)
    for u_part, w_part, corner, above in (
        (ua_ref, wa_ref, ca_ref, odd_x == 1),
        (ub_ref, wb_ref, cb_ref, odd_x == 0),
    ):
        for f in range(FLUOR):
            at = A_HALO * f
            left = roll(corner[at : at + 32, :], -spare)
            right = roll(corner[at + 32 : at + 48, :], P_HALO - spare)
            rest = corner[REST + 4 * f : REST + 4 * f + 4, :]
            last = jnp.concatenate([roll(rest, P_HALO - 32 * k) for k in range(4)], axis=0)
            side_ref[f, :16, :] = jnp.where(lane16 < P_HALO, left[:16], jnp.where(lane16 < 2 * P_HALO, right, 0.0))
            side_ref[f, 16:24, :] = jnp.where(
                lane8 < P_HALO, left[16:24], jnp.where(lane8 < 2 * P_HALO, last[:8], 0.0)
            )
            side_ref[f, 24:, :] = jnp.where(lane8 < P_HALO, left[24:], jnp.where(lane8 < 2 * P_HALO, last[8:], 0.0))
        a_at = jnp.where(above, 0, A_HALO + ROWS)
        p_at = jnp.where(above, 0, P_HALO + ROWS)
        along_half(
            lambda part: side_ref[part],
            py,
            128,
            lambda f, x: put_stack(sw_ref, f, p_at, P_ROWS, x + w_part[f]),
        )
        along_half(
            lambda part: corner[A_HALO * part.start : A_HALO * part.stop, :].reshape(-1, A_HALO, 128),
            my,
            128,
            lambda f, x: put_stack(su_ref, f, a_at, A_ROWS, x + u_part[f]),
        )
    for f in range(FLUOR):
        put_stack(sw_ref, f, P_HALO, P_ROWS, w_ref[f])
        put_stack(su_ref, f, A_HALO, A_ROWS, u_ref[f])
    along_x(px[...], lambda f: sw_ref[f], d_ref)
    along_x(mx[...], lambda f: su_ref[f], v_ref)
    mix(gram_ref, v_ref, d_ref, g_ref)
    lane = lane_of((24, 128))
    for f in range(FLUOR):
        edges = []
        for start in (G_HALO, COLS - G_HALO - 32):
            out = roll(g_ref[f, :24, :COLS], -start)
            for k in range(1, 4):
                piece = roll(g_ref[f, 24 * k : 24 * k + 24, :COLS], 32 * k - start)
                out = jnp.where(lane < 32 * k, out, piece)
            edges.append(out)
        ya_ref[f] = choose(odd_y, edges[0], edges[1])
        yb_ref[f] = choose(odd_y, edges[1], edges[0])


def probe_body(gram_ref, g_ref, by, bx, sum_ref, y_ref, z_ref):
    sums(gram_ref, g_ref, by, bx, y_ref, z_ref, sum_ref)


def relay(near_ref, out_ref):
    out_ref[...] = jnp.broadcast_to(jnp.sum(near_ref[...], axis=0, keepdims=True), out_ref.shape)


def outer_body(near_ref, g_ref, ya_ref, yb_ref, far_ref, side_ref, send_ref):
    relay(near_ref, far_ref)
    odd_y = index(GY) % 2
    lane = lane_of((24, 128))
    for f in range(FLUOR):
        left = choose(odd_y, ya_ref[f], yb_ref[f])
        right = choose(odd_y, yb_ref[f], ya_ref[f])
        for k in range(4):
            own = roll(g_ref[f, 24 * k : 24 * k + 24, COLS:], 32)
            side_ref[f, 24 * k : 24 * k + 24, :] = jnp.where(
                lane < 32,
                roll(left, -32 * k),
                jnp.where(lane < 64, own, jnp.where(lane < 96, roll(right, 64 - 32 * k), 0.0)),
            )
        send_ref[f, :32, :] = g_ref[f, 2 * G_HALO : 2 * G_HALO + 32, :COLS]
        send_ref[f, 32:, :] = side_ref[f, 2 * G_HALO : 2 * G_HALO + 32, :]


def second_body(
    gram_ref, total_ref, a_ref, side_ref, za_ref, zb_ref, ca_ref, cb_ref, d_ref, g_ref, gs_ref, xa_ref, xb_ref,
    my, mx, by, bx,
    a_out, g_out, sum_ref, v_ref, n_ref, y_ref, z_ref, x_ref, u_ref,
):
    odd_x = index(GX) % 2
    t = step_length(total_ref)
    for f in range(FLUOR):
        tile = jnp.maximum(a_ref[f] - t * g_ref[f, G_HALO : G_HALO + ROWS, :COLS], 0.0)
        a_out[f] = tile
        x_ref[f, A_HALO : A_HALO + ROWS, :COLS] = tile
        x_ref[f, A_HALO : A_HALO + ROWS, COLS:] = jnp.maximum(
            side_ref[f] - t * gs_ref[f, G_HALO : G_HALO + ROWS, :], 0.0
        )
        for above, main, corner, far, near in (
            (True, choose(odd_x, za_ref[f, :A_HALO, :], zb_ref[f, :A_HALO, :]),
             choose(odd_x, ca_ref[A_HALO * f : A_HALO * f + A_HALO, :], cb_ref[A_HALO * f : A_HALO * f + A_HALO, :]), choose(odd_x, xa_ref[f], xb_ref[f]),
             slice(0, G_HALO)),
            (False, choose(odd_x, zb_ref[f, :A_HALO, :], za_ref[f, :A_HALO, :]),
             choose(odd_x, cb_ref[A_HALO * f : A_HALO * f + A_HALO, :], ca_ref[A_HALO * f : A_HALO * f + A_HALO, :]), choose(odd_x, xb_ref[f], xa_ref[f]),
             slice(G_ROWS - G_HALO, G_ROWS)),
        ):
            parts = [far[:32], g_ref[f, near, :COLS]], [far[32:], gs_ref[f, near, :]]
            if not above:
                parts = [part[::-1] for part in parts]
            rows = slice(0, A_HALO) if above else slice(A_HALO + ROWS, A_ROWS)
            x_ref[f, rows, :COLS] = jnp.maximum(main - t * jnp.concatenate(parts[0], axis=0), 0.0)
            x_ref[f, rows, COLS:] = jnp.maximum(corner - t * jnp.concatenate(parts[1], axis=0), 0.0)

    def put(f, u):
        u_ref[f] = u

    along_y(lambda part: x_ref[part], my[...], put)
    along_x(mx[...], lambda f: stacked(u_ref[f], 512), v_ref)
    mix(gram_ref, v_ref, d_ref, n_ref)
    sums(gram_ref, n_ref, by, bx, y_ref, z_ref, sum_ref)
    for f in range(FLUOR):
        g_out[f] = n_ref[f, G_HALO : G_HALO + ROWS, :COLS]


def last_body(total_ref, a_ref, g_ref, out_hbm, out_ref, sems):
    t = step_length(total_ref)
    copies = []
    for k in range(4):
        fields = slice(3 * k, 3 * k + 3)
        out_ref[fields] = jnp.maximum(a_ref[fields] - t * g_ref[fields], 0.0)
        part = pl.ds(3 * k, 3)
        copies.append(pltpu.make_async_copy(out_ref.at[part], out_hbm.at[part], sems.at[k]))
        copies[-1].start()
    for copy in copies:
        copy.wait()


TILE = (FLUOR, ROWS, COLS)
G_SHAPE = (FLUOR, G_ROWS, 256)
PROBE_SCRATCH = (pltpu.VMEM((FLUOR, ROWS, 256), f32), pltpu.VMEM(TILE, f32))
OWN_COST = 10**10
NEAR_COUNT = 32
FAR_COUNT = 16

first_call = kernel(
    first_body,
    "s" + "v" * 12,
    [(G_SHAPE, f32)] * 2 + [((FLUOR, 24, 128), f32)] * 2,
    10**9,
    [
        pltpu.VMEM(G_SHAPE, f32),
        pltpu.VMEM((FLUOR, 512, 256), bf16),
        pltpu.VMEM((FLUOR, 3 * P_ROWS, 256), bf16),
        pltpu.VMEM((FLUOR, P_HALO, 128), f32),
    ],
)
probe_call = kernel(probe_body, "svvv", [((NEAR_COUNT, 128), f32)], 10**9, PROBE_SCRATCH)
second_call = kernel(
    second_body,
    "s" + "v" * 16,
    [(TILE, f32)] * 2 + [((NEAR_COUNT, 128), f32)],
    10**9,
    [
        pltpu.VMEM(G_SHAPE, f32),
        pltpu.VMEM(G_SHAPE, f32),
        *PROBE_SCRATCH,
        pltpu.VMEM((FLUOR, A_ROWS, 256), f32),
        pltpu.VMEM((FLUOR, A_ROWS, 256), f32),
    ],
)


def length(axes):
    count = 1
    for axis in axes:
        count *= lax.axis_size(axis)
    return count


def trade(first, second, axes):
    return trade_first(first, axes), trade_second(second, axes)


def trade_first(edge, axes):
    return lax.ppermute(edge, axes, [(i, i ^ 1) for i in range(length(axes))])


def trade_second(edge, axes):
    count = length(axes)
    return lax.ppermute(edge, axes, [(i, (i + (1 if i % 2 else -1)) % count) for i in range(count)])


def spread(rows, axes):
    got = lax.all_to_all(rows.reshape(rows.shape[0], 1, 128), axes, 0, 0, tiled=True)
    return got.reshape(rows.shape[0], 128)


def local(sizes, abundance_start, measured, spectra, taps_x, taps_y):
    assert (length(NEAR), length((FAR,))) == (NEAR_COUNT, FAR_COUNT)

    edge = (FLUOR, A_HALO + P_HALO, 128)
    a0 = abundance_start[0]
    p, xb, xa, ya, yb = kernel(
        project_body,
        "hhh",
        [(TILE, f32)] + [(edge, f32)] * 2 + [((FLUOR, 40, 128), f32)] * 2,
        10**7,
        [
            pltpu.SMEM((FLUOR, CHAN), f32),
            pltpu.VMEM(TILE, f32),
            pltpu.VMEM((CHAN, ROWS, COLS), bf16),
            pltpu.VMEM(TILE, f32),
            pltpu.VMEM((FLUOR, 40, 128), f32),
            pltpu.VMEM((FLUOR, 40, 128), f32),
            pltpu.SemaphoreType.DMA((6,)),
            pltpu.SemaphoreType.DMA((7,)),
        ],
        60_000_000,
        pltpu.HBM,
    )(spectra.T, a0, measured[0])
    za, zb = trade(xa, xb, GX)
    ya, yb = trade(ya, yb, GY)
    my, py, by = kernel(
        functools.partial(y_matrices_body, sizes[1]),
        "s",
        [((768, 256), bf16)] * 2 + [((768, 128), bf16)],
        10**9,
    )(taps_y)
    corner = (REST + 4 * FLUOR, 128)
    side, ps, cb, ca = kernel(corner_body, "vv", [(TILE, f32)] * 2 + [(corner, f32)] * 2, 10**7)(ya, yb)
    ca, cb = trade(ca, cb, GX)
    gram, mx, px, bx = kernel(
        functools.partial(x_matrices_body, sizes[0]),
        "svv",
        [((FLUOR, FLUOR), f32), ((G_ROWS, 512), bf16), ((G_ROWS, 384), bf16), ((ROWS, 384), bf16)],
        10**9,
    )(taps_x, spectra.T, ps)
    u, w, ub, wb = kernel(
        own_body,
        "v" * 7,
        [((FLUOR, rows, 256), f32) for rows in (ROWS, ROWS, A_HALO, P_HALO)],
        OWN_COST,
    )(a0, side, p, ps, zb, my, py)
    ua, wa = kernel(first_rows_body, "vvv", [((FLUOR, rows, 256), f32) for rows in (A_HALO, P_HALO)], 10**7)(za, my, py)
    d, g, ya, yb = first_call(gram, u, w, ua, ub, wa, wb, cb, ca, my, py, mx, px)
    ya, yb = trade(ya, yb, GY)
    (partial,) = probe_call(gram, g, by, bx)
    near = spread(partial, NEAR)
    far, g_side, send = kernel(
        outer_body,
        "vvvv",
        [((FAR_COUNT, 128), f32), ((FLUOR, G_ROWS, 128), f32), ((FLUOR, 64, 128), f32)],
        10**8,
    )(near, g, ya, yb)
    xa, xb = trade(send, send, GX)
    total = spread(far, FAR)
    a1, g1, partial = second_call(
        gram, total, a0, side, za, zb, ca, cb, d, g, g_side, xa, xb, my, mx, by, bx
    )
    (far,) = kernel(relay, "v", [((FAR_COUNT, 128), f32)], 10**6)(spread(partial, NEAR))
    total = spread(far, FAR)
    (out,) = kernel(
        last_body,
        "vvv",
        [(TILE, f32)],
        10**7,
        [pltpu.VMEM(TILE, f32), pltpu.SemaphoreType.DMA((4,))],
        space=pltpu.HBM,
    )(total, a1, g1)
    return out[None]


def solution(mesh):
    count_x, count_y = mesh.shape["gx"], mesh.shape["gy"]
    parts = Mesh(
        mesh.devices.reshape(count_x // 4, 2, 2, 2, count_y // 2), ("y", "x_hi", "core", "x_lo", "z")
    )
    sizes = (count_x * ROWS, count_y * COLS)
    tiles = P(None, None, GX, GY)
    return jax.shard_map(
        functools.partial(local, sizes),
        mesh=parts,
        in_specs=(tiles, tiles, P(), P(), P()),
        out_specs=tiles,
        check_vma=False,
    )
```

```python
import functools

import jax
import jax.numpy as jnp
from jax import lax
from jax.experimental import pallas as pl
from jax.experimental.pallas import tpu as pltpu
from jax.sharding import Mesh
from jax.sharding import PartitionSpec as P

TAPS = 33
ITERS = 2
FLUOR = 12
CHAN = 32
ROWS = 64
COLS = 128

HALF = TAPS // 2
A_HALO = 3 * HALF
P_HALO = 2 * HALF
G_HALO = HALF
A_ROWS = ROWS + 2 * A_HALO
P_ROWS = ROWS + 2 * P_HALO
G_ROWS = ROWS + 2 * G_HALO

GX = ("y", "x_hi", "core")
GY = ("x_lo", "z")
NEAR = ("y", "x_hi", "core", "x_lo")
FAR = "z"

tiny_floor = 1e-06
f32 = jnp.float32
bf16 = jnp.bfloat16


SPACES = {"s": pltpu.SMEM, "v": pltpu.VMEM, "h": pltpu.HBM}


def kernel(body, ins, outs, cost, scratch=(), limit=32 * 2**20, space=pltpu.VMEM):
    return pl.pallas_call(
        body,
        in_specs=[pl.BlockSpec(memory_space=SPACES[kind]) for kind in ins],
        out_specs=[pl.BlockSpec(memory_space=space) for _ in outs],
        out_shape=[jax.ShapeDtypeStruct(shape, dtype) for shape, dtype in outs],
        scratch_shapes=list(scratch),
        compiler_params=pltpu.CompilerParams(vmem_limit_bytes=limit),
        cost_estimate=pl.CostEstimate(flops=cost, bytes_accessed=cost // 100, transcendentals=0),
    )


def index(axes):
    place = 0
    for axis in axes:
        place = place * lax.axis_size(axis) + lax.axis_index(axis)
    return place


def roll(x, by):
    by = by % 128
    return x if by == 0 else pltpu.roll(x, by, axis=x.ndim - 1)


def lane_of(shape):
    return lax.broadcasted_iota(jnp.int32, shape, len(shape) - 1)


def split(x):
    high = x.astype(bf16)
    return high, (x - high.astype(f32)).astype(bf16)


def dot(a, b):
    return jnp.dot(a, b, preferred_element_type=f32)


def dot_right(x, w):
    high, low = split(x)
    return dot(jnp.concatenate([high, low, high], axis=1), w)


def stacked(x, depth):
    high, low = split(x)
    parts = [high, low, high]
    spare = depth - 3 * x.shape[0]
    if spare:
        parts.append(jnp.zeros((spare, x.shape[1]), bf16))
    return jnp.concatenate(parts, axis=0)


def side_position(index, halo):
    left = index - COLS - halo
    right = index - halo
    position = jnp.where(index < COLS, index, jnp.where(index < COLS + halo, left, right))
    return jnp.where(index < COLS + 2 * halo, position, 1 << 20)


def tap_matrix(taps_ref, offset):
    out = jnp.zeros(offset.shape, f32)
    for t in range(TAPS):
        out = jnp.where(offset == t, taps_ref[t], out)
    return out


def inside(position, base, size):
    where = position + base
    return jnp.logical_and(where >= 0, where < size)


def exact_dot(a, b):
    return lax.dot_general(a, b, (((1,), (0,)), ((), ())), precision=lax.Precision.HIGHEST, preferred_element_type=f32)


def rows_cols(shape):
    return lax.broadcasted_iota(jnp.int32, shape, 0), lax.broadcasted_iota(jnp.int32, shape, 1)


def put_right(x, ref):
    high, low = split(x)
    rows = x.shape[0]
    ref[:rows, :] = high
    ref[rows : 2 * rows, :] = high
    ref[2 * rows :, :] = low


def put_left(x, part, ref):
    high, low = split(x)
    ref[...] = jnp.where(part < 2, high.astype(f32), low.astype(f32)).astype(bf16)


def y_matrices_body(size_y, ty_ref, my, py, by):
    base_y = index(GY) * COLS
    r, c = rows_cols((256, 256))
    source = side_position(r, P_HALO)
    target = side_position(c, G_HALO)
    okay = jnp.logical_and(inside(source, base_y, size_y), inside(target, base_y, size_y))
    put_right(jnp.where(okay, tap_matrix(ty_ref, target - source + HALF), 0.0), py)
    source = side_position(r, A_HALO)
    middle = c - P_HALO
    okay = jnp.logical_and(inside(source, base_y, size_y), inside(middle, base_y, size_y))
    first = jnp.where(okay, tap_matrix(ty_ref, source - middle + HALF), 0.0)
    middle = r - P_HALO
    second = jnp.where(inside(target, base_y, size_y), tap_matrix(ty_ref, target - middle + HALF), 0.0)
    put_right(exact_dot(first, second), my)
    r, c = rows_cols((256, 128))
    source = side_position(r, G_HALO)
    okay = inside(source, base_y, size_y)
    put_right(jnp.where(okay, tap_matrix(ty_ref, source - c + HALF), 0.0), by)


def x_matrices_body(size_x, tx_ref, spectra_ref, after_ref, gram_ref, mx, px, bx):
    spectra = spectra_ref[...]
    gram_ref[...] = lax.dot_general(
        spectra, spectra, (((1,), (1,)), ((), ())), precision=lax.Precision.HIGHEST, preferred_element_type=f32
    )
    base_x = index(GX) * ROWS
    r, c = rows_cols((128, 512))
    part = c // A_ROWS
    source = c - part * A_ROWS - A_HALO
    middle = r - P_HALO
    okay = jnp.logical_and(inside(source, base_x, size_x), inside(middle, base_x, size_x))
    okay = jnp.logical_and(okay, part < 3)
    first = jnp.where(okay, tap_matrix(tx_ref, source - middle + HALF), 0.0)
    r, c = rows_cols((G_ROWS, 128))
    target = r - G_HALO
    middle = c - P_HALO
    second = jnp.where(inside(target, base_x, size_x), tap_matrix(tx_ref, target - middle + HALF), 0.0)
    r, c = rows_cols((G_ROWS, 512))
    put_left(exact_dot(second, first), c // A_ROWS, mx)
    r, c = rows_cols((G_ROWS, 384))
    part = c // P_ROWS
    source = c - part * P_ROWS - P_HALO
    target = r - G_HALO
    okay = jnp.logical_and(inside(source, base_x, size_x), inside(target, base_x, size_x))
    put_left(jnp.where(okay, tap_matrix(tx_ref, target - source + HALF), 0.0), part, px)
    r, c = rows_cols((ROWS, 384))
    part = c // G_ROWS
    source = c - part * G_ROWS - G_HALO
    okay = jnp.logical_and(inside(source, base_x, size_x), part < 3)
    put_left(jnp.where(okay, tap_matrix(tx_ref, source - r + HALF), 0.0), part, bx)


def choose(odd, if_odd, if_even):
    return jnp.where(odd == 1, if_odd, if_even)


def edge_rows(odd_x, pairing, depth):
    top = odd_x == 1 if pairing == 0 else odd_x == 0
    return pl.multiple_of(jnp.where(top, 0, ROWS - depth), 16)


def project_body(
    s_hbm, a_hbm, m_hbm, p_hbm, xb_hbm, xa_hbm, ya_hbm, yb_hbm,
    spectra_ref, a_ref, m_ref, p_ref, ya_ref, yb_ref, sems, out_sems,
):
    step = 32
    copy_s = pltpu.make_async_copy(s_hbm, spectra_ref, sems.at[5])
    copy_s.start()
    copies = [
        pltpu.make_async_copy(m_hbm.at[:, pl.ds(k * step, step), :], m_ref.at[:, pl.ds(k * step, step), :], sems.at[k])
        for k in range(ROWS // step)
    ]
    for copy in copies:
        copy.start()
    copy_a = pltpu.make_async_copy(a_hbm, a_ref, sems.at[ROWS // step])
    copy_a.start()
    odd_x = index(GX) % 2
    edges = []
    copy_s.wait()
    for k, copy in enumerate(copies):
        copy.wait()
        start = k * step
        acc = [jnp.zeros((step, COLS), f32) for _ in range(FLUOR)]
        for c in range(CHAN):
            seen = m_ref[c, start : start + step, :].astype(f32)
            for f in range(FLUOR):
                acc[f] = acc[f] + spectra_ref[f, c] * seen
        for f in range(FLUOR):
            p_ref[f, start : start + step, :] = acc[f]
        if k == 0:
            copy_a.wait()
            for pairing, x_hbm in ((1, xb_hbm), (0, xa_hbm)):
                rows = pl.ds(edge_rows(odd_x, pairing, A_HALO), A_HALO)
                edges.append(
                    pltpu.make_async_copy(a_ref.at[:, rows, :], x_hbm.at[:, pl.ds(0, A_HALO), :], out_sems.at[pairing])
                )
                edges[-1].start()
    for k, x_hbm in ((1, xb_hbm), (0, xa_hbm)):
        rows = pl.ds(edge_rows(odd_x, k, P_HALO), P_HALO)
        edges.append(
            pltpu.make_async_copy(p_ref.at[:, rows, :], x_hbm.at[:, pl.ds(A_HALO, P_HALO), :], out_sems.at[2 + k])
        )
        edges[-1].start()
    edges.append(pltpu.make_async_copy(p_ref, p_hbm, out_sems.at[4]))
    edges[-1].start()
    odd_y = index(GY) % 2
    lane = lane_of((32, 128))
    lane8 = lane_of((8, 128))
    for f in range(FLUOR):
        sides = []
        for a_from, p_from in ((0, 0), (COLS - A_HALO, COLS - P_HALO)):
            top = roll(a_ref[f, :32, :], -a_from)
            low = roll(a_ref[f, 32:, :], A_HALO - a_from)
            side = roll(p_ref[f, :32, :], 2 * A_HALO - p_from)
            main = jnp.where(lane < A_HALO, top, jnp.where(lane < 2 * A_HALO, low, side))
            rest = roll(p_ref[f, 32:40, :], -p_from)
            for k in range(1, 4):
                piece = roll(p_ref[f, 32 + 8 * k : 40 + 8 * k, :], 32 * k - p_from)
                rest = jnp.where(lane8 < 32 * k, rest, piece)
            sides.append((main, rest))
        (left, left_rest), (right, right_rest) = sides
        ya_ref[f, :32, :] = choose(odd_y, left, right)
        yb_ref[f, :32, :] = choose(odd_y, right, left)
        ya_ref[f, 32:, :] = choose(odd_y, left_rest, right_rest)
        yb_ref[f, 32:, :] = choose(odd_y, right_rest, left_rest)
    for k, (ref, y_hbm) in enumerate(((ya_ref, ya_hbm), (yb_ref, yb_hbm))):
        edges.append(pltpu.make_async_copy(ref, y_hbm, out_sems.at[5 + k]))
        edges[-1].start()
    for copy in edges:
        copy.wait()


REST = FLUOR * A_HALO


def pack_corner(odd_x, pairing, side_ref, ps_ref, out_ref):
    lane = lane_of((32, 128))
    lane4 = lane_of((4, 128))
    lane16 = lane_of((16, 128))
    spare = 2 * A_HALO
    a_rows = pl.ds(edge_rows(odd_x, pairing, A_HALO), A_HALO)
    p_rows = pl.ds(edge_rows(odd_x, pairing, P_HALO), P_HALO)
    for f in range(FLUOR):
        p_top = ps_ref[f, p_rows, :]
        a_side = side_ref[f, a_rows, :]
        at = A_HALO * f
        out_ref[at : at + 32, :] = jnp.where(lane < spare, a_side[:32], roll(p_top, spare))
        out_ref[at + 32 : at + 48, :] = jnp.where(lane16 < spare, a_side[32:], roll(p_top[:16], spare - P_HALO))
        rest = roll(p_top[16:20], -P_HALO)
        for k in range(1, 4):
            rest = jnp.where(lane4 < 32 * k, rest, roll(p_top[16 + 4 * k : 20 + 4 * k], 32 * k - P_HALO))
        out_ref[REST + 4 * f : REST + 4 * f + 4, :] = rest


def corner_body(ya_ref, yb_ref, side_ref, ps_ref, cb_ref, ca_ref):
    odd_x = index(GX) % 2
    odd_y = index(GY) % 2
    lane = lane_of((32, 128))
    lane8 = lane_of((8, 128))
    for f in range(FLUOR):
        first = ya_ref[f, :32, :]
        second = yb_ref[f, :32, :]
        left = choose(odd_y, first, second)
        right = choose(odd_y, second, first)
        side_ref[f, :32, :] = jnp.where(lane < A_HALO, left, jnp.where(lane < 2 * A_HALO, roll(right, A_HALO), 0.0))
        side_ref[f, 32:, :] = jnp.where(lane < A_HALO, roll(left, -A_HALO), jnp.where(lane < 2 * A_HALO, right, 0.0))
        ps_ref[f, :32, :] = jnp.where(
            lane < P_HALO, roll(left, -2 * A_HALO), jnp.where(lane < 2 * P_HALO, roll(right, P_HALO - 2 * A_HALO), 0.0)
        )
        first = ya_ref[f, 32:, :]
        second = yb_ref[f, 32:, :]
        left = choose(odd_y, first, second)
        right = choose(odd_y, second, first)
        for k in range(4):
            ps_ref[f, 32 + 8 * k : 40 + 8 * k, :] = jnp.where(
                lane8 < P_HALO, roll(left, -32 * k), jnp.where(lane8 < 2 * P_HALO, roll(right, P_HALO - 32 * k), 0.0)
            )
    pack_corner(odd_x, 0, side_ref, ps_ref, ca_ref)
    pack_corner(odd_x, 1, side_ref, ps_ref, cb_ref)


GROUP = 4


def along_y(x, w, put):
    for f in range(0, FLUOR, GROUP):
        part = x(slice(f, f + GROUP))
        out = dot_right(part.reshape(-1, part.shape[2]), w)
        out = out.reshape(GROUP, part.shape[1], out.shape[1])
        for k in range(GROUP):
            put(f + k, out[k])


X_GROUP = 4


def along_x(m, stack, out_ref):
    for f in range(0, FLUOR, X_GROUP):
        out = dot(m, jnp.concatenate([stack(f + k) for k in range(X_GROUP)], axis=1))
        for k in range(X_GROUP):
            out_ref[f + k] = out[:, 256 * k : 256 * k + 256]


def wide(main, side):
    return jnp.concatenate([main, side], axis=2)


def mix(gram_ref, v_ref, d_ref, g_ref):
    step = 8

    def mixed(part, f):
        acc = gram_ref[f, 0] * part[0]
        for k in range(1, FLUOR):
            acc = acc + gram_ref[f, k] * part[k]
        return acc

    for start in range(0, G_ROWS, step):
        part = [v_ref[f, start : start + step, :COLS] for f in range(FLUOR)]
        for f in range(FLUOR):
            g_ref[f, start : start + step, :COLS] = mixed(part, f) - d_ref[f, start : start + step, :COLS]
    lane = lane_of((step, 128))
    group = G_ROWS // 4
    for start in range(0, group, step):
        rows = [slice(k * group + start, k * group + start + step) for k in range(4)]
        part = []
        for f in range(FLUOR):
            packed = v_ref[f, rows[0], COLS:]
            for k in range(1, 4):
                packed = packed + roll(v_ref[f, rows[k], COLS:], 32 * k)
            part.append(packed)
        for f in range(FLUOR):
            out = mixed(part, f)
            for k in range(4):
                side = jnp.where(lane < 2 * G_HALO, roll(out, -32 * k), 0.0)
                g_ref[f, rows[k], COLS:] = side - d_ref[f, rows[k], COLS:]


def sums(gram_ref, g_ref, by, bx, y_ref, z_ref, sum_ref):
    along_x(bx[...], lambda f: stacked(g_ref[f], 384), y_ref)

    def put(f, z):
        z_ref[f] = z

    along_y(lambda part: y_ref[part], by[...], put)
    grad = jnp.zeros((8, 128), f32)
    image = jnp.zeros((8, 128), f32)
    for start in range(0, ROWS, 8):
        part = [z_ref[f, start : start + 8, :] for f in range(FLUOR)]
        for f in range(FLUOR):
            acc = gram_ref[f, 0] * part[0]
            for k in range(1, FLUOR):
                acc = acc + gram_ref[f, k] * part[k]
            image = image + acc * part[f]
            g = g_ref[f, G_HALO + start : G_HALO + start + 8, :COLS]
            grad = grad + g * g
    grad = jnp.sum(grad, axis=0, keepdims=True)
    image = jnp.sum(image, axis=0, keepdims=True)
    lane = lane_of((1, 128))
    row = jnp.where(lane < 64, grad + roll(grad, 64), image + roll(image, 64))
    sum_ref[...] = jnp.broadcast_to(row, sum_ref.shape)


def step_length(total_ref):
    total = jnp.sum(total_ref[...], axis=0, keepdims=True)
    lane = lane_of((1, 128))
    grad = jnp.sum(jnp.where(lane < 64, total, 0.0), axis=1, keepdims=True)
    image = jnp.sum(jnp.where(lane < 64, 0.0, total), axis=1, keepdims=True)
    return grad / (image + tiny_floor)


def put_stack(ref, f, start, depth, x):
    high, low = split(x)
    for at, part in ((0, high), (depth, low), (2 * depth, high)):
        ref[f, pl.ds(pl.multiple_of(start + at, 16), x.shape[0]), :] = part


def along_half(x, w_ref, start, put):
    w = jnp.concatenate([w_ref[256 * k + start : 256 * k + start + 128, :] for k in range(3)], axis=0)
    along_y(x, w, put)


def store(ref):
    def put(f, x):
        ref[f] = x

    return put


def own_body(a_ref, side_ref, p_ref, ps_ref, xb_ref, my, py, u_ref, w_ref, ub_ref, wb_ref):
    along_y(lambda part: wide(p_ref[part], ps_ref[part]), py[...], store(w_ref))
    along_y(lambda part: wide(a_ref[part], side_ref[part]), my[...], store(u_ref))
    along_half(lambda part: xb_ref[part, :A_HALO, :], my, 0, store(ub_ref))
    along_half(lambda part: xb_ref[part, A_HALO:, :], py, 0, store(wb_ref))


def first_rows_body(xa_ref, my, py, ua_ref, wa_ref):
    along_half(lambda part: xa_ref[part, :A_HALO, :], my, 0, store(ua_ref))
    along_half(lambda part: xa_ref[part, A_HALO:, :], py, 0, store(wa_ref))


def first_body(
    gram_ref, u_ref, w_ref, ua_ref, ub_ref, wa_ref, wb_ref, cb_ref, ca_ref, my, py, mx, px,
    d_ref, g_ref, ya_ref, yb_ref, v_ref, su_ref, sw_ref, side_ref,
):
    odd_x = index(GX) % 2
    odd_y = index(GY) % 2
    lane = lane_of((32, 128))
    lane16 = lane_of((16, 128))
    lane8 = lane_of((8, 128))
    spare = 2 * A_HALO
    su_ref[:, 3 * A_ROWS :, :] = jnp.zeros((FLUOR, 512 - 3 * A_ROWS, 256), bf16)
    for u_part, w_part, corner, above in (
        (ua_ref, wa_ref, ca_ref, odd_x == 1),
        (ub_ref, wb_ref, cb_ref, odd_x == 0),
    ):
        for f in range(FLUOR):
            at = A_HALO * f
            left = roll(corner[at : at + 32, :], -spare)
            right = roll(corner[at + 32 : at + 48, :], P_HALO - spare)
            rest = corner[REST + 4 * f : REST + 4 * f + 4, :]
            last = jnp.concatenate([roll(rest, P_HALO - 32 * k) for k in range(4)], axis=0)
            side_ref[f, :16, :] = jnp.where(lane16 < P_HALO, left[:16], jnp.where(lane16 < 2 * P_HALO, right, 0.0))
            side_ref[f, 16:24, :] = jnp.where(
                lane8 < P_HALO, left[16:24], jnp.where(lane8 < 2 * P_HALO, last[:8], 0.0)
            )
            side_ref[f, 24:, :] = jnp.where(lane8 < P_HALO, left[24:], jnp.where(lane8 < 2 * P_HALO, last[8:], 0.0))
        a_at = jnp.where(above, 0, A_HALO + ROWS)
        p_at = jnp.where(above, 0, P_HALO + ROWS)
        along_half(
            lambda part: side_ref[part],
            py,
            128,
            lambda f, x: put_stack(sw_ref, f, p_at, P_ROWS, x + w_part[f]),
        )
        along_half(
            lambda part: corner[A_HALO * part.start : A_HALO * part.stop, :].reshape(-1, A_HALO, 128),
            my,
            128,
            lambda f, x: put_stack(su_ref, f, a_at, A_ROWS, x + u_part[f]),
        )
    for f in range(FLUOR):
        put_stack(sw_ref, f, P_HALO, P_ROWS, w_ref[f])
        put_stack(su_ref, f, A_HALO, A_ROWS, u_ref[f])
    along_x(px[...], lambda f: sw_ref[f], d_ref)
    along_x(mx[...], lambda f: su_ref[f], v_ref)
    mix(gram_ref, v_ref, d_ref, g_ref)
    lane = lane_of((24, 128))
    for f in range(FLUOR):
        edges = []
        for start in (G_HALO, COLS - G_HALO - 32):
            out = roll(g_ref[f, :24, :COLS], -start)
            for k in range(1, 4):
                piece = roll(g_ref[f, 24 * k : 24 * k + 24, :COLS], 32 * k - start)
                out = jnp.where(lane < 32 * k, out, piece)
            edges.append(out)
        ya_ref[f] = choose(odd_y, edges[0], edges[1])
        yb_ref[f] = choose(odd_y, edges[1], edges[0])


def probe_body(gram_ref, g_ref, by, bx, sum_ref, y_ref, z_ref):
    sums(gram_ref, g_ref, by, bx, y_ref, z_ref, sum_ref)


def relay(near_ref, out_ref):
    out_ref[...] = jnp.broadcast_to(jnp.sum(near_ref[...], axis=0, keepdims=True), out_ref.shape)


def outer_body(near_ref, g_ref, ya_ref, yb_ref, far_ref, side_ref, send_ref):
    relay(near_ref, far_ref)
    odd_y = index(GY) % 2
    lane = lane_of((24, 128))
    for f in range(FLUOR):
        left = choose(odd_y, ya_ref[f], yb_ref[f])
        right = choose(odd_y, yb_ref[f], ya_ref[f])
        for k in range(4):
            own = roll(g_ref[f, 24 * k : 24 * k + 24, COLS:], 32)
            side_ref[f, 24 * k : 24 * k + 24, :] = jnp.where(
                lane < 32,
                roll(left, -32 * k),
                jnp.where(lane < 64, own, jnp.where(lane < 96, roll(right, 64 - 32 * k), 0.0)),
            )
        send_ref[f, :32, :] = g_ref[f, 2 * G_HALO : 2 * G_HALO + 32, :COLS]
        send_ref[f, 32:, :] = side_ref[f, 2 * G_HALO : 2 * G_HALO + 32, :]


def second_body(
    gram_ref, total_ref, a_ref, side_ref, za_ref, zb_ref, ca_ref, cb_ref, d_ref, g_ref, gs_ref, xb_ref, xa_ref,
    my, mx, by, bx,
    a_out, g_out, sum_ref, v_ref, n_ref, y_ref, z_ref, x_ref, u_ref,
):
    odd_x = index(GX) % 2
    t = step_length(total_ref)
    for f in range(FLUOR):
        tile = jnp.maximum(a_ref[f] - t * g_ref[f, G_HALO : G_HALO + ROWS, :COLS], 0.0)
        a_out[f] = tile
        x_ref[f, A_HALO : A_HALO + ROWS, :COLS] = tile
        x_ref[f, A_HALO : A_HALO + ROWS, COLS:] = jnp.maximum(
            side_ref[f] - t * gs_ref[f, G_HALO : G_HALO + ROWS, :], 0.0
        )
        for above, main, corner, far, near in (
            (True, choose(odd_x, za_ref[f, :A_HALO, :], zb_ref[f, :A_HALO, :]),
             choose(odd_x, ca_ref[A_HALO * f : A_HALO * f + A_HALO, :], cb_ref[A_HALO * f : A_HALO * f + A_HALO, :]), choose(odd_x, xa_ref[f], xb_ref[f]),
             slice(0, G_HALO)),
            (False, choose(odd_x, zb_ref[f, :A_HALO, :], za_ref[f, :A_HALO, :]),
             choose(odd_x, cb_ref[A_HALO * f : A_HALO * f + A_HALO, :], ca_ref[A_HALO * f : A_HALO * f + A_HALO, :]), choose(odd_x, xb_ref[f], xa_ref[f]),
             slice(G_ROWS - G_HALO, G_ROWS)),
        ):
            parts = [far[:32], g_ref[f, near, :COLS]], [far[32:], gs_ref[f, near, :]]
            if not above:
                parts = [part[::-1] for part in parts]
            rows = slice(0, A_HALO) if above else slice(A_HALO + ROWS, A_ROWS)
            x_ref[f, rows, :COLS] = jnp.maximum(main - t * jnp.concatenate(parts[0], axis=0), 0.0)
            x_ref[f, rows, COLS:] = jnp.maximum(corner - t * jnp.concatenate(parts[1], axis=0), 0.0)

    def put(f, u):
        u_ref[f] = u

    along_y(lambda part: x_ref[part], my[...], put)
    along_x(mx[...], lambda f: stacked(u_ref[f], 512), v_ref)
    mix(gram_ref, v_ref, d_ref, n_ref)
    sums(gram_ref, n_ref, by, bx, y_ref, z_ref, sum_ref)
    for f in range(FLUOR):
        g_out[f] = n_ref[f, G_HALO : G_HALO + ROWS, :COLS]


def last_body(total_ref, a_ref, g_ref, out_hbm, out_ref, sems):
    t = step_length(total_ref)
    copies = []
    for k in range(4):
        fields = slice(3 * k, 3 * k + 3)
        out_ref[fields] = jnp.maximum(a_ref[fields] - t * g_ref[fields], 0.0)
        part = pl.ds(3 * k, 3)
        copies.append(pltpu.make_async_copy(out_ref.at[part], out_hbm.at[part], sems.at[k]))
        copies[-1].start()
    for copy in copies:
        copy.wait()


TILE = (FLUOR, ROWS, COLS)
G_SHAPE = (FLUOR, G_ROWS, 256)
PROBE_SCRATCH = (pltpu.VMEM((FLUOR, ROWS, 256), f32), pltpu.VMEM(TILE, f32))
OWN_COST = 10**10
NEAR_COUNT = 32
FAR_COUNT = 16

first_call = kernel(
    first_body,
    "s" + "v" * 12,
    [(G_SHAPE, f32)] * 2 + [((FLUOR, 24, 128), f32)] * 2,
    10**9,
    [
        pltpu.VMEM(G_SHAPE, f32),
        pltpu.VMEM((FLUOR, 512, 256), bf16),
        pltpu.VMEM((FLUOR, 3 * P_ROWS, 256), bf16),
        pltpu.VMEM((FLUOR, P_HALO, 128), f32),
    ],
)
probe_call = kernel(probe_body, "svvv", [((NEAR_COUNT, 128), f32)], 10**9, PROBE_SCRATCH)
second_call = kernel(
    second_body,
    "s" + "v" * 16,
    [(TILE, f32)] * 2 + [((NEAR_COUNT, 128), f32)],
    10**9,
    [
        pltpu.VMEM(G_SHAPE, f32),
        pltpu.VMEM(G_SHAPE, f32),
        *PROBE_SCRATCH,
        pltpu.VMEM((FLUOR, A_ROWS, 256), f32),
        pltpu.VMEM((FLUOR, A_ROWS, 256), f32),
    ],
)


def length(axes):
    count = 1
    for axis in axes:
        count *= lax.axis_size(axis)
    return count


def trade(first, second, axes):
    return trade_first(first, axes), trade_second(second, axes)


def trade_first(edge, axes):
    return lax.ppermute(edge, axes, [(i, i ^ 1) for i in range(length(axes))])


def trade_second(edge, axes):
    count = length(axes)
    return lax.ppermute(edge, axes, [(i, (i + (1 if i % 2 else -1)) % count) for i in range(count)])


def spread(rows, axes):
    got = lax.all_to_all(rows.reshape(rows.shape[0], 1, 128), axes, 0, 0, tiled=True)
    return got.reshape(rows.shape[0], 128)


def local(sizes, abundance_start, measured, spectra, taps_x, taps_y):
    assert (length(NEAR), length((FAR,))) == (NEAR_COUNT, FAR_COUNT)

    edge = (FLUOR, A_HALO + P_HALO, 128)
    a0 = abundance_start[0]
    p, xb, xa, ya, yb = kernel(
        project_body,
        "hhh",
        [(TILE, f32)] + [(edge, f32)] * 2 + [((FLUOR, 40, 128), f32)] * 2,
        10**7,
        [
            pltpu.SMEM((FLUOR, CHAN), f32),
            pltpu.VMEM(TILE, f32),
            pltpu.VMEM((CHAN, ROWS, COLS), bf16),
            pltpu.VMEM(TILE, f32),
            pltpu.VMEM((FLUOR, 40, 128), f32),
            pltpu.VMEM((FLUOR, 40, 128), f32),
            pltpu.SemaphoreType.DMA((6,)),
            pltpu.SemaphoreType.DMA((7,)),
        ],
        60_000_000,
        pltpu.HBM,
    )(spectra.T, a0, measured[0])
    za, zb = trade(xa, xb, GX)
    ya, yb = trade(ya, yb, GY)
    my, py, by = kernel(
        functools.partial(y_matrices_body, sizes[1]),
        "s",
        [((768, 256), bf16)] * 2 + [((768, 128), bf16)],
        10**9,
    )(taps_y)
    corner = (REST + 4 * FLUOR, 128)
    side, ps, cb, ca = kernel(corner_body, "vv", [(TILE, f32)] * 2 + [(corner, f32)] * 2, 10**7)(ya, yb)
    ca, cb = trade(ca, cb, GX)
    gram, mx, px, bx = kernel(
        functools.partial(x_matrices_body, sizes[0]),
        "svv",
        [((FLUOR, FLUOR), f32), ((G_ROWS, 512), bf16), ((G_ROWS, 384), bf16), ((ROWS, 384), bf16)],
        10**9,
    )(taps_x, spectra.T, ps)
    u, w, ub, wb = kernel(
        own_body,
        "v" * 7,
        [((FLUOR, rows, 256), f32) for rows in (ROWS, ROWS, A_HALO, P_HALO)],
        OWN_COST,
    )(a0, side, p, ps, zb, my, py)
    ua, wa = kernel(first_rows_body, "vvv", [((FLUOR, rows, 256), f32) for rows in (A_HALO, P_HALO)], 10**7)(za, my, py)
    d, g, ya, yb = first_call(gram, u, w, ua, ub, wa, wb, cb, ca, my, py, mx, px)
    ya, yb = trade(ya, yb, GY)
    (partial,) = probe_call(gram, g, by, bx)
    near = spread(partial, NEAR)
    far, g_side, send = kernel(
        outer_body,
        "vvvv",
        [((FAR_COUNT, 128), f32), ((FLUOR, G_ROWS, 128), f32), ((FLUOR, 64, 128), f32)],
        10**8,
    )(near, g, ya, yb)
    xa, xb = trade(send, send, GX)
    total = spread(far, FAR)
    a1, g1, partial = second_call(
        gram, total, a0, side, za, zb, ca, cb, d, g, g_side, xb, xa, my, mx, by, bx
    )
    (far,) = kernel(relay, "v", [((FAR_COUNT, 128), f32)], 10**6)(spread(partial, NEAR))
    total = spread(far, FAR)
    (out,) = kernel(
        last_body,
        "vvv",
        [(TILE, f32)],
        10**7,
        [pltpu.VMEM(TILE, f32), pltpu.SemaphoreType.DMA((4,))],
        space=pltpu.HBM,
    )(total, a1, g1)
    return out[None]


def solution(mesh):
    count_x, count_y = mesh.shape["gx"], mesh.shape["gy"]
    parts = Mesh(
        mesh.devices.reshape(count_x // 4, 2, 2, 2, count_y // 2), ("y", "x_hi", "core", "x_lo", "z")
    )
    sizes = (count_x * ROWS, count_y * COLS)
    tiles = P(None, None, GX, GY)
    return jax.shard_map(
        functools.partial(local, sizes),
        mesh=parts,
        in_specs=(tiles, tiles, P(), P(), P()),
        out_specs=tiles,
        check_vma=False,
    )
```

```python
import functools

import jax
import jax.numpy as jnp
from jax import lax
from jax.experimental import pallas as pl
from jax.experimental.pallas import tpu as pltpu
from jax.sharding import Mesh
from jax.sharding import PartitionSpec as P

TAPS = 33
ITERS = 2
FLUOR = 12
CHAN = 32
ROWS = 64
COLS = 128

HALF = TAPS // 2
A_HALO = 3 * HALF
P_HALO = 2 * HALF
G_HALO = HALF
A_ROWS = ROWS + 2 * A_HALO
P_ROWS = ROWS + 2 * P_HALO
G_ROWS = ROWS + 2 * G_HALO

GX = ("y", "x_hi", "core")
GY = ("x_lo", "z")
NEAR = ("y", "x_hi", "core", "x_lo")
FAR = "z"

tiny_floor = 1e-06
f32 = jnp.float32
bf16 = jnp.bfloat16


SPACES = {"s": pltpu.SMEM, "v": pltpu.VMEM, "h": pltpu.HBM}


def kernel(body, ins, outs, cost, scratch=(), limit=32 * 2**20, space=pltpu.VMEM):
    return pl.pallas_call(
        body,
        in_specs=[pl.BlockSpec(memory_space=SPACES[kind]) for kind in ins],
        out_specs=[pl.BlockSpec(memory_space=space) for _ in outs],
        out_shape=[jax.ShapeDtypeStruct(shape, dtype) for shape, dtype in outs],
        scratch_shapes=list(scratch),
        compiler_params=pltpu.CompilerParams(vmem_limit_bytes=limit),
        cost_estimate=pl.CostEstimate(flops=cost, bytes_accessed=cost // 100, transcendentals=0),
    )


def index(axes):
    place = 0
    for axis in axes:
        place = place * lax.axis_size(axis) + lax.axis_index(axis)
    return place


def roll(x, by):
    by = by % 128
    return x if by == 0 else pltpu.roll(x, by, axis=x.ndim - 1)


def lane_of(shape):
    return lax.broadcasted_iota(jnp.int32, shape, len(shape) - 1)


def split(x):
    high = x.astype(bf16)
    return high, (x - high.astype(f32)).astype(bf16)


def dot(a, b):
    return jnp.dot(a, b, preferred_element_type=f32)


def dot_right(x, w):
    high, low = split(x)
    return dot(jnp.concatenate([high, low, high], axis=1), w)


def stacked(x, depth):
    high, low = split(x)
    parts = [high, low, high]
    spare = depth - 3 * x.shape[0]
    if spare:
        parts.append(jnp.zeros((spare, x.shape[1]), bf16))
    return jnp.concatenate(parts, axis=0)


def side_position(index, halo):
    left = index - COLS - halo
    right = index - halo
    position = jnp.where(index < COLS, index, jnp.where(index < COLS + halo, left, right))
    return jnp.where(index < COLS + 2 * halo, position, 1 << 20)


def tap_matrix(taps_ref, offset):
    out = jnp.zeros(offset.shape, f32)
    for t in range(TAPS):
        out = jnp.where(offset == t, taps_ref[t], out)
    return out


def inside(position, base, size):
    where = position + base
    return jnp.logical_and(where >= 0, where < size)


def exact_dot(a, b):
    return lax.dot_general(a, b, (((1,), (0,)), ((), ())), precision=lax.Precision.HIGHEST, preferred_element_type=f32)


def rows_cols(shape):
    return lax.broadcasted_iota(jnp.int32, shape, 0), lax.broadcasted_iota(jnp.int32, shape, 1)


def put_right(x, ref):
    high, low = split(x)
    rows = x.shape[0]
    ref[:rows, :] = high
    ref[rows : 2 * rows, :] = high
    ref[2 * rows :, :] = low


def put_left(x, part, ref):
    high, low = split(x)
    ref[...] = jnp.where(part < 2, high.astype(f32), low.astype(f32)).astype(bf16)


def y_matrices_body(size_y, ty_ref, my, py, by):
    base_y = index(GY) * COLS
    r, c = rows_cols((256, 256))
    source = side_position(r, P_HALO)
    target = side_position(c, G_HALO)
    okay = jnp.logical_and(inside(source, base_y, size_y), inside(target, base_y, size_y))
    put_right(jnp.where(okay, tap_matrix(ty_ref, target - source + HALF), 0.0), py)
    source = side_position(r, A_HALO)
    middle = c - P_HALO
    okay = jnp.logical_and(inside(source, base_y, size_y), inside(middle, base_y, size_y))
    first = jnp.where(okay, tap_matrix(ty_ref, source - middle + HALF), 0.0)
    middle = r - P_HALO
    second = jnp.where(inside(target, base_y, size_y), tap_matrix(ty_ref, target - middle + HALF), 0.0)
    put_right(exact_dot(first, second), my)
    r, c = rows_cols((256, 128))
    source = side_position(r, G_HALO)
    okay = inside(source, base_y, size_y)
    put_right(jnp.where(okay, tap_matrix(ty_ref, source - c + HALF), 0.0), by)


def x_matrices_body(size_x, tx_ref, spectra_ref, after_ref, gram_ref, mx, px, bx):
    spectra = spectra_ref[...]
    gram_ref[...] = lax.dot_general(
        spectra, spectra, (((1,), (1,)), ((), ())), precision=lax.Precision.HIGHEST, preferred_element_type=f32
    )
    base_x = index(GX) * ROWS
    r, c = rows_cols((128, 512))
    part = c // A_ROWS
    source = c - part * A_ROWS - A_HALO
    middle = r - P_HALO
    okay = jnp.logical_and(inside(source, base_x, size_x), inside(middle, base_x, size_x))
    okay = jnp.logical_and(okay, part < 3)
    first = jnp.where(okay, tap_matrix(tx_ref, source - middle + HALF), 0.0)
    r, c = rows_cols((G_ROWS, 128))
    target = r - G_HALO
    middle = c - P_HALO
    second = jnp.where(inside(target, base_x, size_x), tap_matrix(tx_ref, target - middle + HALF), 0.0)
    r, c = rows_cols((G_ROWS, 512))
    put_left(exact_dot(second, first), c // A_ROWS, mx)
    r, c = rows_cols((G_ROWS, 384))
    part = c // P_ROWS
    source = c - part * P_ROWS - P_HALO
    target = r - G_HALO
    okay = jnp.logical_and(inside(source, base_x, size_x), inside(target, base_x, size_x))
    put_left(jnp.where(okay, tap_matrix(tx_ref, target - source + HALF), 0.0), part, px)
    r, c = rows_cols((ROWS, 384))
    part = c // G_ROWS
    source = c - part * G_ROWS - G_HALO
    okay = jnp.logical_and(inside(source, base_x, size_x), part < 3)
    put_left(jnp.where(okay, tap_matrix(tx_ref, source - r + HALF), 0.0), part, bx)


def choose(odd, if_odd, if_even):
    return jnp.where(odd == 1, if_odd, if_even)


def edge_rows(odd_x, pairing, depth):
    top = odd_x == 1 if pairing == 0 else odd_x == 0
    return pl.multiple_of(jnp.where(top, 0, ROWS - depth), 16)


def project_body(
    s_hbm, a_hbm, m_hbm, p_hbm, xb_hbm, xa_hbm, ya_hbm, yb_hbm,
    spectra_ref, a_ref, m_ref, p_ref, ya_ref, yb_ref, sems, out_sems,
):
    step = 32
    copy_s = pltpu.make_async_copy(s_hbm, spectra_ref, sems.at[5])
    copy_s.start()
    copies = [
        pltpu.make_async_copy(m_hbm.at[:, pl.ds(k * step, step), :], m_ref.at[:, pl.ds(k * step, step), :], sems.at[k])
        for k in range(ROWS // step)
    ]
    for copy in copies:
        copy.start()
    copy_a = pltpu.make_async_copy(a_hbm, a_ref, sems.at[ROWS // step])
    copy_a.start()
    odd_x = index(GX) % 2
    edges = []
    copy_s.wait()
    for k, copy in enumerate(copies):
        copy.wait()
        start = k * step
        acc = [jnp.zeros((step, COLS), f32) for _ in range(FLUOR)]
        for c in range(CHAN):
            seen = m_ref[c, start : start + step, :].astype(f32)
            for f in range(FLUOR):
                acc[f] = acc[f] + spectra_ref[f, c] * seen
        for f in range(FLUOR):
            p_ref[f, start : start + step, :] = acc[f]
        if k == 0:
            copy_a.wait()
            for pairing, x_hbm in ((1, xb_hbm), (0, xa_hbm)):
                rows = pl.ds(edge_rows(odd_x, pairing, A_HALO), A_HALO)
                edges.append(
                    pltpu.make_async_copy(a_ref.at[:, rows, :], x_hbm.at[:, pl.ds(0, A_HALO), :], out_sems.at[pairing])
                )
                edges[-1].start()
    for k, x_hbm in ((1, xb_hbm), (0, xa_hbm)):
        rows = pl.ds(edge_rows(odd_x, k, P_HALO), P_HALO)
        edges.append(
            pltpu.make_async_copy(p_ref.at[:, rows, :], x_hbm.at[:, pl.ds(A_HALO, P_HALO), :], out_sems.at[2 + k])
        )
        edges[-1].start()
    edges.append(pltpu.make_async_copy(p_ref, p_hbm, out_sems.at[4]))
    edges[-1].start()
    odd_y = index(GY) % 2
    lane = lane_of((32, 128))
    lane8 = lane_of((8, 128))
    for f in range(FLUOR):
        sides = []
        for a_from, p_from in ((0, 0), (COLS - A_HALO, COLS - P_HALO)):
            top = roll(a_ref[f, :32, :], -a_from)
            low = roll(a_ref[f, 32:, :], A_HALO - a_from)
            side = roll(p_ref[f, :32, :], 2 * A_HALO - p_from)
            main = jnp.where(lane < A_HALO, top, jnp.where(lane < 2 * A_HALO, low, side))
            rest = roll(p_ref[f, 32:40, :], -p_from)
            for k in range(1, 4):
                piece = roll(p_ref[f, 32 + 8 * k : 40 + 8 * k, :], 32 * k - p_from)
                rest = jnp.where(lane8 < 32 * k, rest, piece)
            sides.append((main, rest))
        (left, left_rest), (right, right_rest) = sides
        ya_ref[f, :32, :] = choose(odd_y, left, right)
        yb_ref[f, :32, :] = choose(odd_y, right, left)
        ya_ref[f, 32:, :] = choose(odd_y, left_rest, right_rest)
        yb_ref[f, 32:, :] = choose(odd_y, right_rest, left_rest)
    for k, (ref, y_hbm) in enumerate(((ya_ref, ya_hbm), (yb_ref, yb_hbm))):
        edges.append(pltpu.make_async_copy(ref, y_hbm, out_sems.at[5 + k]))
        edges[-1].start()
    for copy in edges:
        copy.wait()


REST = FLUOR * A_HALO


def pack_corner(odd_x, pairing, side_ref, ps_ref, out_ref):
    lane = lane_of((32, 128))
    lane4 = lane_of((4, 128))
    lane16 = lane_of((16, 128))
    spare = 2 * A_HALO
    a_rows = pl.ds(edge_rows(odd_x, pairing, A_HALO), A_HALO)
    p_rows = pl.ds(edge_rows(odd_x, pairing, P_HALO), P_HALO)
    for f in range(FLUOR):
        p_top = ps_ref[f, p_rows, :]
        a_side = side_ref[f, a_rows, :]
        at = A_HALO * f
        out_ref[at : at + 32, :] = jnp.where(lane < spare, a_side[:32], roll(p_top, spare))
        out_ref[at + 32 : at + 48, :] = jnp.where(lane16 < spare, a_side[32:], roll(p_top[:16], spare - P_HALO))
        rest = roll(p_top[16:20], -P_HALO)
        for k in range(1, 4):
            rest = jnp.where(lane4 < 32 * k, rest, roll(p_top[16 + 4 * k : 20 + 4 * k], 32 * k - P_HALO))
        out_ref[REST + 4 * f : REST + 4 * f + 4, :] = rest


def corner_body(ya_ref, yb_ref, side_ref, ps_ref, cb_ref, ca_ref):
    odd_x = index(GX) % 2
    odd_y = index(GY) % 2
    lane = lane_of((32, 128))
    lane8 = lane_of((8, 128))
    for f in range(FLUOR):
        first = ya_ref[f, :32, :]
        second = yb_ref[f, :32, :]
        left = choose(odd_y, first, second)
        right = choose(odd_y, second, first)
        side_ref[f, :32, :] = jnp.where(lane < A_HALO, left, jnp.where(lane < 2 * A_HALO, roll(right, A_HALO), 0.0))
        side_ref[f, 32:, :] = jnp.where(lane < A_HALO, roll(left, -A_HALO), jnp.where(lane < 2 * A_HALO, right, 0.0))
        ps_ref[f, :32, :] = jnp.where(
            lane < P_HALO, roll(left, -2 * A_HALO), jnp.where(lane < 2 * P_HALO, roll(right, P_HALO - 2 * A_HALO), 0.0)
        )
        first = ya_ref[f, 32:, :]
        second = yb_ref[f, 32:, :]
        left = choose(odd_y, first, second)
        right = choose(odd_y, second, first)
        for k in range(4):
            ps_ref[f, 32 + 8 * k : 40 + 8 * k, :] = jnp.where(
                lane8 < P_HALO, roll(left, -32 * k), jnp.where(lane8 < 2 * P_HALO, roll(right, P_HALO - 32 * k), 0.0)
            )
    pack_corner(odd_x, 0, side_ref, ps_ref, ca_ref)
    pack_corner(odd_x, 1, side_ref, ps_ref, cb_ref)


GROUP = 4


def along_y(x, w, put):
    for f in range(0, FLUOR, GROUP):
        part = x(slice(f, f + GROUP))
        out = dot_right(part.reshape(-1, part.shape[2]), w)
        out = out.reshape(GROUP, part.shape[1], out.shape[1])
        for k in range(GROUP):
            put(f + k, out[k])


X_GROUP = 4


def along_x(m, stack, out_ref):
    for f in range(0, FLUOR, X_GROUP):
        out = dot(m, jnp.concatenate([stack(f + k) for k in range(X_GROUP)], axis=1))
        for k in range(X_GROUP):
            out_ref[f + k] = out[:, 256 * k : 256 * k + 256]


def wide(main, side):
    return jnp.concatenate([main, side], axis=2)


def mix(gram_ref, v_ref, d_ref, g_ref):
    step = 8

    def mixed(part, f):
        acc = gram_ref[f, 0] * part[0]
        for k in range(1, FLUOR):
            acc = acc + gram_ref[f, k] * part[k]
        return acc

    for start in range(0, G_ROWS, step):
        part = [v_ref[f, start : start + step, :COLS] for f in range(FLUOR)]
        for f in range(FLUOR):
            g_ref[f, start : start + step, :COLS] = mixed(part, f) - d_ref[f, start : start + step, :COLS]
    lane = lane_of((step, 128))
    group = G_ROWS // 4
    for start in range(0, group, step):
        rows = [slice(k * group + start, k * group + start + step) for k in range(4)]
        part = []
        for f in range(FLUOR):
            packed = v_ref[f, rows[0], COLS:]
            for k in range(1, 4):
                packed = packed + roll(v_ref[f, rows[k], COLS:], 32 * k)
            part.append(packed)
        for f in range(FLUOR):
            out = mixed(part, f)
            for k in range(4):
                side = jnp.where(lane < 2 * G_HALO, roll(out, -32 * k), 0.0)
                g_ref[f, rows[k], COLS:] = side - d_ref[f, rows[k], COLS:]


def sums(gram_ref, g_ref, by, bx, y_ref, z_ref, sum_ref):
    along_x(bx[...], lambda f: stacked(g_ref[f], 384), y_ref)

    def put(f, z):
        z_ref[f] = z

    along_y(lambda part: y_ref[part], by[...], put)
    grad = jnp.zeros((8, 128), f32)
    image = jnp.zeros((8, 128), f32)
    for start in range(0, ROWS, 8):
        part = [z_ref[f, start : start + 8, :] for f in range(FLUOR)]
        for f in range(FLUOR):
            acc = 0.5 * gram_ref[f, f] * part[f]
            for k in range(f):
                acc = acc + gram_ref[f, k] * part[k]
            image = image + acc * part[f]
            g = g_ref[f, G_HALO + start : G_HALO + start + 8, :COLS]
            grad = grad + g * g
    grad = jnp.sum(grad, axis=0, keepdims=True)
    image = 2.0 * jnp.sum(image, axis=0, keepdims=True)
    lane = lane_of((1, 128))
    row = jnp.where(lane < 64, grad + roll(grad, 64), image + roll(image, 64))
    sum_ref[...] = jnp.broadcast_to(row, sum_ref.shape)


def step_length(total_ref):
    total = jnp.sum(total_ref[...], axis=0, keepdims=True)
    lane = lane_of((1, 128))
    grad = jnp.sum(jnp.where(lane < 64, total, 0.0), axis=1, keepdims=True)
    image = jnp.sum(jnp.where(lane < 64, 0.0, total), axis=1, keepdims=True)
    return grad / (image + tiny_floor)


def put_stack(ref, f, start, depth, x):
    high, low = split(x)
    for at, part in ((0, high), (depth, low), (2 * depth, high)):
        ref[f, pl.ds(pl.multiple_of(start + at, 16), x.shape[0]), :] = part


def along_half(x, w_ref, start, put):
    w = jnp.concatenate([w_ref[256 * k + start : 256 * k + start + 128, :] for k in range(3)], axis=0)
    along_y(x, w, put)


def store(ref):
    def put(f, x):
        ref[f] = x

    return put


def own_body(a_ref, side_ref, p_ref, ps_ref, xb_ref, my, py, u_ref, w_ref, ub_ref, wb_ref):
    along_y(lambda part: wide(p_ref[part], ps_ref[part]), py[...], store(w_ref))
    along_y(lambda part: wide(a_ref[part], side_ref[part]), my[...], store(u_ref))
    along_half(lambda part: xb_ref[part, :A_HALO, :], my, 0, store(ub_ref))
    along_half(lambda part: xb_ref[part, A_HALO:, :], py, 0, store(wb_ref))


def first_rows_body(xa_ref, my, py, ua_ref, wa_ref):
    along_half(lambda part: xa_ref[part, :A_HALO, :], my, 0, store(ua_ref))
    along_half(lambda part: xa_ref[part, A_HALO:, :], py, 0, store(wa_ref))


def first_body(
    gram_ref, u_ref, w_ref, ua_ref, ub_ref, wa_ref, wb_ref, cb_ref, ca_ref, my, py, mx, px,
    d_ref, g_ref, ya_ref, yb_ref, v_ref, su_ref, sw_ref, side_ref,
):
    odd_x = index(GX) % 2
    odd_y = index(GY) % 2
    lane = lane_of((32, 128))
    lane16 = lane_of((16, 128))
    lane8 = lane_of((8, 128))
    spare = 2 * A_HALO
    su_ref[:, 3 * A_ROWS :, :] = jnp.zeros((FLUOR, 512 - 3 * A_ROWS, 256), bf16)
    for u_part, w_part, corner, above in (
        (ua_ref, wa_ref, ca_ref, odd_x == 1),
        (ub_ref, wb_ref, cb_ref, odd_x == 0),
    ):
        for f in range(FLUOR):
            at = A_HALO * f
            left = roll(corner[at : at + 32, :], -spare)
            right = roll(corner[at + 32 : at + 48, :], P_HALO - spare)
            rest = corner[REST + 4 * f : REST + 4 * f + 4, :]
            last = jnp.concatenate([roll(rest, P_HALO - 32 * k) for k in range(4)], axis=0)
            side_ref[f, :16, :] = jnp.where(lane16 < P_HALO, left[:16], jnp.where(lane16 < 2 * P_HALO, right, 0.0))
            side_ref[f, 16:24, :] = jnp.where(
                lane8 < P_HALO, left[16:24], jnp.where(lane8 < 2 * P_HALO, last[:8], 0.0)
            )
            side_ref[f, 24:, :] = jnp.where(lane8 < P_HALO, left[24:], jnp.where(lane8 < 2 * P_HALO, last[8:], 0.0))
        a_at = jnp.where(above, 0, A_HALO + ROWS)
        p_at = jnp.where(above, 0, P_HALO + ROWS)
        along_half(
            lambda part: side_ref[part],
            py,
            128,
            lambda f, x: put_stack(sw_ref, f, p_at, P_ROWS, x + w_part[f]),
        )
        along_half(
            lambda part: corner[A_HALO * part.start : A_HALO * part.stop, :].reshape(-1, A_HALO, 128),
            my,
            128,
            lambda f, x: put_stack(su_ref, f, a_at, A_ROWS, x + u_part[f]),
        )
    for f in range(FLUOR):
        put_stack(sw_ref, f, P_HALO, P_ROWS, w_ref[f])
        put_stack(su_ref, f, A_HALO, A_ROWS, u_ref[f])
    along_x(px[...], lambda f: sw_ref[f], d_ref)
    along_x(mx[...], lambda f: su_ref[f], v_ref)
    mix(gram_ref, v_ref, d_ref, g_ref)
    lane = lane_of((24, 128))
    for f in range(FLUOR):
        edges = []
        for start in (G_HALO, COLS - G_HALO - 32):
            out = roll(g_ref[f, :24, :COLS], -start)
            for k in range(1, 4):
                piece = roll(g_ref[f, 24 * k : 24 * k + 24, :COLS], 32 * k - start)
                out = jnp.where(lane < 32 * k, out, piece)
            edges.append(out)
        ya_ref[f] = choose(odd_y, edges[0], edges[1])
        yb_ref[f] = choose(odd_y, edges[1], edges[0])


def probe_body(gram_ref, g_ref, by, bx, sum_ref, y_ref, z_ref):
    sums(gram_ref, g_ref, by, bx, y_ref, z_ref, sum_ref)


def relay(near_ref, out_ref):
    out_ref[...] = jnp.broadcast_to(jnp.sum(near_ref[...], axis=0, keepdims=True), out_ref.shape)


def outer_body(near_ref, g_ref, ya_ref, yb_ref, far_ref, side_ref, send_ref):
    relay(near_ref, far_ref)
    odd_y = index(GY) % 2
    lane = lane_of((24, 128))
    for f in range(FLUOR):
        left = choose(odd_y, ya_ref[f], yb_ref[f])
        right = choose(odd_y, yb_ref[f], ya_ref[f])
        for k in range(4):
            own = roll(g_ref[f, 24 * k : 24 * k + 24, COLS:], 32)
            side_ref[f, 24 * k : 24 * k + 24, :] = jnp.where(
                lane < 32,
                roll(left, -32 * k),
                jnp.where(lane < 64, own, jnp.where(lane < 96, roll(right, 64 - 32 * k), 0.0)),
            )
        send_ref[f, :32, :] = g_ref[f, 2 * G_HALO : 2 * G_HALO + 32, :COLS]
        send_ref[f, 32:, :] = side_ref[f, 2 * G_HALO : 2 * G_HALO + 32, :]


def second_body(
    gram_ref, total_ref, a_ref, side_ref, za_ref, zb_ref, ca_ref, cb_ref, d_ref, g_ref, gs_ref, xb_ref, xa_ref,
    my, mx, by, bx,
    a_out, g_out, sum_ref, v_ref, n_ref, y_ref, z_ref, x_ref, u_ref,
):
    odd_x = index(GX) % 2
    t = step_length(total_ref)
    for f in range(FLUOR):
        tile = jnp.maximum(a_ref[f] - t * g_ref[f, G_HALO : G_HALO + ROWS, :COLS], 0.0)
        a_out[f] = tile
        x_ref[f, A_HALO : A_HALO + ROWS, :COLS] = tile
        x_ref[f, A_HALO : A_HALO + ROWS, COLS:] = jnp.maximum(
            side_ref[f] - t * gs_ref[f, G_HALO : G_HALO + ROWS, :], 0.0
        )
        for above, main, corner, far, near in (
            (True, choose(odd_x, za_ref[f, :A_HALO, :], zb_ref[f, :A_HALO, :]),
             choose(odd_x, ca_ref[A_HALO * f : A_HALO * f + A_HALO, :], cb_ref[A_HALO * f : A_HALO * f + A_HALO, :]), choose(odd_x, xa_ref[f], xb_ref[f]),
             slice(0, G_HALO)),
            (False, choose(odd_x, zb_ref[f, :A_HALO, :], za_ref[f, :A_HALO, :]),
             choose(odd_x, cb_ref[A_HALO * f : A_HALO * f + A_HALO, :], ca_ref[A_HALO * f : A_HALO * f + A_HALO, :]), choose(odd_x, xb_ref[f], xa_ref[f]),
             slice(G_ROWS - G_HALO, G_ROWS)),
        ):
            parts = [far[:32], g_ref[f, near, :COLS]], [far[32:], gs_ref[f, near, :]]
            if not above:
                parts = [part[::-1] for part in parts]
            rows = slice(0, A_HALO) if above else slice(A_HALO + ROWS, A_ROWS)
            x_ref[f, rows, :COLS] = jnp.maximum(main - t * jnp.concatenate(parts[0], axis=0), 0.0)
            x_ref[f, rows, COLS:] = jnp.maximum(corner - t * jnp.concatenate(parts[1], axis=0), 0.0)

    def put(f, u):
        u_ref[f] = u

    along_y(lambda part: x_ref[part], my[...], put)
    along_x(mx[...], lambda f: stacked(u_ref[f], 512), v_ref)
    mix(gram_ref, v_ref, d_ref, n_ref)
    sums(gram_ref, n_ref, by, bx, y_ref, z_ref, sum_ref)
    for f in range(FLUOR):
        g_out[f] = n_ref[f, G_HALO : G_HALO + ROWS, :COLS]


def last_body(total_ref, a_ref, g_ref, out_hbm, out_ref, sems):
    t = step_length(total_ref)
    copies = []
    for k in range(4):
        fields = slice(3 * k, 3 * k + 3)
        out_ref[fields] = jnp.maximum(a_ref[fields] - t * g_ref[fields], 0.0)
        part = pl.ds(3 * k, 3)
        copies.append(pltpu.make_async_copy(out_ref.at[part], out_hbm.at[part], sems.at[k]))
        copies[-1].start()
    for copy in copies:
        copy.wait()


TILE = (FLUOR, ROWS, COLS)
G_SHAPE = (FLUOR, G_ROWS, 256)
PROBE_SCRATCH = (pltpu.VMEM((FLUOR, ROWS, 256), f32), pltpu.VMEM(TILE, f32))
OWN_COST = 10**10
NEAR_COUNT = 32
FAR_COUNT = 16

first_call = kernel(
    first_body,
    "s" + "v" * 12,
    [(G_SHAPE, f32)] * 2 + [((FLUOR, 24, 128), f32)] * 2,
    10**9,
    [
        pltpu.VMEM(G_SHAPE, f32),
        pltpu.VMEM((FLUOR, 512, 256), bf16),
        pltpu.VMEM((FLUOR, 3 * P_ROWS, 256), bf16),
        pltpu.VMEM((FLUOR, P_HALO, 128), f32),
    ],
)
probe_call = kernel(probe_body, "svvv", [((NEAR_COUNT, 128), f32)], 10**9, PROBE_SCRATCH)
second_call = kernel(
    second_body,
    "s" + "v" * 16,
    [(TILE, f32)] * 2 + [((NEAR_COUNT, 128), f32)],
    10**9,
    [
        pltpu.VMEM(G_SHAPE, f32),
        pltpu.VMEM(G_SHAPE, f32),
        *PROBE_SCRATCH,
        pltpu.VMEM((FLUOR, A_ROWS, 256), f32),
        pltpu.VMEM((FLUOR, A_ROWS, 256), f32),
    ],
)


def length(axes):
    count = 1
    for axis in axes:
        count *= lax.axis_size(axis)
    return count


def trade(first, second, axes):
    return trade_first(first, axes), trade_second(second, axes)


def trade_first(edge, axes):
    return lax.ppermute(edge, axes, [(i, i ^ 1) for i in range(length(axes))])


def trade_second(edge, axes):
    count = length(axes)
    return lax.ppermute(edge, axes, [(i, (i + (1 if i % 2 else -1)) % count) for i in range(count)])


def spread(rows, axes):
    got = lax.all_to_all(rows.reshape(rows.shape[0], 1, 128), axes, 0, 0, tiled=True)
    return got.reshape(rows.shape[0], 128)


def local(sizes, abundance_start, measured, spectra, taps_x, taps_y):
    assert (length(NEAR), length((FAR,))) == (NEAR_COUNT, FAR_COUNT)

    edge = (FLUOR, A_HALO + P_HALO, 128)
    a0 = abundance_start[0]
    p, xb, xa, ya, yb = kernel(
        project_body,
        "hhh",
        [(TILE, f32)] + [(edge, f32)] * 2 + [((FLUOR, 40, 128), f32)] * 2,
        10**7,
        [
            pltpu.SMEM((FLUOR, CHAN), f32),
            pltpu.VMEM(TILE, f32),
            pltpu.VMEM((CHAN, ROWS, COLS), bf16),
            pltpu.VMEM(TILE, f32),
            pltpu.VMEM((FLUOR, 40, 128), f32),
            pltpu.VMEM((FLUOR, 40, 128), f32),
            pltpu.SemaphoreType.DMA((6,)),
            pltpu.SemaphoreType.DMA((7,)),
        ],
        60_000_000,
        pltpu.HBM,
    )(spectra.T, a0, measured[0])
    za, zb = trade(xa, xb, GX)
    ya, yb = trade(ya, yb, GY)
    my, py, by = kernel(
        functools.partial(y_matrices_body, sizes[1]),
        "s",
        [((768, 256), bf16)] * 2 + [((768, 128), bf16)],
        10**9,
    )(taps_y)
    corner = (REST + 4 * FLUOR, 128)
    side, ps, cb, ca = kernel(corner_body, "vv", [(TILE, f32)] * 2 + [(corner, f32)] * 2, 10**7)(ya, yb)
    ca, cb = trade(ca, cb, GX)
    gram, mx, px, bx = kernel(
        functools.partial(x_matrices_body, sizes[0]),
        "svv",
        [((FLUOR, FLUOR), f32), ((G_ROWS, 512), bf16), ((G_ROWS, 384), bf16), ((ROWS, 384), bf16)],
        10**9,
    )(taps_x, spectra.T, ps)
    u, w, ub, wb = kernel(
        own_body,
        "v" * 7,
        [((FLUOR, rows, 256), f32) for rows in (ROWS, ROWS, A_HALO, P_HALO)],
        OWN_COST,
    )(a0, side, p, ps, zb, my, py)
    ua, wa = kernel(first_rows_body, "vvv", [((FLUOR, rows, 256), f32) for rows in (A_HALO, P_HALO)], 10**7)(za, my, py)
    d, g, ya, yb = first_call(gram, u, w, ua, ub, wa, wb, cb, ca, my, py, mx, px)
    ya, yb = trade(ya, yb, GY)
    (partial,) = probe_call(gram, g, by, bx)
    near = spread(partial, NEAR)
    far, g_side, send = kernel(
        outer_body,
        "vvvv",
        [((FAR_COUNT, 128), f32), ((FLUOR, G_ROWS, 128), f32), ((FLUOR, 64, 128), f32)],
        10**8,
    )(near, g, ya, yb)
    xa, xb = trade(send, send, GX)
    total = spread(far, FAR)
    a1, g1, partial = second_call(
        gram, total, a0, side, za, zb, ca, cb, d, g, g_side, xb, xa, my, mx, by, bx
    )
    (far,) = kernel(relay, "v", [((FAR_COUNT, 128), f32)], 10**6)(spread(partial, NEAR))
    total = spread(far, FAR)
    (out,) = kernel(
        last_body,
        "vvv",
        [(TILE, f32)],
        10**7,
        [pltpu.VMEM(TILE, f32), pltpu.SemaphoreType.DMA((4,))],
        space=pltpu.HBM,
    )(total, a1, g1)
    return out[None]


def solution(mesh):
    count_x, count_y = mesh.shape["gx"], mesh.shape["gy"]
    parts = Mesh(
        mesh.devices.reshape(count_x // 4, 2, 2, 2, count_y // 2), ("y", "x_hi", "core", "x_lo", "z")
    )
    sizes = (count_x * ROWS, count_y * COLS)
    tiles = P(None, None, GX, GY)
    return jax.shard_map(
        functools.partial(local, sizes),
        mesh=parts,
        in_specs=(tiles, tiles, P(), P(), P()),
        out_specs=tiles,
        check_vma=False,
    )
```
